32 devices in a mesh: patch: 16 (over z, y, x), vec: 2 (over core).
Axes of the slice: x: 2, y: 2, z: 4, core: 2. Of those that a mesh axis runs over, the one named last changes fastest.
Arguments:
- vectors: float32 [8192, 512], P('patch', 'vec'), may hold values from -6 to 6
- blocks: bfloat16 [1024, 256, 256], P('patch'), may hold values from -0.075 to 0.075, as said below
- block_row: int32 [1024], P('patch'), may hold values from 0 to 31, as said below
- block_col: int32 [1024], P('patch'), may hold values from 0 to 31, as said below
- block_count: int32 [16], P('patch'), may hold values from 0 to 58, as said below
Outputs:
- subspace: float32 [8192, 512], P('patch', 'vec')
- residual: float32 [8192, 512], P('patch', 'vec')
The draws below stay inside these ranges and needn't reach their ends.
Inputs may be any that keep to these rules, and one draw needn't show every extreme that they name: `block_row`: device p owns entries p * 64 to (p + 1) * 64 - 1. Its used slots come first and hold tiles of block rows 4 * (p // 2) to 4 * (p // 2) + 3 whose block column is at most the row and at least 4 * (p // 2) - 12; both devices of a pair p // 2 share these rows, tiles grouped by 4 x 4 patches each on one device. Every lower tile of the pattern stands in exactly one used slot, every diagonal tile is present, and unused slots name block row and column 4 * (p // 2). `block_col`: the block column of the tile in the same slot, as described for block_row. `block_count`: at most 58 used slots on a device, reached by some device in every draw; the loads are uneven. `blocks`: entries of unused slots are never read.
All inputs are finite; a program needn't handle non-finite values.
Results may differ from the reference program's by a relative error of at most 0.0038.
Values may be sent and summed in bfloat16 or wider, within the bound.
No kernel may reach another device: no remote copies, remote signals or barrier semaphores. Data moves between devices by JAX's collectives and lax.ppermute only.
A program may use at most 128 MiB of HBM per device.

```python
import jax
import jax.numpy as jnp
from jax import lax

BS = 256
K = 512
BLK_DEV = 64
STEPS = 2
NH = 8192


def slot_layout(key):
    key = jax.random.fold_in(key, 7919)
    pair_total = NH // (4 * BS)
    key_owner, key_keep, key_star = jax.random.split(key, 3)
    owners = jax.random.randint(key_owner, (pair_total, 4), 0, 2)
    keeps = jax.random.randint(key_keep, (pair_total, 4, 4, 4), 0, 4) > 0
    starred = jax.random.randint(key_star, (), 3, pair_total)
    is_star = jnp.arange(pair_total) == starred
    owners = jnp.where(is_star[:, None], 0, owners)
    keeps = keeps | is_star[:, None, None, None]
    pair_ids = jnp.arange(pair_total)[:, None, None, None]
    diag_off = jnp.arange(4)[None, :, None, None]
    sub_row = jnp.arange(4)[None, None, :, None]
    sub_col = jnp.arange(4)[None, None, None, :]
    shape_full = (pair_total, 4, 4, 4)
    row_ids = jnp.broadcast_to(4 * pair_ids + sub_row, shape_full)
    col_ids = jnp.broadcast_to(4 * (pair_ids - diag_off) + sub_col, shape_full)
    valid = (pair_ids - diag_off >= 0) & ((diag_off > 0) | (sub_row >= sub_col))
    present = valid & (keeps | (diag_off == 0) & (sub_row == sub_col))
    owner_full = owners[:, :, None, None]
    take_low = present & (owner_full == 0)
    take_high = present & (owner_full == 1)
    taken = jnp.stack([take_low, take_high], axis=1).reshape(pair_total * 2, 64)
    rows_flat = jnp.broadcast_to(row_ids.reshape(pair_total, 1, 64), (pair_total, 2, 64)).reshape(pair_total * 2, 64)
    cols_flat = jnp.broadcast_to(col_ids.reshape(pair_total, 1, 64), (pair_total, 2, 64)).reshape(pair_total * 2, 64)
    position = jnp.arange(64)[None, :]
    sort_key = jnp.where(taken, position, 64 + position)
    order = jnp.argsort(sort_key, axis=1)
    taken_sorted = jnp.take_along_axis(taken, order, axis=1)
    rows_sorted = jnp.take_along_axis(rows_flat, order, axis=1)
    cols_sorted = jnp.take_along_axis(cols_flat, order, axis=1)
    home = (4 * (jnp.arange(pair_total * 2) // 2))[:, None]
    rows_final = jnp.where(taken_sorted, rows_sorted, home).reshape(-1).astype(jnp.int32)
    cols_final = jnp.where(taken_sorted, cols_sorted, home).reshape(-1).astype(jnp.int32)
    counts = jnp.sum(taken.astype(jnp.int32), axis=1).astype(jnp.int32)
    return (rows_final, cols_final, counts)


def draw_block_row(key, part):
    return slot_layout(key)[0]


def draw_block_col(key, part):
    return slot_layout(key)[1]


def draw_block_count(key, part):
    return slot_layout(key)[2]


def draw_blocks(key, part):
    key = jax.random.fold_in(key, 4241)
    slot_total = NH // (2 * BS) * BLK_DEV
    spread = 1.0 / (5.0 * BS ** 0.5)
    limit = 0.99 * 6.0 * spread
    shared = 0.9 / BS
    noise = jnp.clip(jax.random.normal(key, (slot_total, BS, BS), jnp.float32), -5.5, 5.5) * spread
    values = jnp.clip(noise + shared, -limit, limit)
    return values.astype(jnp.bfloat16)


def level_of(own_key, shape, cuts, smallest, largest):
    loudness, own = 1.0, jax.random.fold_in(own_key, 6)
    for axis_at, shards_of in cuts:
        draws = jnp.exp(jax.random.uniform(jax.random.fold_in(own, axis_at), (shards_of,), jnp.float32, smallest / len(cuts), largest / len(cuts)))
        loudness = loudness * jnp.repeat(draws, shape[axis_at] // shards_of).reshape([-1 if axis == axis_at else 1 for axis in range(len(shape))])
    return loudness


def centred(own_key, extent, scale, most, pieces=(), kind=jnp.bfloat16):
    factor_of = level_of(own_key, extent, pieces, -0.22, 0.18) if pieces else 1.0
    values = jax.random.normal(own_key, extent, jnp.float32) * scale * factor_of
    return jnp.minimum(jnp.maximum(values, -most), most).astype(kind)


def setup_inputs(seed: int = 0) -> dict:
    seeds = jax.random.split(jax.random.key(seed), 6)
    return {
        "vectors": centred(seeds[0], (NH, K), 1.0, 6.0, ((0, 16), (1, 2)), jnp.float32),
        "blocks": draw_blocks(jax.random.fold_in(seeds[5], 71), 0),
        "block_row": draw_block_row(jax.random.fold_in(seeds[5], 71), 0),
        "block_col": draw_block_col(jax.random.fold_in(seeds[5], 71), 0),
        "block_count": draw_block_count(jax.random.fold_in(seeds[5], 71), 0),
    }


step_rate = 0.25
exact_mode = lax.Precision.HIGHEST

def hessian_apply(rounded, blocks, block_row, block_col, block_count):
    nblock = NH // BS
    ndevice = NH // (2 * BS)
    block_tiles = rounded.astype(jnp.float32).reshape(nblock, BS, K)

    def per_device(totals, device):
        slot_start = device * BLK_DEV
        chosen = lax.dynamic_slice_in_dim(blocks, slot_start, BLK_DEV, 0).astype(jnp.float32)
        row_ids = lax.dynamic_slice_in_dim(block_row, slot_start, BLK_DEV, 0)
        col_ids = lax.dynamic_slice_in_dim(block_col, slot_start, BLK_DEV, 0)
        used_slots = lax.dynamic_index_in_dim(block_count, device, 0, keepdims=False)
        alive_mask = (jnp.arange(BLK_DEV, dtype=jnp.int32) < used_slots).astype(jnp.float32)
        weight = (jnp.where(row_ids == col_ids, 0.5, 1.0).astype(jnp.float32) * alive_mask)[:, None, None]
        direct = jnp.einsum('sab,sbk->sak', chosen, block_tiles[col_ids], precision=exact_mode) * weight
        mirror = jnp.einsum('sba,sbk->sak', chosen, block_tiles[row_ids], precision=exact_mode) * weight
        totals = totals.at[row_ids].add(direct).at[col_ids].add(mirror)
        return (totals, None)
    start_total = jnp.zeros((nblock, BS, K), jnp.float32)
    totals, _unused = lax.scan(per_device, start_total, jnp.arange(ndevice, dtype=jnp.int32))
    return totals.reshape(NH, K)

def reference(vectors, blocks, block_row, block_col, block_count):
    current = vectors
    residual = vectors
    for iteration in range(STEPS):
        rounded = current.astype(jnp.bfloat16)
        applied = hessian_apply(rounded, blocks, block_row, block_col, block_count)
        rayleigh = jnp.dot(current.T.astype(jnp.float32), applied.astype(jnp.float32), precision=exact_mode, preferred_element_type=jnp.float32) / NH
        residual = applied - jnp.dot(current.astype(jnp.float32), rayleigh.astype(jnp.float32), precision=exact_mode, preferred_element_type=jnp.float32)
        update = current - step_rate * residual
        gram_matrix = jnp.dot(update.T.astype(jnp.float32), update.astype(jnp.float32), precision=exact_mode, preferred_element_type=jnp.float32) / NH
        factor = jnp.linalg.cholesky(gram_matrix)
        current = lax.linalg.triangular_solve(factor, update, left_side=False, lower=True, transpose_a=True)
    return (current, residual)
```

```python
import jax
import jax.numpy as jnp
from jax import lax
from jax.experimental import pallas as pl
from jax.experimental.pallas import tpu as pltpu
from jax.sharding import PartitionSpec as P

STEPS = 2
STEP_RATE = 0.25
GROUP = 8
REACH = 4

f32, bf16 = jnp.float32, jnp.bfloat16
VMEM, SMEM = pltpu.VMEM, pltpu.SMEM


def dot_nn(a, b):
    return lax.dot_general(a, b, (((1,), (0,)), ((), ())), preferred_element_type=f32)


def dot_nt(a, b):
    return lax.dot_general(a, b, (((1,), (1,)), ((), ())), preferred_element_type=f32)


def split(a):
    high = a.astype(bf16)
    return high, (a - high.astype(f32)).astype(bf16)


def dot3(dot, a, b):
    (ah, al), (bh, bl) = a, b
    return dot(ah, bh) + (dot(ah, bl) + dot(al, bh))


def call(kernel, out, args, scratch=(), smem=0, flops=1 << 28):
    moved = sum(a.size * a.dtype.itemsize for a in args) + sum(o.size * o.dtype.itemsize for o in out)
    return pl.pallas_call(
        kernel,
        out_shape=out,
        in_specs=[pl.BlockSpec(memory_space=SMEM)] * smem + [pl.BlockSpec(memory_space=VMEM)] * (len(args) - smem),
        out_specs=[pl.BlockSpec(memory_space=VMEM)] * len(out),
        scratch_shapes=list(scratch),
        compiler_params=pltpu.CompilerParams(vmem_limit_bytes=48 << 20),
        cost_estimate=pl.CostEstimate(flops=flops, bytes_accessed=moved, transcendentals=0),
    )(*args)


def shape(dtype, *dims):
    return jax.ShapeDtypeStruct(dims, dtype)


def pack_kernel(vectors, columns, chunk):
    size = chunk.shape[2]
    for t in range(chunk.shape[0]):
        turned = vectors[pl.ds(t * size, size), :].T
        columns[:, pl.ds(t * size, size)] = turned
        chunk[t] = turned.astype(bf16)


def apply_kernel(meta, rows, cols, *refs):
    pieces, tiles = refs[: 2 * REACH], refs[2 * REACH]
    same, cross = refs[2 * REACH + 1 : 3 * REACH + 1], refs[3 * REACH + 1 : 4 * REACH + 1]
    everything, window, total, sems = refs[4 * REACH + 1 :]
    step = pl.program_id(0)
    used, start, odd = meta[0], meta[1], meta[2]

    @pl.when(step == 0)
    def _():
        copies = [
            pltpu.make_async_copy(piece, window.at[pl.ds(2 * s, 2)], sems.at[s]) for s, piece in enumerate(pieces)
        ]
        for copy in copies:
            copy.start()
        total[...] = jnp.zeros_like(total)
        for copy in copies:
            copy.wait()

    def place(tile):
        w = tile - start
        return (REACH - 1 - w // 4) * 4 + 2 * (((w % 4) // 2) ^ odd) + w % 2

    @pl.when(step * GROUP < used)
    def _():
        found = []
        for k in range(GROUP):
            slot = step * GROUP + k
            row, col = rows[slot], cols[slot]
            weight = jnp.where(row == col, 0.5, 1.0).astype(f32)
            r, c = place(row), place(col)
            tile = jnp.where(slot < used, tiles[k], jnp.zeros_like(tiles[k]))
            found.append((r, dot_nt(window[c], tile), weight))
            found.append((c, dot_nn(window[r], tile), weight))
        for at, part, weight in found:
            total[at] += part * weight

    @pl.when(step == pl.num_programs(0) - 1)
    def _():
        for d in range(REACH):
            for s in range(2):
                same[d][s] = total[4 * d + s]
                cross[d][s] = total[4 * d + 2 + s].astype(bf16)
        everything[...] = total[...].astype(bf16)


def apply_tiles(pieces, blocks, rows, cols, meta):
    slots, size, _ = blocks.shape
    width = pieces[0].shape[1]

    def tile_map(i, meta, rows, cols):
        last = jnp.maximum((meta[0] + GROUP - 1) // GROUP - 1, 0)
        return (jnp.minimum(i, last), 0, 0)

    def whole(dims):
        return pl.BlockSpec(dims, lambda i, *_: (0,) * len(dims))

    segment, window = (2, width, size), (4 * REACH, width, size)
    out = pl.pallas_call(
        apply_kernel,
        grid_spec=pltpu.PrefetchScalarGridSpec(
            num_scalar_prefetch=3,
            grid=(slots // GROUP,),
            in_specs=[pl.BlockSpec(memory_space=pl.ANY)] * (2 * REACH)
            + [pl.BlockSpec((GROUP, size, size), tile_map)],
            out_specs=[whole(segment)] * (2 * REACH) + [whole(window)],
            scratch_shapes=[VMEM(window, bf16), VMEM(window, f32), pltpu.SemaphoreType.DMA((2 * REACH,))],
        ),
        out_shape=[shape(f32, *segment)] * REACH + [shape(bf16, *segment)] * REACH + [shape(bf16, *window)],
        compiler_params=pltpu.CompilerParams(vmem_limit_bytes=48 << 20),
        cost_estimate=pl.CostEstimate(flops=4 << 30, bytes_accessed=16 << 20, transcendentals=0),
    )(meta, rows, cols, *pieces, blocks)
    return out[:REACH], out[REACH : 2 * REACH], out[2 * REACH]


def inner_kernel(*refs):
    pieces, mine, theirs, out = refs[: 2 * REACH], refs[2 * REACH], refs[2 * REACH + 1], refs[-1]
    size = out.shape[1]
    own = jnp.zeros((size, size), f32)
    other = jnp.zeros((size, size), f32)
    for s, piece in enumerate(pieces):
        for t in range(2):
            own += dot_nt(mine[2 * s + t], piece[t])
            other += dot_nt(piece[t], theirs[2 * s + t])
    out[pl.ds(0, size), :] = own
    out[pl.ds(size, size), :] = other


def update_kernel(rows_total, x, x_other, kept, near, far1, far2, far3, inner, update, *residual):
    width, count = x.shape
    size = kept.shape[2]
    own = split(inner[pl.ds(0, width), :] / rows_total)
    other = split(inner[pl.ds(width, width), :] / rows_total)
    for t in range(count // size):
        part = pl.ds(t * size, size)
        applied = kept[t] + near[t].astype(f32)
        applied += far1[t].astype(f32) + far2[t].astype(f32) + far3[t].astype(f32)
        now = x[:, part]
        rest = applied - (dot3(dot_nn, own, split(now)) + dot3(dot_nn, other, split(x_other[:, part])))
        update[:, part] = now - STEP_RATE * rest
        if residual:
            residual[0][part, :] = rest.T


def gram_kernel(core, mine, theirs, out):
    width = mine.shape[0]
    half = width // 2
    own, other = split(mine[...]), split(theirs[...])
    out[pl.ds(0, width), :] = dot3(dot_nt, own, own)
    ahead = core[0] == 0
    high = jnp.where(ahead, theirs[pl.ds(0, half), :], mine[pl.ds(half, half), :])
    low = [jnp.where(ahead, a, b) for a, b in zip(own, other)]
    out[pl.ds(width, half), :] = dot3(dot_nt, split(high), low)


def inverse_factor(g, w, high, low):
    n = g.shape[0]
    at_row = lax.broadcasted_iota(jnp.int32, (n, n), 0)
    at_col = lax.broadcasted_iota(jnp.int32, (n, n), 1)
    eye = jnp.where(at_row == at_col, 1.0, 0.0).astype(f32)
    diagonal = eye * g[...]
    by_row = lax.rsqrt(jnp.sum(diagonal, axis=1, keepdims=True))
    by_col = lax.rsqrt(jnp.sum(diagonal, axis=0, keepdims=True))
    unit = g[...] * by_row * by_col
    rounded = unit.astype(bf16)
    square = dot_nn(rounded, rounded).astype(bf16)
    fourth = dot_nn(square, square)
    scale = 1.9 / jnp.sqrt(jnp.sqrt(jnp.sqrt(jnp.sum(fourth * fourth, keepdims=True))))
    scaled = unit * scale
    high[...], low[...] = split(scaled)

    def lower(e):
        return jnp.where(at_row > at_col, e, 0.5 * eye * e)

    p = lower(scaled - eye)
    pb = p.astype(bf16)
    w[...] = eye - p + dot_nn(pb, pb)

    def improve(e):
        p = lower(e)
        pb = p.astype(bf16)
        first = dot_nn(pb, w[...].astype(bf16))
        w[...] = w[...] - first + dot_nn(pb, first.astype(bf16))
        return jnp.sqrt(jnp.sum(p * p))

    def rough(state):
        wb = w[...].astype(bf16)
        e = dot_nt(dot_nn(wb, high[...]).astype(bf16), wb) - eye
        return state[0] + 1, improve(e)

    def fine(state):
        ws = split(w[...])
        e = dot3(dot_nt, split(dot3(dot_nn, ws, (high[...], low[...]))), ws) - eye
        return state[0] + 1, improve(e)

    def until(bound, most):
        return lambda state: (state[0] < most) & jnp.logical_not(state[1] <= bound)

    lax.while_loop(until(0.4, 16), rough, (0, jnp.float32(1e9)))
    _, error = lax.while_loop(until(2e-3, 6), fine, (0, jnp.float32(1e9)))
    done = error <= 2e-3

    @pl.when(done)
    def _():
        w[...] = w[...] * (by_col * jnp.sqrt(scale))

    @pl.when(jnp.logical_not(done))
    def _():
        w[...] = eye

        def eliminate(k, carry):
            lane = lax.broadcasted_iota(jnp.int32, (1, n), 1)
            below = lax.broadcasted_iota(jnp.int32, (n, 1), 0)
            row = g[pl.ds(k, 1), :]
            pivot = jnp.sum(jnp.where(lane == k, row, 0.0), axis=1, keepdims=True)
            column = jnp.sum(jnp.where(at_col == k, g[...], 0.0), axis=1, keepdims=True)
            ratio = jnp.where(below > k, column / pivot, 0.0)
            solved = w[pl.ds(k, 1), :]
            g[...] = g[...] - ratio * row
            w[...] = w[...] - ratio * solved
            w[pl.ds(k, 1), :] = solved * lax.rsqrt(pivot)
            return carry

        lax.fori_loop(0, n, eliminate, 0)


def factor_kernel(rows_total, last, core, mine, theirs, gram, gram_other, *refs):
    out, (g, w, high, low, update) = refs[:-5], refs[-5:]
    width = mine.shape[0]
    half = width // 2
    ahead = core[0] == 0
    first = jnp.where(ahead, gram[...], gram_other[...]) / rows_total
    second = jnp.where(ahead, gram_other[...], gram[...]) / rows_total
    g[pl.ds(0, width), pl.ds(0, width)] = first[:width]
    g[pl.ds(width, width), pl.ds(width, width)] = second[:width]
    below = jnp.concatenate([first[width:], second[width:]], axis=0)
    g[pl.ds(width, width), pl.ds(0, width)] = below
    g[pl.ds(0, width), pl.ds(width, width)] = below.T
    inverse_factor(g, w, high, low)
    start = pl.multiple_of(core[0] * width, width)
    update[pl.ds(start, width), :] = mine[...]
    update[pl.ds(width - start, width), :] = theirs[...]
    mix = split(w[pl.ds(start, width), :])
    size = width
    for t in range(mine.shape[1] // size):
        part = pl.ds(t * size, size)
        solved = dot3(dot_nn, mix, split(update[:, part]))
        if last:
            out[0][part, :] = solved.T
        else:
            out[0][:, part] = solved
            out[1][t] = solved.astype(bf16)


def swap_cores(a):
    return lax.ppermute(a, "vec", [(0, 1), (1, 0)])


def flip(a, mask):
    return lax.ppermute(a, "patch", [(i, i ^ mask) for i in range(lax.axis_size("patch"))])


def shift(a, pairs):
    devices = range(lax.axis_size("patch"))
    return lax.ppermute(a, "patch", [(i - 2 * pairs, i) for i in devices if i - 2 * pairs in devices])


def summed(a):
    position = lax.axis_index("patch")
    left, stride, stages = lax.axis_size("patch"), 1, []
    while left > 1:
        radix = 4 if left % 4 == 0 else 2
        stages.append((radix, stride))
        left, stride = left // radix, stride * radix
    for radix, stride in stages:
        place = (position // stride) % radix
        parts = a.reshape(radix, a.shape[0] // radix, a.shape[1])
        a = lax.dynamic_index_in_dim(parts, place, 0, False)
        for m in range(1, radix):
            a = a + flip(lax.dynamic_index_in_dim(parts, place ^ m, 0, False), m * stride)
    for radix, stride in stages[::-1]:
        place = (position // stride) % radix
        parts = jnp.stack([a] + [flip(a, m * stride) for m in range(1, radix)])
        a = parts[jnp.arange(radix) ^ place].reshape(radix * a.shape[0], a.shape[1])
    return a


def shards(vectors, blocks, block_row, block_col, block_count):
    count, width = vectors.shape
    size = blocks.shape[1]
    rows_total = float(count * lax.axis_size("patch"))
    position = lax.axis_index("patch")
    odd = position % 2
    meta = jnp.stack([block_count[0], 2 * (position - odd) - 4 * (REACH - 1), odd]).astype(jnp.int32)
    core = lax.axis_index("vec").astype(jnp.int32).reshape(1)
    flat, chunk = shape(f32, width, count), shape(bf16, count // size, width, size)
    x, u = call(pack_kernel, [flat, chunk], [vectors])
    for step in range(STEPS):
        last = step == STEPS - 1
        reached = [u] + [shift(u, d) for d in range(1, REACH)]
        pieces = [a for own in reached for a in (own, flip(own, 1))]
        x_other = swap_cores(x)
        same, cross, everything = apply_tiles(pieces, blocks, block_row, block_col, meta)
        joined = [None] * REACH
        for d in range(REACH - 1, 0, -1):
            joined[d] = shift((same[d] + flip(cross[d], 1).astype(f32)).astype(bf16), -d)
        joined[0] = flip(cross[0], 1)
        (inner,) = call(inner_kernel, [shape(f32, 2 * width, width)], pieces + [everything, swap_cores(everything)])
        inner = summed(inner)
        out = [flat] + ([shape(f32, count, width)] if last else [])
        update, *residual = call(
            lambda *refs: update_kernel(rows_total, *refs), out, [x, x_other, same[0], *joined, inner]
        )
        update_other = swap_cores(update)
        (gram,) = call(
            gram_kernel, [shape(f32, width + width // 2, width)], [core, update, update_other], smem=1
        )
        gram = summed(gram)
        full = (2 * width, 2 * width)
        out = call(
            lambda *refs: factor_kernel(rows_total, last, *refs),
            [shape(f32, count, width)] if last else [flat, chunk],
            [core, update, update_other, gram, swap_cores(gram)],
            scratch=[VMEM(full, f32), VMEM(full, f32), VMEM(full, bf16), VMEM(full, bf16), VMEM((2 * width, count), f32)],
            smem=1,
            flops=16 << 30,
        )
        if last:
            return out[0], residual[0]
        x, u = out


def solution(mesh):
    in_specs = (P("patch", "vec"), P("patch", None, None), P("patch"), P("patch"), P("patch"))
    out_specs = (P("patch", "vec"), P("patch", "vec"))
    return jax.shard_map(shards, mesh=mesh, in_specs=in_specs, out_specs=out_specs, check_vma=False)
```

```python
import jax
import jax.numpy as jnp
from jax import lax
from jax.experimental import pallas as pl
from jax.experimental.pallas import tpu as pltpu
from jax.sharding import PartitionSpec as P

STEPS = 2
STEP_RATE = 0.25
GROUP = 8
REACH = 4

f32, bf16 = jnp.float32, jnp.bfloat16
VMEM, SMEM = pltpu.VMEM, pltpu.SMEM


def dot_nn(a, b):
    return lax.dot_general(a, b, (((1,), (0,)), ((), ())), preferred_element_type=f32)


def dot_nt(a, b):
    return lax.dot_general(a, b, (((1,), (1,)), ((), ())), preferred_element_type=f32)


def split(a):
    high = a.astype(bf16)
    return high, (a - high.astype(f32)).astype(bf16)


def dot3(dot, a, b):
    (ah, al), (bh, bl) = a, b
    return dot(ah, bh) + (dot(ah, bl) + dot(al, bh))


def call(kernel, out, args, scratch=(), smem=0, flops=1 << 28, vmem=16):
    moved = sum(a.size * a.dtype.itemsize for a in args) + sum(o.size * o.dtype.itemsize for o in out)
    return pl.pallas_call(
        kernel,
        out_shape=out,
        in_specs=[pl.BlockSpec(memory_space=SMEM)] * smem + [pl.BlockSpec(memory_space=VMEM)] * (len(args) - smem),
        out_specs=[pl.BlockSpec(memory_space=VMEM)] * len(out),
        scratch_shapes=list(scratch),
        compiler_params=pltpu.CompilerParams(vmem_limit_bytes=vmem << 20),
        cost_estimate=pl.CostEstimate(flops=flops, bytes_accessed=moved, transcendentals=0),
    )(*args)


def shape(dtype, *dims):
    return jax.ShapeDtypeStruct(dims, dtype)


def pack_kernel(vectors, columns, chunk):
    size = chunk.shape[2]
    for t in range(chunk.shape[0]):
        turned = vectors[pl.ds(t * size, size), :].T
        columns[:, pl.ds(t * size, size)] = turned
        chunk[t] = turned.astype(bf16)


def apply_kernel(meta, rows, cols, *refs):
    pieces, tiles = refs[: 2 * REACH], refs[2 * REACH]
    same, cross = refs[2 * REACH + 1 : 3 * REACH + 1], refs[3 * REACH + 1 : 4 * REACH + 1]
    everything, window, total, sems = refs[4 * REACH + 1 :]
    step = pl.program_id(0)
    used, start, odd, pair_odd = meta[0], meta[1], meta[2], meta[3]

    @pl.when(step == 0)
    def _():
        copies = [
            pltpu.make_async_copy(piece, window.at[pl.ds(2 * s, 2)], sems.at[s]) for s, piece in enumerate(pieces)
        ]
        for copy in copies:
            copy.start()
        total[...] = jnp.zeros_like(total)
        for copy in copies:
            copy.wait()

    def place(tile):
        w = tile - start
        back = REACH - 1 - w // 4
        role = jnp.where(back % 2 == 1, 2 + ((back // 2) ^ pair_odd ^ 1), back // 2)
        return role * 4 + 2 * (((w % 4) // 2) ^ odd) + w % 2

    @pl.when(step * GROUP < used)
    def _():
        found = []
        for k in range(GROUP):
            slot = step * GROUP + k
            row, col = rows[slot], cols[slot]
            weight = jnp.where(row == col, 0.5, 1.0).astype(f32)
            r, c = place(row), place(col)
            tile = jnp.where(slot < used, tiles[k], jnp.zeros_like(tiles[k]))
            found.append((r, dot_nt(window[c], tile), weight))
            found.append((c, dot_nn(window[r], tile), weight))
        for at, part, weight in found:
            total[at] += part * weight

    @pl.when(step == pl.num_programs(0) - 1)
    def _():
        for d in range(REACH):
            for s in range(2):
                same[d][s] = total[4 * d + s]
                cross[d][s] = total[4 * d + 2 + s].astype(bf16)
        everything[...] = total[...].astype(bf16)


def apply_tiles(pieces, blocks, rows, cols, meta):
    slots, size, _ = blocks.shape
    width = pieces[0].shape[1]

    def tile_map(i, meta, rows, cols):
        last = jnp.maximum((meta[0] + GROUP - 1) // GROUP - 1, 0)
        return (jnp.minimum(i, last), 0, 0)

    def whole(dims):
        return pl.BlockSpec(dims, lambda i, *_: (0,) * len(dims))

    segment, window = (2, width, size), (4 * REACH, width, size)
    out = pl.pallas_call(
        apply_kernel,
        grid_spec=pltpu.PrefetchScalarGridSpec(
            num_scalar_prefetch=3,
            grid=(slots // GROUP,),
            in_specs=[pl.BlockSpec(memory_space=pl.ANY)] * (2 * REACH)
            + [pl.BlockSpec((GROUP, size, size), tile_map)],
            out_specs=[whole(segment)] * (2 * REACH) + [whole(window)],
            scratch_shapes=[VMEM(window, bf16), VMEM(window, f32), pltpu.SemaphoreType.DMA((2 * REACH,))],
        ),
        out_shape=[shape(f32, *segment)] * REACH + [shape(bf16, *segment)] * REACH + [shape(bf16, *window)],
        compiler_params=pltpu.CompilerParams(vmem_limit_bytes=32 << 20),
        cost_estimate=pl.CostEstimate(flops=4 << 30, bytes_accessed=16 << 20, transcendentals=0),
    )(meta, rows, cols, *pieces, blocks)
    return out[:REACH], out[REACH : 2 * REACH], out[2 * REACH]


def inner_kernel(*refs):
    pieces, mine, theirs, out = refs[: 2 * REACH], refs[2 * REACH], refs[2 * REACH + 1], refs[-1]
    size = out.shape[1]
    own = jnp.zeros((size, size), f32)
    other = jnp.zeros((size, size), f32)
    for s, piece in enumerate(pieces):
        for t in range(2):
            own += dot_nt(mine[2 * s + t], piece[t])
            other += dot_nt(piece[t], theirs[2 * s + t])
    out[pl.ds(0, size), :] = own
    out[pl.ds(size, size), :] = other


def update_kernel(rows_total, x, x_other, kept, near, far, two, inner, update, *residual):
    width, count = x.shape
    size = kept.shape[2]
    own = split(inner[pl.ds(0, width), :] / rows_total)
    other = split(inner[pl.ds(width, width), :] / rows_total)
    for t in range(count // size):
        part = pl.ds(t * size, size)
        applied = kept[t] + near[t].astype(f32) + (far[t].astype(f32) + two[t].astype(f32))
        now = x[:, part]
        rest = applied - (dot3(dot_nn, own, split(now)) + dot3(dot_nn, other, split(x_other[:, part])))
        update[:, part] = now - STEP_RATE * rest
        if residual:
            residual[0][part, :] = rest.T


def gram_kernel(core, mine, theirs, out):
    width = mine.shape[0]
    half = width // 2
    own, other = split(mine[...]), split(theirs[...])
    out[pl.ds(0, width), :] = dot3(dot_nt, own, own)
    ahead = core[0] == 0
    high = jnp.where(ahead, theirs[pl.ds(0, half), :], mine[pl.ds(half, half), :])
    low = [jnp.where(ahead, a, b) for a, b in zip(own, other)]
    out[pl.ds(width, half), :] = dot3(dot_nt, split(high), low)


def inverse_factor(g, w, high, low):
    n = g.shape[0]
    at_row = lax.broadcasted_iota(jnp.int32, (n, n), 0)
    at_col = lax.broadcasted_iota(jnp.int32, (n, n), 1)
    eye = jnp.where(at_row == at_col, 1.0, 0.0).astype(f32)
    diagonal = eye * g[...]
    by_row = lax.rsqrt(jnp.sum(diagonal, axis=1, keepdims=True))
    by_col = lax.rsqrt(jnp.sum(diagonal, axis=0, keepdims=True))
    unit = g[...] * by_row * by_col
    rounded = unit.astype(bf16)
    square = dot_nn(rounded, rounded).astype(bf16)
    fourth = dot_nn(square, square)
    scale = 1.9 / jnp.sqrt(jnp.sqrt(jnp.sqrt(jnp.sum(fourth * fourth, keepdims=True))))
    scaled = unit * scale
    high[...], low[...] = split(scaled)

    def lower(e):
        return jnp.where(at_row > at_col, e, 0.5 * eye * e)

    p = lower(scaled - eye)
    pb = p.astype(bf16)
    w[...] = eye - p + dot_nn(pb, pb)

    def improve(e):
        p = lower(e)
        pb = p.astype(bf16)
        first = dot_nn(pb, w[...].astype(bf16))
        w[...] = w[...] - first + dot_nn(pb, first.astype(bf16))
        return jnp.sqrt(jnp.sum(p * p))

    def rough(state):
        wb = w[...].astype(bf16)
        e = dot_nt(dot_nn(wb, high[...]).astype(bf16), wb) - eye
        return state[0] + 1, improve(e)

    def fine(state):
        ws = split(w[...])
        e = dot3(dot_nt, split(dot3(dot_nn, ws, (high[...], low[...]))), ws) - eye
        return state[0] + 1, improve(e)

    def until(bound, most):
        return lambda state: (state[0] < most) & jnp.logical_not(state[1] <= bound)

    lax.while_loop(until(0.4, 16), rough, (0, jnp.float32(1e9)))
    _, error = lax.while_loop(until(2e-3, 6), fine, (0, jnp.float32(1e9)))
    done = error <= 2e-3

    @pl.when(done)
    def _():
        w[...] = w[...] * (by_col * jnp.sqrt(scale))

    @pl.when(jnp.logical_not(done))
    def _():
        w[...] = eye

        def eliminate(k, carry):
            lane = lax.broadcasted_iota(jnp.int32, (1, n), 1)
            below = lax.broadcasted_iota(jnp.int32, (n, 1), 0)
            row = g[pl.ds(k, 1), :]
            pivot = jnp.sum(jnp.where(lane == k, row, 0.0), axis=1, keepdims=True)
            column = jnp.sum(jnp.where(at_col == k, g[...], 0.0), axis=1, keepdims=True)
            ratio = jnp.where(below > k, column / pivot, 0.0)
            solved = w[pl.ds(k, 1), :]
            g[...] = g[...] - ratio * row
            w[...] = w[...] - ratio * solved
            w[pl.ds(k, 1), :] = solved * lax.rsqrt(pivot)
            return carry

        lax.fori_loop(0, n, eliminate, 0)


def factor_kernel(rows_total, last, core, mine, theirs, gram, gram_other, *refs):
    out, (g, w, high, low, update) = refs[:-5], refs[-5:]
    width = mine.shape[0]
    half = width // 2
    ahead = core[0] == 0
    first = jnp.where(ahead, gram[...], gram_other[...]) / rows_total
    second = jnp.where(ahead, gram_other[...], gram[...]) / rows_total
    g[pl.ds(0, width), pl.ds(0, width)] = first[:width]
    g[pl.ds(width, width), pl.ds(width, width)] = second[:width]
    below = jnp.concatenate([first[width:], second[width:]], axis=0)
    g[pl.ds(width, width), pl.ds(0, width)] = below
    g[pl.ds(0, width), pl.ds(width, width)] = below.T
    inverse_factor(g, w, high, low)
    start = pl.multiple_of(core[0] * width, width)
    update[pl.ds(start, width), :] = mine[...]
    update[pl.ds(width - start, width), :] = theirs[...]
    mix = split(w[pl.ds(start, width), :])
    size = width
    for t in range(mine.shape[1] // size):
        part = pl.ds(t * size, size)
        solved = dot3(dot_nn, mix, split(update[:, part]))
        if last:
            out[0][part, :] = solved.T
        else:
            out[0][:, part] = solved
            out[1][t] = solved.astype(bf16)


def swap_cores(a):
    return lax.ppermute(a, "vec", [(0, 1), (1, 0)])


def flip(a, mask):
    return lax.ppermute(a, "patch", [(i, i ^ mask) for i in range(lax.axis_size("patch"))])


def shift(a, pairs):
    devices = range(lax.axis_size("patch"))
    return lax.ppermute(a, "patch", [(i - 2 * pairs, i) for i in devices if i - 2 * pairs in devices])


def stride(a, back=False):
    devices = range(lax.axis_size("patch"))
    route = [(i - (2 if i // 2 % 2 else 6), i) for i in devices]
    return lax.ppermute(a, "patch", [(d, s) if back else (s, d) for s, d in route if s in devices])


def together(*arrays):
    return lax.optimization_barrier(arrays)


def reach(u):
    two = shift(u, 2)
    own = flip(u, 1)
    far = stride(u)
    two, own = together(two, own)
    side, two_x = flip(two, 2), flip(two, 1)
    far, two_x = together(far, two_x)
    return [u, own, two, two_x, far, flip(far, 1), side, flip(side, 1)]


def place_order(parts, place):
    radix = len(parts)
    bit = 1
    while bit < radix:
        swapped = [parts[j ^ bit] for j in range(radix)]
        parts = [jnp.where(place & bit, b, a) for a, b in zip(parts, swapped)]
        bit *= 2
    return parts


def summed(a, gates=()):
    position = lax.axis_index("patch")
    left, step, stages = lax.axis_size("patch"), 1, []
    while left > 1:
        radix = 4 if left % 4 == 0 else 2
        stages.append((radix, step))
        left, step = left // radix, step * radix
    gates = list(gates)

    def gated(x):
        return together(x, *gates.pop(0))[0] if gates else x

    for radix, step in stages[:-1]:
        place = (position // step) % radix
        parts = gated(a).reshape(radix, a.shape[0] // radix, a.shape[1])
        a = lax.dynamic_index_in_dim(parts, place, 0, False)
        for m in range(1, radix):
            a = a + flip(lax.dynamic_index_in_dim(parts, place ^ m, 0, False), m * step)
    radix, step = stages[-1]
    a = gated(a)
    a = sum([flip(a, m * step) for m in range(1, radix)], a)
    for radix, step in stages[-2::-1]:
        place = (position // step) % radix
        a = gated(a)
        parts = place_order([a] + [flip(a, m * step) for m in range(1, radix)], place)
        a = jnp.concatenate(parts, axis=0)
    return a


def shards(vectors, blocks, block_row, block_col, block_count):
    count, width = vectors.shape
    size = blocks.shape[1]
    rows_total = float(count * lax.axis_size("patch"))
    position = lax.axis_index("patch")
    odd = position % 2
    meta = jnp.stack([block_count[0], 2 * (position - odd) - 4 * (REACH - 1), odd, position // 2 % 2]).astype(jnp.int32)
    core = lax.axis_index("vec").astype(jnp.int32).reshape(1)
    flat, chunk = shape(f32, width, count), shape(bf16, count // size, width, size)
    x, u = call(pack_kernel, [flat, chunk], [vectors])
    for step in range(STEPS):
        last = step == STEPS - 1
        pieces = reach(u)
        x_other = swap_cores(x)
        same, cross, everything = apply_tiles(pieces, blocks, block_row, block_col, meta)
        side_x, two_x = flip(cross[3], 1), flip(cross[1], 1)
        side = flip((same[3] + side_x.astype(f32)).astype(bf16), 2)
        theirs, _ = together(swap_cores(everything), side_x)
        (inner,) = call(inner_kernel, [shape(f32, 2 * width, width)], pieces + [everything, theirs])
        far_x, own_x = flip(cross[2], 1), flip(cross[0], 1)
        far = (same[2] + far_x.astype(f32)).astype(bf16)
        two = (same[1] + (two_x.astype(f32) + side.astype(f32))).astype(bf16)
        joined = [own_x, stride(far, True), shift(two, -2)]
        inner = summed(inner, [(two_x,), (far, two, own_x), joined[1:]])
        out = [flat] + ([shape(f32, count, width)] if last else [])
        update, *residual = call(
            lambda *refs: update_kernel(rows_total, *refs), out, [x, x_other, same[0], *joined, inner]
        )
        update_other = swap_cores(update)
        (gram,) = call(
            gram_kernel, [shape(f32, width + width // 2, width)], [core, update, update_other], smem=1
        )
        gram = summed(gram)
        full = (2 * width, 2 * width)
        out = call(
            lambda *refs: factor_kernel(rows_total, last, *refs),
            [shape(f32, count, width)] if last else [flat, chunk],
            [core, update, update_other, gram, swap_cores(gram)],
            scratch=[VMEM(full, f32), VMEM(full, f32), VMEM(full, bf16), VMEM(full, bf16), VMEM((2 * width, count), f32)],
            smem=1,
            flops=16 << 30,
            vmem=40,
        )
        if last:
            return out[0], residual[0]
        x, u = out


def solution(mesh):
    in_specs = (P("patch", "vec"), P("patch", None, None), P("patch"), P("patch"), P("patch"))
    out_specs = (P("patch", "vec"), P("patch", "vec"))
    return jax.shard_map(shards, mesh=mesh, in_specs=in_specs, out_specs=out_specs, check_vma=False)
```

```python
import jax
import jax.numpy as jnp
from jax import lax
from jax.experimental import pallas as pl
from jax.experimental.pallas import tpu as pltpu
from jax.sharding import PartitionSpec as P

STEPS = 2
STEP_RATE = 0.25
GROUP = 8
REACH = 4

f32, bf16 = jnp.float32, jnp.bfloat16
SEGMENT_KINDS = (f32, bf16, f32, f32, f32, bf16, bf16, bf16)
VMEM, SMEM = pltpu.VMEM, pltpu.SMEM


def dot_nn(a, b):
    return lax.dot_general(a, b, (((1,), (0,)), ((), ())), preferred_element_type=f32)


def dot_nt(a, b):
    return lax.dot_general(a, b, (((1,), (1,)), ((), ())), preferred_element_type=f32)


def split(a):
    high = a.astype(bf16)
    return high, (a - high.astype(f32)).astype(bf16)


def dot3(dot, a, b):
    (ah, al), (bh, bl) = a, b
    return dot(ah, bh) + (dot(ah, bl) + dot(al, bh))


def call(kernel, out, args, scratch=(), smem=0, flops=1 << 28, vmem=16):
    moved = sum(a.size * a.dtype.itemsize for a in args) + sum(o.size * o.dtype.itemsize for o in out)
    return pl.pallas_call(
        kernel,
        out_shape=out,
        in_specs=[pl.BlockSpec(memory_space=SMEM)] * smem + [pl.BlockSpec(memory_space=VMEM)] * (len(args) - smem),
        out_specs=[pl.BlockSpec(memory_space=VMEM)] * len(out),
        scratch_shapes=list(scratch),
        compiler_params=pltpu.CompilerParams(vmem_limit_bytes=vmem << 20),
        cost_estimate=pl.CostEstimate(flops=flops, bytes_accessed=moved, transcendentals=0),
    )(*args)


def shape(dtype, *dims):
    return jax.ShapeDtypeStruct(dims, dtype)


def pack_kernel(vectors, columns, chunk):
    size = chunk.shape[2]
    for t in range(chunk.shape[0]):
        turned = vectors[pl.ds(t * size, size), :].T
        columns[:, pl.ds(t * size, size)] = turned
        chunk[t] = turned.astype(bf16)


def apply_kernel(meta, rows, cols, *refs):
    pieces, tiles = refs[: 2 * REACH], refs[2 * REACH]
    out = refs[2 * REACH + 1 : 4 * REACH + 1]
    everything, window, total, sems = refs[4 * REACH + 1 :]
    step = pl.program_id(0)
    used, start, odd, pair_odd = meta[0], meta[1], meta[2], meta[3]

    @pl.when(step == 0)
    def _():
        copies = [
            pltpu.make_async_copy(piece, window.at[pl.ds(2 * s, 2)], sems.at[s]) for s, piece in enumerate(pieces)
        ]
        for copy in copies:
            copy.start()
        total[...] = jnp.zeros_like(total)
        for copy in copies:
            copy.wait()

    def place(tile):
        w = tile - start
        back = REACH - 1 - w // 4
        role = jnp.where(back % 2 == 1, 2 + ((back // 2) ^ pair_odd ^ 1), back // 2)
        return role * 4 + 2 * (((w % 4) // 2) ^ odd) + w % 2

    @pl.when(step * GROUP < used)
    def _():
        found = []
        for k in range(GROUP):
            slot = step * GROUP + k
            row, col = rows[slot], cols[slot]
            weight = jnp.where(row == col, 0.5, 1.0).astype(f32)
            r, c = place(row), place(col)
            tile = jnp.where(slot < used, tiles[k], jnp.zeros_like(tiles[k]))
            found.append((r, dot_nt(window[c], tile), weight))
            found.append((c, dot_nn(window[r], tile), weight))
        for at, part, weight in found:
            total[at] += part * weight

    @pl.when(step == pl.num_programs(0) - 1)
    def _():
        for s, segment in enumerate(out):
            segment[...] = total[pl.ds(2 * s, 2)].astype(segment.dtype)
        everything[...] = total[...].astype(bf16)


def apply_tiles(pieces, blocks, rows, cols, meta):
    slots, size, _ = blocks.shape
    width = pieces[0].shape[1]

    def tile_map(i, meta, rows, cols):
        last = jnp.maximum((meta[0] + GROUP - 1) // GROUP - 1, 0)
        return (jnp.minimum(i, last), 0, 0)

    def whole(dims):
        return pl.BlockSpec(dims, lambda i, *_: (0,) * len(dims))

    segment, window = (2, width, size), (4 * REACH, width, size)
    out = pl.pallas_call(
        apply_kernel,
        grid_spec=pltpu.PrefetchScalarGridSpec(
            num_scalar_prefetch=3,
            grid=(slots // GROUP,),
            in_specs=[pl.BlockSpec(memory_space=pl.ANY)] * (2 * REACH)
            + [pl.BlockSpec((GROUP, size, size), tile_map)],
            out_specs=[whole(segment)] * (2 * REACH) + [whole(window)],
            scratch_shapes=[VMEM(window, bf16), VMEM(window, f32), pltpu.SemaphoreType.DMA((2 * REACH,))],
        ),
        out_shape=[shape(kind, *segment) for kind in SEGMENT_KINDS] + [shape(bf16, *window)],
        compiler_params=pltpu.CompilerParams(vmem_limit_bytes=24 << 20),
        cost_estimate=pl.CostEstimate(flops=4 << 30, bytes_accessed=16 << 20, transcendentals=0),
    )(meta, rows, cols, *pieces, blocks)
    return out[: 2 * REACH : 2], out[1 : 2 * REACH : 2], out[2 * REACH]


def inner_kernel(*refs):
    pieces, mine, theirs, out = refs[: 2 * REACH], refs[2 * REACH], refs[2 * REACH + 1], refs[-1]
    size = out.shape[1]
    own = jnp.zeros((size, size), f32)
    other = jnp.zeros((size, size), f32)
    for s, piece in enumerate(pieces):
        for t in range(2):
            own += dot_nt(mine[2 * s + t], piece[t])
            other += dot_nt(piece[t], theirs[2 * s + t])
    out[pl.ds(0, size), :] = own
    out[pl.ds(size, size), :] = other


def update_kernel(rows_total, x, x_other, kept, near, far, two, inner, update, *residual):
    width, count = x.shape
    size = kept.shape[2]
    own = split(inner[pl.ds(0, width), :] / rows_total)
    other = split(inner[pl.ds(width, width), :] / rows_total)
    for t in range(count // size):
        part = pl.ds(t * size, size)
        applied = kept[t] + near[t].astype(f32) + (far[t].astype(f32) + two[t].astype(f32))
        now = x[:, part]
        rest = applied - (dot3(dot_nn, own, split(now)) + dot3(dot_nn, other, split(x_other[:, part])))
        update[:, part] = now - STEP_RATE * rest
        if residual:
            residual[0][part, :] = rest.T


def gram_kernel(core, mine, theirs, out):
    width = mine.shape[0]
    half = width // 2
    own, other = split(mine[...]), split(theirs[...])
    out[pl.ds(0, width), :] = dot3(dot_nt, own, own)
    ahead = core[0] == 0
    high = jnp.where(ahead, theirs[pl.ds(0, half), :], mine[pl.ds(half, half), :])
    low = [jnp.where(ahead, a, b) for a, b in zip(own, other)]
    out[pl.ds(width, half), :] = dot3(dot_nt, split(high), low)


def inverse_factor(g, w, high, low):
    n = g.shape[0]
    at_row = lax.broadcasted_iota(jnp.int32, (n, n), 0)
    at_col = lax.broadcasted_iota(jnp.int32, (n, n), 1)
    eye = jnp.where(at_row == at_col, 1.0, 0.0).astype(f32)
    diagonal = eye * g[...]
    by_row = lax.rsqrt(jnp.sum(diagonal, axis=1, keepdims=True))
    by_col = lax.rsqrt(jnp.sum(diagonal, axis=0, keepdims=True))
    unit = g[...] * by_row * by_col
    rounded = unit.astype(bf16)
    square = dot_nn(rounded, rounded).astype(bf16)
    fourth = dot_nn(square, square)
    scale = 1.9 / jnp.sqrt(jnp.sqrt(jnp.sqrt(jnp.sum(fourth * fourth, keepdims=True))))
    scaled = unit * scale
    high[...], low[...] = split(scaled)

    def lower(e):
        return jnp.where(at_row > at_col, e, 0.5 * eye * e)

    p = lower(scaled - eye)
    pb = p.astype(bf16)
    w[...] = eye - p + dot_nn(pb, pb)

    def improve(e):
        p = lower(e)
        pb = p.astype(bf16)
        first = dot_nn(pb, w[...].astype(bf16))
        w[...] = w[...] - first + dot_nn(pb, first.astype(bf16))
        return jnp.sqrt(jnp.sum(p * p))

    def rough(state):
        wb = w[...].astype(bf16)
        e = dot_nt(dot_nn(wb, high[...]).astype(bf16), wb) - eye
        return state[0] + 1, improve(e)

    def fine(state):
        ws = split(w[...])
        e = dot3(dot_nt, split(dot3(dot_nn, ws, (high[...], low[...]))), ws) - eye
        return state[0] + 1, improve(e)

    def until(bound, most):
        return lambda state: (state[0] < most) & jnp.logical_not(state[1] <= bound)

    lax.while_loop(until(0.4, 16), rough, (0, jnp.float32(1e9)))
    _, error = lax.while_loop(until(2e-3, 6), fine, (0, jnp.float32(1e9)))
    done = error <= 2e-3

    @pl.when(done)
    def _():
        w[...] = w[...] * (by_col * jnp.sqrt(scale))

    @pl.when(jnp.logical_not(done))
    def _():
        w[...] = eye

        def eliminate(k, carry):
            lane = lax.broadcasted_iota(jnp.int32, (1, n), 1)
            below = lax.broadcasted_iota(jnp.int32, (n, 1), 0)
            row = g[pl.ds(k, 1), :]
            pivot = jnp.sum(jnp.where(lane == k, row, 0.0), axis=1, keepdims=True)
            column = jnp.sum(jnp.where(at_col == k, g[...], 0.0), axis=1, keepdims=True)
            ratio = jnp.where(below > k, column / pivot, 0.0)
            solved = w[pl.ds(k, 1), :]
            g[...] = g[...] - ratio * row
            w[...] = w[...] - ratio * solved
            w[pl.ds(k, 1), :] = solved * lax.rsqrt(pivot)
            return carry

        lax.fori_loop(0, n, eliminate, 0)


def factor_kernel(rows_total, last, core, mine, theirs, gram, gram_other, *refs):
    out, (g, w, high, low, update) = refs[:-5], refs[-5:]
    width = mine.shape[0]
    half = width // 2
    ahead = core[0] == 0
    first = jnp.where(ahead, gram[...], gram_other[...]) / rows_total
    second = jnp.where(ahead, gram_other[...], gram[...]) / rows_total
    g[pl.ds(0, width), pl.ds(0, width)] = first[:width]
    g[pl.ds(width, width), pl.ds(width, width)] = second[:width]
    below = jnp.concatenate([first[width:], second[width:]], axis=0)
    g[pl.ds(width, width), pl.ds(0, width)] = below
    g[pl.ds(0, width), pl.ds(width, width)] = below.T
    inverse_factor(g, w, high, low)
    start = pl.multiple_of(core[0] * width, width)
    update[pl.ds(start, width), :] = mine[...]
    update[pl.ds(width - start, width), :] = theirs[...]
    mix = split(w[pl.ds(start, width), :])
    size = width
    for t in range(mine.shape[1] // size):
        part = pl.ds(t * size, size)
        solved = dot3(dot_nn, mix, split(update[:, part]))
        if last:
            out[0][part, :] = solved.T
        else:
            out[0][:, part] = solved
            out[1][t] = solved.astype(bf16)


def swap_cores(a):
    return lax.ppermute(a, "vec", [(0, 1), (1, 0)])


def flip(a, mask):
    return lax.ppermute(a, "patch", [(i, i ^ mask) for i in range(lax.axis_size("patch"))])


def shift(a, pairs):
    devices = range(lax.axis_size("patch"))
    return lax.ppermute(a, "patch", [(i - 2 * pairs, i) for i in devices if i - 2 * pairs in devices])


def stride(a, back=False):
    devices = range(lax.axis_size("patch"))
    route = [(i - (2 if i // 2 % 2 else 6), i) for i in devices]
    return lax.ppermute(a, "patch", [(d, s) if back else (s, d) for s, d in route if s in devices])


def together(*arrays):
    return lax.optimization_barrier(arrays)


def reach(u):
    two = shift(u, 2)
    far = stride(u)
    own_x = flip(u, 1)
    two, own_x = together(two, own_x)
    two_x, side = flip(two, 1), flip(two, 2)
    far, two_x, side = together(far, two_x, side)
    return [u, own_x, two, two_x, far, flip(far, 1), side, flip(two_x, 2)]


def place_order(parts, place):
    radix = len(parts)
    bit = 1
    while bit < radix:
        swapped = [parts[j ^ bit] for j in range(radix)]
        parts = [jnp.where(place & bit, b, a) for a, b in zip(parts, swapped)]
        bit *= 2
    return parts


def summed(a, gates=()):
    position = lax.axis_index("patch")
    left, step, stages = lax.axis_size("patch"), 1, []
    while left > 1:
        radix = 4 if left % 4 == 0 else 2
        stages.append((radix, step))
        left, step = left // radix, step * radix
    gates = list(gates)

    def gated(x):
        return together(x, *gates.pop(0))[0] if gates else x

    for radix, step in stages[:-1]:
        place = (position // step) % radix
        parts = gated(a).reshape(radix, a.shape[0] // radix, a.shape[1])
        a = lax.dynamic_index_in_dim(parts, place, 0, False)
        for m in range(1, radix):
            a = a + flip(lax.dynamic_index_in_dim(parts, place ^ m, 0, False), m * step)
    radix, step = stages[-1]
    a = gated(a)
    a = sum([flip(a, m * step) for m in range(1, radix)], a)
    for radix, step in stages[-2::-1]:
        place = (position // step) % radix
        a = gated(a)
        parts = place_order([a] + [flip(a, m * step) for m in range(1, radix)], place)
        a = jnp.concatenate(parts, axis=0)
    return a


def shards(vectors, blocks, block_row, block_col, block_count):
    count, width = vectors.shape
    size = blocks.shape[1]
    rows_total = float(count * lax.axis_size("patch"))
    position = lax.axis_index("patch")
    odd = position % 2
    meta = jnp.stack([block_count[0], 2 * (position - odd) - 4 * (REACH - 1), odd, position // 2 % 2]).astype(jnp.int32)
    core = lax.axis_index("vec").astype(jnp.int32).reshape(1)
    flat, chunk = shape(f32, width, count), shape(bf16, count // size, width, size)
    x, u = call(pack_kernel, [flat, chunk], [vectors])
    for step in range(STEPS):
        last = step == STEPS - 1
        pieces = reach(u)
        x_other = swap_cores(x)
        same, cross, everything = apply_tiles(pieces, blocks, block_row, block_col, meta)
        side_x, far_x, side, own_x = flip(cross[3], 2), flip(cross[2], 1), flip(same[3], 2), flip(cross[0], 1)
        theirs, side_x, far_x = together(swap_cores(everything), side_x, far_x)
        two_x = (cross[1] + side_x.astype(f32)).astype(bf16)
        far = (same[2] + far_x.astype(f32)).astype(bf16)
        (inner,) = call(inner_kernel, [shape(f32, 2 * width, width)], pieces + [everything, theirs])
        two = (same[1] + (flip(two_x, 1).astype(f32) + side.astype(f32))).astype(bf16)
        joined = [own_x, stride(far, True), shift(two, -2)]
        inner = summed(inner, [(two_x, far), (joined[1], two), (joined[2], own_x)])
        out = [flat] + ([shape(f32, count, width)] if last else [])
        update, *residual = call(
            lambda *refs: update_kernel(rows_total, *refs), out, [x, x_other, same[0], *joined, inner]
        )
        update_other = swap_cores(update)
        (gram,) = call(
            gram_kernel, [shape(f32, width + width // 2, width)], [core, update, update_other], smem=1
        )
        gram = summed(gram)
        full = (2 * width, 2 * width)
        out = call(
            lambda *refs: factor_kernel(rows_total, last, *refs),
            [shape(f32, count, width)] if last else [flat, chunk],
            [core, update, update_other, gram, swap_cores(gram)],
            scratch=[VMEM(full, f32), VMEM(full, f32), VMEM(full, bf16), VMEM(full, bf16), VMEM((2 * width, count), f32)],
            smem=1,
            flops=16 << 30,
            vmem=28,
        )
        if last:
            return out[0], residual[0]
        x, u = out


def solution(mesh):
    in_specs = (P("patch", "vec"), P("patch", None, None), P("patch"), P("patch"), P("patch"))
    out_specs = (P("patch", "vec"), P("patch", "vec"))
    return jax.shard_map(shards, mesh=mesh, in_specs=in_specs, out_specs=out_specs, check_vma=False)
```

```python
import jax
import jax.numpy as jnp
from jax import lax
from jax.experimental import pallas as pl
from jax.experimental.pallas import tpu as pltpu
from jax.sharding import PartitionSpec as P

STEPS = 2
STEP_RATE = 0.25
GROUP = 8
REACH = 4

f32, bf16 = jnp.float32, jnp.bfloat16
SEGMENT_KINDS = (f32, bf16, f32, f32, f32, bf16, bf16, bf16)
VMEM, SMEM = pltpu.VMEM, pltpu.SMEM


def dot_nn(a, b):
    return lax.dot_general(a, b, (((1,), (0,)), ((), ())), preferred_element_type=f32)


def dot_nt(a, b):
    return lax.dot_general(a, b, (((1,), (1,)), ((), ())), preferred_element_type=f32)


def split(a):
    high = a.astype(bf16)
    return high, (a - high.astype(f32)).astype(bf16)


def dot3(dot, a, b):
    (ah, al), (bh, bl) = a, b
    return dot(ah, bh) + (dot(ah, bl) + dot(al, bh))


def call(kernel, out, args, scratch=(), smem=0, flops=1 << 28, vmem=16):
    moved = sum(a.size * a.dtype.itemsize for a in args) + sum(o.size * o.dtype.itemsize for o in out)
    return pl.pallas_call(
        kernel,
        out_shape=out,
        in_specs=[pl.BlockSpec(memory_space=SMEM)] * smem + [pl.BlockSpec(memory_space=VMEM)] * (len(args) - smem),
        out_specs=[pl.BlockSpec(memory_space=VMEM)] * len(out),
        scratch_shapes=list(scratch),
        compiler_params=pltpu.CompilerParams(vmem_limit_bytes=vmem << 20),
        cost_estimate=pl.CostEstimate(flops=flops, bytes_accessed=moved, transcendentals=0),
    )(*args)


def shape(dtype, *dims):
    return jax.ShapeDtypeStruct(dims, dtype)


def pack_kernel(vectors, columns, chunk):
    size = chunk.shape[2]
    for t in range(chunk.shape[0]):
        turned = vectors[pl.ds(t * size, size), :].T
        columns[:, pl.ds(t * size, size)] = turned
        chunk[t] = turned.astype(bf16)


def apply_kernel(meta, rows, cols, *refs):
    pieces, blocks, out = refs[: 2 * REACH], refs[2 * REACH], refs[2 * REACH + 1 : 4 * REACH + 1]
    everything, window, total, tiles, piece_sems, tile_sems = refs[4 * REACH + 1 :]
    used, start, odd, pair_odd = meta[0], meta[1], meta[2], meta[3]
    groups = (used + GROUP - 1) // GROUP

    def fetch(group):
        at = group % 2
        return pltpu.make_async_copy(blocks.at[pl.ds(group * GROUP, GROUP)], tiles.at[at], tile_sems.at[at])

    @pl.when(groups > 0)
    def _():
        fetch(0).start()

    copies = [
        pltpu.make_async_copy(piece, window.at[pl.ds(2 * s, 2)], piece_sems.at[s]) for s, piece in enumerate(pieces)
    ]
    for copy in copies:
        copy.start()
    total[...] = jnp.zeros_like(total)
    for copy in copies:
        copy.wait()

    def place(tile):
        w = tile - start
        back = REACH - 1 - w // 4
        role = jnp.where(back % 2 == 1, 2 + ((back // 2) ^ pair_odd ^ 1), back // 2)
        return role * 4 + 2 * (((w % 4) // 2) ^ odd) + w % 2

    def multiply(group, carry):
        @pl.when(group + 1 < groups)
        def _():
            fetch(group + 1).start()

        fetch(group).wait()
        found = []
        for k in range(GROUP):
            slot = group * GROUP + k
            row, col = rows[slot], cols[slot]
            weight = jnp.where(row == col, 0.5, 1.0).astype(f32)
            r, c = place(row), place(col)
            tile = tiles[group % 2, k]
            tile = jnp.where(slot < used, tile, jnp.zeros_like(tile))
            found.append((r, dot_nt(window[c], tile), weight))
            found.append((c, dot_nn(window[r], tile), weight))
        for at, part, weight in found:
            total[at] += part * weight
        return carry

    lax.fori_loop(0, groups, multiply, 0)
    for s, segment in enumerate(out):
        segment[...] = total[pl.ds(2 * s, 2)].astype(segment.dtype)
    everything[...] = total[...].astype(bf16)


def apply_tiles(pieces, blocks, rows, cols, meta):
    size = blocks.shape[1]
    width = pieces[0].shape[1]
    segment, window = (2, width, size), (4 * REACH, width, size)
    out = pl.pallas_call(
        apply_kernel,
        in_specs=[pl.BlockSpec(memory_space=SMEM)] * 3
        + [pl.BlockSpec(memory_space=pl.ANY)] * (2 * REACH)
        + [pl.BlockSpec(memory_space=pltpu.HBM)],
        out_specs=[pl.BlockSpec(memory_space=VMEM)] * (2 * REACH + 1),
        scratch_shapes=[
            VMEM(window, bf16),
            VMEM(window, f32),
            VMEM((2, GROUP, size, size), bf16),
            pltpu.SemaphoreType.DMA((2 * REACH,)),
            pltpu.SemaphoreType.DMA((2,)),
        ],
        out_shape=[shape(kind, *segment) for kind in SEGMENT_KINDS] + [shape(bf16, *window)],
        compiler_params=pltpu.CompilerParams(vmem_limit_bytes=50 << 20),
        cost_estimate=pl.CostEstimate(flops=4 << 30, bytes_accessed=16 << 20, transcendentals=0),
    )(meta, rows, cols, *pieces, blocks)
    return out[: 2 * REACH : 2], out[1 : 2 * REACH : 2], out[2 * REACH]


def inner_kernel(*refs):
    pieces, theirs, mine, out = refs[: 2 * REACH], refs[2 * REACH : -2], refs[-2], refs[-1]
    size = out.shape[1]
    own = jnp.zeros((size, size), f32)
    other = jnp.zeros((size, size), f32)
    for s, piece in enumerate(pieces):
        group, start = GROUPED[s]
        for t in range(2):
            own += dot_nt(mine[2 * s + t], piece[t])
            other += dot_nt(mine[2 * s + t], theirs[group][start + t])
    out[pl.ds(0, size), :] = own
    out[pl.ds(size, size), :] = other


def update_kernel(rows_total, x, x_other, kept, near, far, two, inner, update, *residual):
    width, count = x.shape
    size = kept.shape[2]
    own = split(inner[pl.ds(0, width), :] / rows_total)
    other = split(inner[pl.ds(width, width), :] / rows_total)
    for t in range(count // size):
        part = pl.ds(t * size, size)
        applied = kept[t] + near[t].astype(f32) + (far[t].astype(f32) + two[t].astype(f32))
        now = x[:, part]
        rest = applied - (dot3(dot_nn, own, split(now)) + dot3(dot_nn, other, split(x_other[:, part])))
        update[:, part] = now - STEP_RATE * rest
        if residual:
            residual[0][part, :] = rest.T


def gram_kernel(core, mine, theirs, out):
    width = mine.shape[0]
    half = width // 2
    own, other = split(mine[...]), split(theirs[...])
    out[pl.ds(0, width), :] = dot3(dot_nt, own, own)
    ahead = core[0] == 0
    high = jnp.where(ahead, theirs[pl.ds(0, half), :], mine[pl.ds(half, half), :])
    low = [jnp.where(ahead, a, b) for a, b in zip(own, other)]
    out[pl.ds(width, half), :] = dot3(dot_nt, split(high), low)


def inverse_factor(g, w, high, low):
    n = g.shape[0]
    at_row = lax.broadcasted_iota(jnp.int32, (n, n), 0)
    at_col = lax.broadcasted_iota(jnp.int32, (n, n), 1)
    eye = jnp.where(at_row == at_col, 1.0, 0.0).astype(f32)
    diagonal = eye * g[...]
    by_row = lax.rsqrt(jnp.sum(diagonal, axis=1, keepdims=True))
    by_col = lax.rsqrt(jnp.sum(diagonal, axis=0, keepdims=True))
    unit = g[...] * by_row * by_col
    rounded = unit.astype(bf16)
    square = dot_nn(rounded, rounded).astype(bf16)
    fourth = dot_nn(square, square)
    scale = 1.9 / jnp.sqrt(jnp.sqrt(jnp.sqrt(jnp.sum(fourth * fourth, keepdims=True))))
    scaled = unit * scale
    high[...], low[...] = split(scaled)

    def lower(e):
        return jnp.where(at_row > at_col, e, 0.5 * eye * e)

    p = lower(scaled - eye)
    pb = p.astype(bf16)
    w[...] = eye - p + dot_nn(pb, pb)

    def improve(e):
        p = lower(e)
        pb = p.astype(bf16)
        first = dot_nn(pb, w[...].astype(bf16))
        w[...] = w[...] - first + dot_nn(pb, first.astype(bf16))
        return jnp.sqrt(jnp.sum(p * p))

    def rough(state):
        wb = w[...].astype(bf16)
        e = dot_nt(dot_nn(wb, high[...]).astype(bf16), wb) - eye
        return state[0] + 1, improve(e)

    def fine(state):
        ws = split(w[...])
        e = dot3(dot_nt, split(dot3(dot_nn, ws, (high[...], low[...]))), ws) - eye
        return state[0] + 1, improve(e)

    def until(bound, most):
        return lambda state: (state[0] < most) & jnp.logical_not(state[1] <= bound)

    lax.while_loop(until(0.4, 16), rough, (0, jnp.float32(1e9)))
    _, error = lax.while_loop(until(2e-3, 6), fine, (0, jnp.float32(1e9)))
    done = error <= 2e-3

    @pl.when(done)
    def _():
        w[...] = w[...] * (by_col * jnp.sqrt(scale))

    @pl.when(jnp.logical_not(done))
    def _():
        w[...] = eye

        def eliminate(k, carry):
            lane = lax.broadcasted_iota(jnp.int32, (1, n), 1)
            below = lax.broadcasted_iota(jnp.int32, (n, 1), 0)
            row = g[pl.ds(k, 1), :]
            pivot = jnp.sum(jnp.where(lane == k, row, 0.0), axis=1, keepdims=True)
            column = jnp.sum(jnp.where(at_col == k, g[...], 0.0), axis=1, keepdims=True)
            ratio = jnp.where(below > k, column / pivot, 0.0)
            solved = w[pl.ds(k, 1), :]
            g[...] = g[...] - ratio * row
            w[...] = w[...] - ratio * solved
            w[pl.ds(k, 1), :] = solved * lax.rsqrt(pivot)
            return carry

        lax.fori_loop(0, n, eliminate, 0)


def factor_kernel(rows_total, last, core, mine, theirs, gram, gram_other, *refs):
    out, (g, w, high, low, update) = refs[:-5], refs[-5:]
    width = mine.shape[0]
    half = width // 2
    ahead = core[0] == 0
    first = jnp.where(ahead, gram[...], gram_other[...]) / rows_total
    second = jnp.where(ahead, gram_other[...], gram[...]) / rows_total
    g[pl.ds(0, width), pl.ds(0, width)] = first[:width]
    g[pl.ds(width, width), pl.ds(width, width)] = second[:width]
    below = jnp.concatenate([first[width:], second[width:]], axis=0)
    g[pl.ds(width, width), pl.ds(0, width)] = below
    g[pl.ds(0, width), pl.ds(width, width)] = below.T
    inverse_factor(g, w, high, low)
    start = pl.multiple_of(core[0] * width, width)
    update[pl.ds(start, width), :] = mine[...]
    update[pl.ds(width - start, width), :] = theirs[...]
    mix = split(w[pl.ds(start, width), :])
    size = width
    for t in range(mine.shape[1] // size):
        part = pl.ds(t * size, size)
        solved = dot3(dot_nn, mix, split(update[:, part]))
        if last:
            out[0][part, :] = solved.T
        else:
            out[0][:, part] = solved
            out[1][t] = solved.astype(bf16)


def swap_cores(a):
    return lax.ppermute(a, "vec", [(0, 1), (1, 0)])


def flip(a, mask):
    return lax.ppermute(a, "patch", [(i, i ^ mask) for i in range(lax.axis_size("patch"))])


def shift(a, pairs):
    devices = range(lax.axis_size("patch"))
    return lax.ppermute(a, "patch", [(i - 2 * pairs, i) for i in devices if i - 2 * pairs in devices])


def stride(a, back=False):
    devices = range(lax.axis_size("patch"))
    route = [(i - (2 if i // 2 % 2 else 6), i) for i in devices]
    return lax.ppermute(a, "patch", [(d, s) if back else (s, d) for s, d in route if s in devices])


def together(*arrays):
    return lax.optimization_barrier(arrays)


def reach(u):
    two = shift(u, 2)
    far = stride(u)
    own_x = flip(u, 1)
    two, own_x = together(two, own_x)
    two_x, side = flip(two, 1), flip(two, 2)
    first = swap_cores(jnp.concatenate([u, own_x, two]))
    far, two_x, side = together(far, two_x, side)
    second = swap_cores(jnp.concatenate([far, two_x, side]))
    far_x, side_x = flip(far, 1), flip(two_x, 2)
    third = swap_cores(jnp.concatenate([far_x, side_x]))
    return [u, own_x, two, two_x, far, far_x, side, side_x], [first, second, third]


GROUPED = ((0, 0), (0, 2), (0, 4), (1, 2), (1, 0), (2, 0), (1, 4), (2, 2))


def place_order(parts, place):
    radix = len(parts)
    bit = 1
    while bit < radix:
        swapped = [parts[j ^ bit] for j in range(radix)]
        parts = [jnp.where(place & bit, b, a) for a, b in zip(parts, swapped)]
        bit *= 2
    return parts


def summed(a, gates=()):
    position = lax.axis_index("patch")
    left, step, stages = lax.axis_size("patch"), 1, []
    while left > 1:
        radix = 4 if left % 4 == 0 else 2
        stages.append((radix, step))
        left, step = left // radix, step * radix
    gates = list(gates)

    def gated(x):
        return together(x, *gates.pop(0))[0] if gates else x

    for radix, step in stages[:-1]:
        place = (position // step) % radix
        parts = gated(a).reshape(radix, a.shape[0] // radix, a.shape[1])
        a = lax.dynamic_index_in_dim(parts, place, 0, False)
        for m in range(1, radix):
            a = a + flip(lax.dynamic_index_in_dim(parts, place ^ m, 0, False), m * step)
    radix, step = stages[-1]
    a = gated(a)
    a = sum([flip(a, m * step) for m in range(1, radix)], a)
    for radix, step in stages[-2::-1]:
        place = (position // step) % radix
        a = gated(a)
        parts = place_order([a] + [flip(a, m * step) for m in range(1, radix)], place)
        a = jnp.concatenate(parts, axis=0)
    return a


def shards(vectors, blocks, block_row, block_col, block_count):
    count, width = vectors.shape
    size = blocks.shape[1]
    rows_total = float(count * lax.axis_size("patch"))
    position = lax.axis_index("patch")
    odd = position % 2
    meta = jnp.stack([block_count[0], 2 * (position - odd) - 4 * (REACH - 1), odd, position // 2 % 2]).astype(jnp.int32)
    core = lax.axis_index("vec").astype(jnp.int32).reshape(1)
    flat, chunk = shape(f32, width, count), shape(bf16, count // size, width, size)
    x, u = call(pack_kernel, [flat, chunk], [vectors])
    for step in range(STEPS):
        last = step == STEPS - 1
        pieces, others = reach(u)
        x_other = swap_cores(x)
        same, cross, everything = apply_tiles(pieces, blocks, block_row, block_col, meta)
        side_x, far_x, side, own_x = flip(cross[3], 2), flip(cross[2], 1), flip(same[3], 2), flip(cross[0], 1)
        (inner,) = call(
            inner_kernel, [shape(f32, 2 * width, width)], pieces + others + [everything], flops=1 << 30
        )
        side_x, far_x, inner = together(side_x, far_x, inner)
        two_x = flip((cross[1] + side_x.astype(f32)).astype(bf16), 1)
        far = stride((same[2] + far_x.astype(f32)).astype(bf16), True)
        two = (same[1] + (two_x.astype(f32) + side.astype(f32))).astype(bf16)
        joined = [own_x, far, shift(two, -2)]
        inner = summed(inner, [(two_x, far), (joined[2],), (own_x,)])
        out = [flat] + ([shape(f32, count, width)] if last else [])
        update, *residual = call(
            lambda *refs: update_kernel(rows_total, *refs), out, [x, x_other, same[0], *joined, inner]
        )
        update_other = swap_cores(update)
        (gram,) = call(
            gram_kernel, [shape(f32, width + width // 2, width)], [core, update, update_other], smem=1
        )
        gram = summed(gram)
        full = (2 * width, 2 * width)
        out = call(
            lambda *refs: factor_kernel(rows_total, last, *refs),
            [shape(f32, count, width)] if last else [flat, chunk],
            [core, update, update_other, gram, swap_cores(gram)],
            scratch=[VMEM(full, f32), VMEM(full, f32), VMEM(full, bf16), VMEM(full, bf16), VMEM((2 * width, count), f32)],
            smem=1,
            flops=16 << 30,
            vmem=28,
        )
        if last:
            return out[0], residual[0]
        x, u = out


def solution(mesh):
    in_specs = (P("patch", "vec"), P("patch", None, None), P("patch"), P("patch"), P("patch"))
    out_specs = (P("patch", "vec"), P("patch", "vec"))
    return jax.shard_map(shards, mesh=mesh, in_specs=in_specs, out_specs=out_specs, check_vma=False)
```

```python
import jax
import jax.numpy as jnp
from jax import lax
from jax.experimental import pallas as pl
from jax.experimental.pallas import tpu as pltpu
from jax.sharding import PartitionSpec as P

STEPS = 2
STEP_RATE = 0.25
GROUP = 8
REACH = 4

f32, bf16 = jnp.float32, jnp.bfloat16
SEGMENT_KINDS = (f32, bf16, f32, f32, f32, bf16, bf16, bf16)
VMEM, SMEM = pltpu.VMEM, pltpu.SMEM


def dot_nn(a, b):
    return lax.dot_general(a, b, (((1,), (0,)), ((), ())), preferred_element_type=f32)


def dot_nt(a, b):
    return lax.dot_general(a, b, (((1,), (1,)), ((), ())), preferred_element_type=f32)


def split(a):
    high = a.astype(bf16)
    return high, (a - high.astype(f32)).astype(bf16)


def dot3(dot, a, b):
    (ah, al), (bh, bl) = a, b
    return dot(ah, bh) + (dot(ah, bl) + dot(al, bh))


def call(kernel, out, args, scratch=(), smem=0, flops=1 << 28, vmem=16):
    moved = sum(a.size * a.dtype.itemsize for a in args) + sum(o.size * o.dtype.itemsize for o in out)
    return pl.pallas_call(
        kernel,
        out_shape=out,
        in_specs=[pl.BlockSpec(memory_space=SMEM)] * smem + [pl.BlockSpec(memory_space=VMEM)] * (len(args) - smem),
        out_specs=[pl.BlockSpec(memory_space=VMEM)] * len(out),
        scratch_shapes=list(scratch),
        compiler_params=pltpu.CompilerParams(vmem_limit_bytes=vmem << 20),
        cost_estimate=pl.CostEstimate(flops=flops, bytes_accessed=moved, transcendentals=0),
    )(*args)


def shape(dtype, *dims):
    return jax.ShapeDtypeStruct(dims, dtype)


def pack_kernel(vectors, columns, chunk):
    size = chunk.shape[2]
    for t in range(chunk.shape[0]):
        turned = vectors[pl.ds(t * size, size), :].T
        columns[:, pl.ds(t * size, size)] = turned
        chunk[t] = turned.astype(bf16)


def apply_kernel(meta, rows, cols, *refs):
    pieces, blocks, theirs = refs[: 2 * REACH], refs[2 * REACH], refs[2 * REACH + 1 : 2 * REACH + 4]
    out, (inner, window, total, tiles, piece_sems, tile_sems) = refs[2 * REACH + 4 : -6], refs[-6:]
    used, start, odd, pair_odd = meta[0], meta[1], meta[2], meta[3]
    groups = (used + GROUP - 1) // GROUP

    def fetch(group):
        at = group % 2
        return pltpu.make_async_copy(blocks.at[pl.ds(group * GROUP, GROUP)], tiles.at[at], tile_sems.at[at])

    @pl.when(groups > 0)
    def _():
        fetch(0).start()

    copies = [
        pltpu.make_async_copy(piece, window.at[pl.ds(2 * s, 2)], piece_sems.at[s]) for s, piece in enumerate(pieces)
    ]
    for copy in copies:
        copy.start()
    total[...] = jnp.zeros_like(total)
    for copy in copies:
        copy.wait()

    def place(tile):
        w = tile - start
        back = REACH - 1 - w // 4
        role = jnp.where(back % 2 == 1, 2 + ((back // 2) ^ pair_odd ^ 1), back // 2)
        return role * 4 + 2 * (((w % 4) // 2) ^ odd) + w % 2

    def multiply(group, carry):
        @pl.when(group + 1 < groups)
        def _():
            fetch(group + 1).start()

        fetch(group).wait()
        found = []
        for k in range(GROUP):
            slot = group * GROUP + k
            row, col = rows[slot], cols[slot]
            weight = jnp.where(row == col, 0.5, 1.0).astype(f32)
            r, c = place(row), place(col)
            tile = tiles[group % 2, k]
            tile = jnp.where(slot < used, tile, jnp.zeros_like(tile))
            found.append((r, dot_nt(window[c], tile), weight))
            found.append((c, dot_nn(window[r], tile), weight))
        for at, part, weight in found:
            total[at] += part * weight
        return carry

    lax.fori_loop(0, groups, multiply, 0)
    for s, segment in enumerate(out):
        segment[...] = total[pl.ds(2 * s, 2)].astype(segment.dtype)

    size = inner.shape[1]
    own = jnp.zeros((size, size), f32)
    other = jnp.zeros((size, size), f32)
    for s in range(2 * REACH):
        group, start = GROUPED[s]
        for t in range(2):
            mine = total[2 * s + t].astype(bf16)
            own += dot_nt(mine, window[2 * s + t])
            other += dot_nt(mine, theirs[group][start + t])
    inner[pl.ds(0, size), :] = own
    inner[pl.ds(size, size), :] = other


def apply_tiles(pieces, others, blocks, rows, cols, meta):
    size = blocks.shape[1]
    width = pieces[0].shape[1]
    segment, window = (2, width, size), (4 * REACH, width, size)
    out = pl.pallas_call(
        apply_kernel,
        in_specs=[pl.BlockSpec(memory_space=SMEM)] * 3
        + [pl.BlockSpec(memory_space=pl.ANY)] * (2 * REACH)
        + [pl.BlockSpec(memory_space=pltpu.HBM)]
        + [pl.BlockSpec(memory_space=VMEM)] * len(others),
        out_specs=[pl.BlockSpec(memory_space=VMEM)] * (2 * REACH + 1),
        scratch_shapes=[
            VMEM(window, bf16),
            VMEM(window, f32),
            VMEM((2, GROUP, size, size), bf16),
            pltpu.SemaphoreType.DMA((2 * REACH,)),
            pltpu.SemaphoreType.DMA((2,)),
        ],
        out_shape=[shape(kind, *segment) for kind in SEGMENT_KINDS] + [shape(f32, 2 * width, size)],
        compiler_params=pltpu.CompilerParams(vmem_limit_bytes=50 << 20),
        cost_estimate=pl.CostEstimate(flops=4 << 30, bytes_accessed=16 << 20, transcendentals=0),
    )(meta, rows, cols, *pieces, blocks, *others)
    return out[: 2 * REACH : 2], out[1 : 2 * REACH : 2], out[2 * REACH]


def update_kernel(rows_total, x, x_other, kept, near, far, two, inner, update, *residual):
    width, count = x.shape
    size = kept.shape[2]
    own = split(inner[pl.ds(0, width), :] / rows_total)
    other = split(inner[pl.ds(width, width), :] / rows_total)
    for t in range(count // size):
        part = pl.ds(t * size, size)
        applied = kept[t] + near[t].astype(f32) + (far[t].astype(f32) + two[t].astype(f32))
        now = x[:, part]
        rest = applied - (dot3(dot_nn, own, split(now)) + dot3(dot_nn, other, split(x_other[:, part])))
        update[:, part] = now - STEP_RATE * rest
        if residual:
            residual[0][part, :] = rest.T


def gram_kernel(core, mine, theirs, out):
    width = mine.shape[0]
    half = width // 2
    own, other = split(mine[...]), split(theirs[...])
    out[pl.ds(0, width), :] = dot3(dot_nt, own, own)
    ahead = core[0] == 0
    high = jnp.where(ahead, theirs[pl.ds(0, half), :], mine[pl.ds(half, half), :])
    low = [jnp.where(ahead, a, b) for a, b in zip(own, other)]
    out[pl.ds(width, half), :] = dot3(dot_nt, split(high), low)


def inverse_factor(g, w, high, low):
    n = g.shape[0]
    at_row = lax.broadcasted_iota(jnp.int32, (n, n), 0)
    at_col = lax.broadcasted_iota(jnp.int32, (n, n), 1)
    eye = jnp.where(at_row == at_col, 1.0, 0.0).astype(f32)
    diagonal = eye * g[...]
    by_row = lax.rsqrt(jnp.sum(diagonal, axis=1, keepdims=True))
    by_col = lax.rsqrt(jnp.sum(diagonal, axis=0, keepdims=True))
    unit = g[...] * by_row * by_col
    rounded = unit.astype(bf16)
    square = dot_nn(rounded, rounded).astype(bf16)
    fourth = dot_nn(square, square)
    scale = 1.9 / jnp.sqrt(jnp.sqrt(jnp.sqrt(jnp.sum(fourth * fourth, keepdims=True))))
    scaled = unit * scale
    high[...], low[...] = split(scaled)

    def lower(e):
        return jnp.where(at_row > at_col, e, 0.5 * eye * e)

    p = lower(scaled - eye)
    pb = p.astype(bf16)
    w[...] = eye - p + dot_nn(pb, pb)

    def improve(e):
        p = lower(e)
        pb = p.astype(bf16)
        first = dot_nn(pb, w[...].astype(bf16))
        w[...] = w[...] - first + dot_nn(pb, first.astype(bf16))
        return jnp.sqrt(jnp.sum(p * p))

    def rough(state):
        wb = w[...].astype(bf16)
        e = dot_nt(dot_nn(wb, high[...]).astype(bf16), wb) - eye
        return state[0] + 1, improve(e)

    def fine(state):
        ws = split(w[...])
        e = dot3(dot_nt, split(dot3(dot_nn, ws, (high[...], low[...]))), ws) - eye
        return state[0] + 1, improve(e)

    def until(bound, most):
        return lambda state: (state[0] < most) & jnp.logical_not(state[1] <= bound)

    lax.while_loop(until(0.4, 16), rough, (0, jnp.float32(1e9)))
    _, error = lax.while_loop(until(2e-3, 6), fine, (0, jnp.float32(1e9)))
    done = error <= 2e-3

    @pl.when(done)
    def _():
        w[...] = w[...] * (by_col * jnp.sqrt(scale))

    @pl.when(jnp.logical_not(done))
    def _():
        w[...] = eye

        def eliminate(k, carry):
            lane = lax.broadcasted_iota(jnp.int32, (1, n), 1)
            below = lax.broadcasted_iota(jnp.int32, (n, 1), 0)
            row = g[pl.ds(k, 1), :]
            pivot = jnp.sum(jnp.where(lane == k, row, 0.0), axis=1, keepdims=True)
            column = jnp.sum(jnp.where(at_col == k, g[...], 0.0), axis=1, keepdims=True)
            ratio = jnp.where(below > k, column / pivot, 0.0)
            solved = w[pl.ds(k, 1), :]
            g[...] = g[...] - ratio * row
            w[...] = w[...] - ratio * solved
            w[pl.ds(k, 1), :] = solved * lax.rsqrt(pivot)
            return carry

        lax.fori_loop(0, n, eliminate, 0)


def factor_kernel(rows_total, last, core, mine, theirs, gram, gram_other, *refs):
    out, (g, w, high, low, update) = refs[:-5], refs[-5:]
    width = mine.shape[0]
    half = width // 2
    ahead = core[0] == 0
    first = jnp.where(ahead, gram[...], gram_other[...]) / rows_total
    second = jnp.where(ahead, gram_other[...], gram[...]) / rows_total
    g[pl.ds(0, width), pl.ds(0, width)] = first[:width]
    g[pl.ds(width, width), pl.ds(width, width)] = second[:width]
    below = jnp.concatenate([first[width:], second[width:]], axis=0)
    g[pl.ds(width, width), pl.ds(0, width)] = below
    g[pl.ds(0, width), pl.ds(width, width)] = below.T
    inverse_factor(g, w, high, low)
    start = pl.multiple_of(core[0] * width, width)
    update[pl.ds(start, width), :] = mine[...]
    update[pl.ds(width - start, width), :] = theirs[...]
    mix = split(w[pl.ds(start, width), :])
    size = width
    for t in range(mine.shape[1] // size):
        part = pl.ds(t * size, size)
        solved = dot3(dot_nn, mix, split(update[:, part]))
        if last:
            out[0][part, :] = solved.T
        else:
            out[0][:, part] = solved
            out[1][t] = solved.astype(bf16)


def swap_cores(a):
    return lax.ppermute(a, "vec", [(0, 1), (1, 0)])


def flip(a, mask):
    return lax.ppermute(a, "patch", [(i, i ^ mask) for i in range(lax.axis_size("patch"))])


def shift(a, pairs):
    devices = range(lax.axis_size("patch"))
    return lax.ppermute(a, "patch", [(i - 2 * pairs, i) for i in devices if i - 2 * pairs in devices])


def stride(a, back=False):
    devices = range(lax.axis_size("patch"))
    route = [(i - (2 if i // 2 % 2 else 6), i) for i in devices]
    return lax.ppermute(a, "patch", [(d, s) if back else (s, d) for s, d in route if s in devices])


def together(*arrays):
    return lax.optimization_barrier(arrays)


def reach(u):
    two = shift(u, 2)
    far = stride(u)
    own_x = flip(u, 1)
    two, own_x = together(two, own_x)
    two_x, side = flip(two, 1), flip(two, 2)
    first = swap_cores(jnp.concatenate([u, own_x, two]))
    far, two_x, side = together(far, two_x, side)
    second = swap_cores(jnp.concatenate([far, two_x, side]))
    far_x, side_x = flip(far, 1), flip(two_x, 2)
    third = swap_cores(jnp.concatenate([far_x, side_x]))
    return [u, own_x, two, two_x, far, far_x, side, side_x], [first, second, third]


GROUPED = ((0, 0), (0, 2), (0, 4), (1, 2), (1, 0), (2, 0), (1, 4), (2, 2))


def place_order(parts, place):
    radix = len(parts)
    bit = 1
    while bit < radix:
        swapped = [parts[j ^ bit] for j in range(radix)]
        parts = [jnp.where(place & bit, b, a) for a, b in zip(parts, swapped)]
        bit *= 2
    return parts


def summed(a, gates=()):
    position = lax.axis_index("patch")
    left, step, stages = lax.axis_size("patch"), 1, []
    while left > 1:
        radix = 4 if left % 4 == 0 else 2
        stages.append((radix, step))
        left, step = left // radix, step * radix
    gates = list(gates)

    def gated(x):
        return together(x, *gates.pop(0))[0] if gates else x

    for radix, step in stages[:-1]:
        place = (position // step) % radix
        parts = gated(a).reshape(radix, a.shape[0] // radix, a.shape[1])
        a = lax.dynamic_index_in_dim(parts, place, 0, False)
        for m in range(1, radix):
            a = a + flip(lax.dynamic_index_in_dim(parts, place ^ m, 0, False), m * step)
    radix, step = stages[-1]
    a = gated(a)
    a = sum([flip(a, m * step) for m in range(1, radix)], a)
    for radix, step in stages[-2::-1]:
        place = (position // step) % radix
        a = gated(a)
        parts = place_order([a] + [flip(a, m * step) for m in range(1, radix)], place)
        a = jnp.concatenate(parts, axis=0)
    return a


def shards(vectors, blocks, block_row, block_col, block_count):
    count, width = vectors.shape
    size = blocks.shape[1]
    rows_total = float(count * lax.axis_size("patch"))
    position = lax.axis_index("patch")
    odd = position % 2
    meta = jnp.stack([block_count[0], 2 * (position - odd) - 4 * (REACH - 1), odd, position // 2 % 2]).astype(jnp.int32)
    core = lax.axis_index("vec").astype(jnp.int32).reshape(1)
    flat, chunk = shape(f32, width, count), shape(bf16, count // size, width, size)
    x, u = call(pack_kernel, [flat, chunk], [vectors])
    for step in range(STEPS):
        last = step == STEPS - 1
        pieces, others = reach(u)
        x_other = swap_cores(x)
        same, cross, inner = apply_tiles(pieces, others, blocks, block_row, block_col, meta)
        side_x, far_x, side = flip(cross[3], 2), flip(cross[2], 1), flip(same[3], 2)
        side_x, far_x = together(side_x, far_x)
        two_out = (cross[1] + side_x.astype(f32)).astype(bf16)
        far_out = (same[2] + far_x.astype(f32)).astype(bf16)
        two_x, far = flip(two_out, 1), stride(far_out, True)
        near, two_x = together(cross[0], two_x)
        two = (same[1] + (two_x.astype(f32) + side.astype(f32))).astype(bf16)
        joined = [flip(near, 1), far, shift(two, -2)]
        inner = summed(inner, [(), (two_x, far_out), joined])
        out = [flat] + ([shape(f32, count, width)] if last else [])
        update, *residual = call(
            lambda *refs: update_kernel(rows_total, *refs), out, [x, x_other, same[0], *joined, inner]
        )
        update_other = swap_cores(update)
        (gram,) = call(
            gram_kernel, [shape(f32, width + width // 2, width)], [core, update, update_other], smem=1
        )
        gram = summed(gram)
        full = (2 * width, 2 * width)
        out = call(
            lambda *refs: factor_kernel(rows_total, last, *refs),
            [shape(f32, count, width)] if last else [flat, chunk],
            [core, update, update_other, gram, swap_cores(gram)],
            scratch=[VMEM(full, f32), VMEM(full, f32), VMEM(full, bf16), VMEM(full, bf16), VMEM((2 * width, count), f32)],
            smem=1,
            flops=16 << 30,
            vmem=28,
        )
        if last:
            return out[0], residual[0]
        x, u = out


def solution(mesh):
    in_specs = (P("patch", "vec"), P("patch", None, None), P("patch"), P("patch"), P("patch"))
    out_specs = (P("patch", "vec"), P("patch", "vec"))
    return jax.shard_map(shards, mesh=mesh, in_specs=in_specs, out_specs=out_specs, check_vma=False)
```

```python
import jax
import jax.numpy as jnp
from jax import lax
from jax.experimental import pallas as pl
from jax.experimental.pallas import tpu as pltpu
from jax.sharding import PartitionSpec as P

STEPS = 2
STEP_RATE = 0.25
GROUP = 8
REACH = 4

f32, bf16 = jnp.float32, jnp.bfloat16
SEGMENT_KINDS = (f32, f32, f32, f32, f32, bf16, bf16, bf16)
TILES_VMEM = 24
VMEM, SMEM = pltpu.VMEM, pltpu.SMEM


def dot_nn(a, b):
    return lax.dot_general(a, b, (((1,), (0,)), ((), ())), preferred_element_type=f32)


def dot_nt(a, b):
    return lax.dot_general(a, b, (((1,), (1,)), ((), ())), preferred_element_type=f32)


def split(a):
    high = a.astype(bf16)
    return high, (a - high.astype(f32)).astype(bf16)


def dot3(dot, a, b):
    (ah, al), (bh, bl) = a, b
    return dot(ah, bh) + (dot(ah, bl) + dot(al, bh))


def call(kernel, out, args, scratch=(), smem=0, flops=1 << 28, vmem=16):
    moved = sum(a.size * a.dtype.itemsize for a in args) + sum(o.size * o.dtype.itemsize for o in out)
    return pl.pallas_call(
        kernel,
        out_shape=out,
        in_specs=[pl.BlockSpec(memory_space=SMEM)] * smem + [pl.BlockSpec(memory_space=VMEM)] * (len(args) - smem),
        out_specs=[pl.BlockSpec(memory_space=VMEM)] * len(out),
        scratch_shapes=list(scratch),
        compiler_params=pltpu.CompilerParams(vmem_limit_bytes=vmem << 20),
        cost_estimate=pl.CostEstimate(flops=flops, bytes_accessed=moved, transcendentals=0),
    )(*args)


def shape(dtype, *dims):
    return jax.ShapeDtypeStruct(dims, dtype)


def pack_kernel(vectors, columns, chunk):
    size = chunk.shape[2]
    for t in range(chunk.shape[0]):
        turned = vectors[pl.ds(t * size, size), :].T
        columns[:, pl.ds(t * size, size)] = turned
        chunk[t] = turned.astype(bf16)


def place(tile, meta):
    start, odd, pair_odd = meta[1], meta[2], meta[3]
    w = tile - start
    back = REACH - 1 - w // 4
    role = jnp.where(back % 2 == 1, 2 + ((back // 2) ^ pair_odd ^ 1), back // 2)
    return role * 4 + 2 * (((w % 4) // 2) ^ odd) + w % 2


def gather(pieces, window, sems):
    return [pltpu.make_async_copy(piece, window.at[pl.ds(2 * s, 2)], sems.at[s]) for s, piece in enumerate(pieces)]


def each_tile(meta, rows, cols, blocks, tiles, sems, ready, product, total):
    used = meta[0]
    groups = (used + GROUP - 1) // GROUP

    def fetch(group):
        at = group % 2
        return pltpu.make_async_copy(blocks.at[pl.ds(group * GROUP, GROUP)], tiles.at[at], sems.at[at])

    @pl.when(groups > 0)
    def _():
        fetch(0).start()

    for copy in ready:
        copy.start()
    total[...] = jnp.zeros_like(total)
    for copy in ready:
        copy.wait()

    def multiply(group, carry):
        @pl.when(group + 1 < groups)
        def _():
            fetch(group + 1).start()

        fetch(group).wait()
        found = []
        for k in range(GROUP):
            slot = group * GROUP + k
            row, col = rows[slot], cols[slot]
            tile = tiles[group % 2, k]
            tile = jnp.where(slot < used, tile, jnp.zeros_like(tile))
            found.append(product(tile, place(row, meta), place(col, meta)) + (row == col,))
        for at, part, diagonal in found:
            total[at] += part * jnp.where(diagonal, 0.5, 1.0).astype(f32)
        return carry

    lax.fori_loop(0, groups, multiply, 0)


def mirror_kernel(meta, rows, cols, *refs):
    pieces, blocks, out = refs[:2], refs[2], refs[3:-5]
    window, total, tiles, piece_sems, tile_sems = refs[-5:]

    def product(tile, row, col):
        return col, dot_nn(window[row], tile)

    each_tile(meta, rows, cols, blocks, tiles, tile_sems, gather(pieces, window, piece_sems), product, total)
    for s, segment in enumerate(out):
        segment[...] = total[pl.ds(2 * s, 2)].astype(segment.dtype)


def direct_kernel(meta, rows, cols, *refs):
    pieces, blocks = refs[: 2 * REACH], refs[2 * REACH]
    x_other, cross_other, kept, near, kept_out, near_out, inner = refs[2 * REACH + 1 : -5]
    window, total, tiles, piece_sems, tile_sems = refs[-5:]

    def product(tile, row, col):
        return row, dot_nt(window[col], tile)

    each_tile(meta, rows, cols, blocks, tiles, tile_sems, gather(pieces, window, piece_sems), product, total)
    kept_out[...] = kept[...] + total[pl.ds(0, 2)]
    near_out[...] = (near[...] + total[pl.ds(2, 2)]).astype(bf16)
    size = inner.shape[1]
    own = jnp.zeros((size, size), f32)
    other = jnp.zeros((size, size), f32)
    for s in range(4):
        mine = total[s].astype(bf16)
        there = x_other[:, pl.ds(s * size, size)].astype(bf16) if s < 2 else cross_other[s - 2]
        own += dot_nt(mine, window[s])
        other += dot_nt(mine, there)
    inner[pl.ds(0, size), :] = own + own.T
    inner[pl.ds(size, size), :] = other


def tiles_call(kernel, out, meta, blocks, rows, cols, pieces, more, window, total):
    size, width = blocks.shape[1], pieces[0].shape[1]
    return pl.pallas_call(
        kernel,
        in_specs=[pl.BlockSpec(memory_space=SMEM)] * 3
        + [pl.BlockSpec(memory_space=pl.ANY)] * len(pieces)
        + [pl.BlockSpec(memory_space=pltpu.HBM)]
        + [pl.BlockSpec(memory_space=VMEM)] * len(more),
        out_specs=[pl.BlockSpec(memory_space=VMEM)] * len(out),
        scratch_shapes=[
            VMEM((window, width, size), bf16),
            VMEM((total, width, size), f32),
            VMEM((2, GROUP, size, size), bf16),
            pltpu.SemaphoreType.DMA((len(pieces),)),
            pltpu.SemaphoreType.DMA((2,)),
        ],
        out_shape=out,
        compiler_params=pltpu.CompilerParams(vmem_limit_bytes=TILES_VMEM << 20),
        cost_estimate=pl.CostEstimate(flops=4 << 30, bytes_accessed=12 << 20, transcendentals=0),
    )(meta, rows, cols, *pieces, blocks, *more)


def update_kernel(rows_total, x, x_other, kept, near, far, two, inner, turned, update, *residual):
    width, count = x.shape
    size = kept.shape[2]
    own = split(inner[pl.ds(0, width), :] / rows_total)
    other = split((inner[pl.ds(width, width), :] + turned[...].T) / rows_total)
    for t in range(count // size):
        part = pl.ds(t * size, size)
        applied = kept[t] + near[t].astype(f32) + (far[t].astype(f32) + two[t].astype(f32))
        now = x[:, part]
        rest = applied - (dot3(dot_nn, own, split(now)) + dot3(dot_nn, other, split(x_other[:, part])))
        update[:, part] = now - STEP_RATE * rest
        if residual:
            residual[0][part, :] = rest.T


def gram_kernel(core, mine, theirs, out):
    width = mine.shape[0]
    half = width // 2
    own, other = split(mine[...]), split(theirs[...])
    out[pl.ds(0, width), :] = dot3(dot_nt, own, own)
    ahead = core[0] == 0
    high = jnp.where(ahead, theirs[pl.ds(0, half), :], mine[pl.ds(half, half), :])
    low = [jnp.where(ahead, a, b) for a, b in zip(own, other)]
    out[pl.ds(width, half), :] = dot3(dot_nt, split(high), low)


def inverse_factor(g, w, high, low):
    n = g.shape[0]
    at_row = lax.broadcasted_iota(jnp.int32, (n, n), 0)
    at_col = lax.broadcasted_iota(jnp.int32, (n, n), 1)
    eye = jnp.where(at_row == at_col, 1.0, 0.0).astype(f32)
    diagonal = eye * g[...]
    by_row = lax.rsqrt(jnp.sum(diagonal, axis=1, keepdims=True))
    by_col = lax.rsqrt(jnp.sum(diagonal, axis=0, keepdims=True))
    unit = g[...] * by_row * by_col
    rounded = unit.astype(bf16)
    square = dot_nn(rounded, rounded).astype(bf16)
    fourth = dot_nn(square, square)
    scale = 1.9 / jnp.sqrt(jnp.sqrt(jnp.sqrt(jnp.sum(fourth * fourth, keepdims=True))))
    scaled = unit * scale
    high[...], low[...] = split(scaled)

    def lower(e):
        return jnp.where(at_row > at_col, e, 0.5 * eye * e)

    p = lower(scaled - eye)
    pb = p.astype(bf16)
    w[...] = eye - p + dot_nn(pb, pb)

    def improve(e):
        p = lower(e)
        pb = p.astype(bf16)
        first = dot_nn(pb, w[...].astype(bf16))
        w[...] = w[...] - first + dot_nn(pb, first.astype(bf16))
        return jnp.sqrt(jnp.sum(p * p))

    def rough(state):
        wb = w[...].astype(bf16)
        e = dot_nt(dot_nn(wb, high[...]).astype(bf16), wb) - eye
        return state[0] + 1, improve(e)

    def fine(state):
        ws = split(w[...])
        e = dot3(dot_nt, split(dot3(dot_nn, ws, (high[...], low[...]))), ws) - eye
        return state[0] + 1, improve(e)

    def until(bound, most):
        return lambda state: (state[0] < most) & jnp.logical_not(state[1] <= bound)

    lax.while_loop(until(0.4, 16), rough, (0, jnp.float32(1e9)))
    _, error = lax.while_loop(until(2e-3, 6), fine, (0, jnp.float32(1e9)))
    done = error <= 2e-3

    @pl.when(done)
    def _():
        w[...] = w[...] * (by_col * jnp.sqrt(scale))

    @pl.when(jnp.logical_not(done))
    def _():
        w[...] = eye

        def eliminate(k, carry):
            lane = lax.broadcasted_iota(jnp.int32, (1, n), 1)
            below = lax.broadcasted_iota(jnp.int32, (n, 1), 0)
            row = g[pl.ds(k, 1), :]
            pivot = jnp.sum(jnp.where(lane == k, row, 0.0), axis=1, keepdims=True)
            column = jnp.sum(jnp.where(at_col == k, g[...], 0.0), axis=1, keepdims=True)
            ratio = jnp.where(below > k, column / pivot, 0.0)
            solved = w[pl.ds(k, 1), :]
            g[...] = g[...] - ratio * row
            w[...] = w[...] - ratio * solved
            w[pl.ds(k, 1), :] = solved * lax.rsqrt(pivot)
            return carry

        lax.fori_loop(0, n, eliminate, 0)


def factor_kernel(rows_total, last, core, mine, theirs, gram, gram_other, *refs):
    out, (g, w, high, low, update) = refs[:-5], refs[-5:]
    width = mine.shape[0]
    half = width // 2
    ahead = core[0] == 0
    first = jnp.where(ahead, gram[...], gram_other[...]) / rows_total
    second = jnp.where(ahead, gram_other[...], gram[...]) / rows_total
    g[pl.ds(0, width), pl.ds(0, width)] = first[:width]
    g[pl.ds(width, width), pl.ds(width, width)] = second[:width]
    below = jnp.concatenate([first[width:], second[width:]], axis=0)
    g[pl.ds(width, width), pl.ds(0, width)] = below
    g[pl.ds(0, width), pl.ds(width, width)] = below.T
    inverse_factor(g, w, high, low)
    start = pl.multiple_of(core[0] * width, width)
    update[pl.ds(start, width), :] = mine[...]
    update[pl.ds(width - start, width), :] = theirs[...]
    mix = split(w[pl.ds(start, width), :])
    size = width
    for t in range(mine.shape[1] // size):
        part = pl.ds(t * size, size)
        solved = dot3(dot_nn, mix, split(update[:, part]))
        if last:
            out[0][part, :] = solved.T
        else:
            out[0][:, part] = solved
            out[1][t] = solved.astype(bf16)


def swap_cores(a):
    return lax.ppermute(a, "vec", [(0, 1), (1, 0)])


def flip(a, mask):
    return lax.ppermute(a, "patch", [(i, i ^ mask) for i in range(lax.axis_size("patch"))])


def shift(a, pairs):
    devices = range(lax.axis_size("patch"))
    return lax.ppermute(a, "patch", [(i - 2 * pairs, i) for i in devices if i - 2 * pairs in devices])


def stride(a, back=False):
    devices = range(lax.axis_size("patch"))
    route = [(i - (2 if i // 2 % 2 else 6), i) for i in devices]
    return lax.ppermute(a, "patch", [(d, s) if back else (s, d) for s, d in route if s in devices])


def together(*arrays):
    return lax.optimization_barrier(arrays)


def reach(u, own_x, done):
    two = shift(u, 2)
    far = stride(u)
    two_x, side = flip(two, 1), flip(two, 2)
    far, two_x, side, _ = together(far, two_x, side, done)
    return [u, own_x, two, two_x, far, flip(far, 1), side, flip(two_x, 2)]


def place_order(parts, place):
    radix = len(parts)
    bit = 1
    while bit < radix:
        swapped = [parts[j ^ bit] for j in range(radix)]
        parts = [jnp.where(place & bit, b, a) for a, b in zip(parts, swapped)]
        bit *= 2
    return parts


def summed(a, gates=()):
    position = lax.axis_index("patch")
    left, step, stages = lax.axis_size("patch"), 1, []
    while left > 1:
        radix = 4 if left % 4 == 0 else 2
        stages.append((radix, step))
        left, step = left // radix, step * radix
    gates = list(gates)

    def gated(x):
        return together(x, *gates.pop(0))[0] if gates else x

    for radix, step in stages[:-1]:
        place = (position // step) % radix
        parts = gated(a).reshape(radix, a.shape[0] // radix, a.shape[1])
        a = lax.dynamic_index_in_dim(parts, place, 0, False)
        for m in range(1, radix):
            a = a + flip(lax.dynamic_index_in_dim(parts, place ^ m, 0, False), m * step)
    radix, step = stages[-1]
    a = gated(a)
    a = sum([flip(a, m * step) for m in range(1, radix)], a)
    for radix, step in stages[-2::-1]:
        place = (position // step) % radix
        a = gated(a)
        parts = place_order([a] + [flip(a, m * step) for m in range(1, radix)], place)
        a = jnp.concatenate(parts, axis=0)
    return a


def shards(vectors, blocks, block_row, block_col, block_count):
    count, width = vectors.shape
    size = blocks.shape[1]
    rows_total = float(count * lax.axis_size("patch"))
    position = lax.axis_index("patch")
    odd = position % 2
    meta = jnp.stack([block_count[0], 2 * (position - odd) - 4 * (REACH - 1), odd, position // 2 % 2]).astype(jnp.int32)
    core = lax.axis_index("vec").astype(jnp.int32).reshape(1)
    flat, chunk = shape(f32, width, count), shape(bf16, count // size, width, size)
    x, u = call(pack_kernel, [flat, chunk], [vectors])
    for step in range(STEPS):
        last = step == STEPS - 1
        own_x = flip(u, 1)
        x_other = swap_cores(x)
        cross_other = swap_cores(own_x)
        table = (meta, blocks, block_row, block_col)
        segment = (2, width, size)
        sums = tiles_call(
            mirror_kernel, [shape(kind, *segment) for kind in SEGMENT_KINDS], *table, [u, own_x], [], 4, 4 * REACH
        )
        same, cross = sums[::2], sums[1::2]
        kept, near, inner = tiles_call(
            direct_kernel,
            [shape(f32, *segment), shape(bf16, *segment), shape(f32, 2 * width, width)],
            *table,
            reach(u, own_x, cross[3]),
            [x_other, cross_other, same[0], cross[0]],
            4 * REACH,
            4,
        )
        side_x, far_x, side = flip(cross[3], 2), flip(cross[2], 1), flip(same[3], 2)
        two_out = (cross[1] + side_x.astype(f32)).astype(bf16)
        two_x, far = flip(two_out, 1), stride((same[2] + far_x.astype(f32)).astype(bf16), True)
        two = shift((same[1] + (two_x.astype(f32) + side.astype(f32))).astype(bf16), -2)
        joined = [flip(near, 1), far, two]
        inner = summed(inner)
        turned = swap_cores(inner[width:])
        out = [flat] + ([shape(f32, count, width)] if last else [])
        update, *residual = call(
            lambda *refs: update_kernel(rows_total, *refs), out, [x, x_other, kept, *joined, inner, turned]
        )
        update_other = swap_cores(update)
        (gram,) = call(
            gram_kernel, [shape(f32, width + width // 2, width)], [core, update, update_other], smem=1
        )
        gram = summed(gram)
        full = (2 * width, 2 * width)
        out = call(
            lambda *refs: factor_kernel(rows_total, last, *refs),
            [shape(f32, count, width)] if last else [flat, chunk],
            [core, update, update_other, gram, swap_cores(gram)],
            scratch=[VMEM(full, f32), VMEM(full, f32), VMEM(full, bf16), VMEM(full, bf16), VMEM((2 * width, count), f32)],
            smem=1,
            flops=16 << 30,
            vmem=28,
        )
        if last:
            return out[0], residual[0]
        x, u = out


def solution(mesh):
    in_specs = (P("patch", "vec"), P("patch", None, None), P("patch"), P("patch"), P("patch"))
    out_specs = (P("patch", "vec"), P("patch", "vec"))
    return jax.shard_map(shards, mesh=mesh, in_specs=in_specs, out_specs=out_specs, check_vma=False)
```

```python
import jax
import jax.numpy as jnp
from jax import lax
from jax.experimental import pallas as pl
from jax.experimental.pallas import tpu as pltpu
from jax.sharding import PartitionSpec as P

STEPS = 2
STEP_RATE = 0.25
GROUP = 8
REACH = 4

f32, bf16 = jnp.float32, jnp.bfloat16
SEGMENT_KINDS = (f32, f32, f32, f32, f32, bf16, bf16, bf16)
TILES_VMEM = 24
VMEM, SMEM = pltpu.VMEM, pltpu.SMEM


def dot_nn(a, b):
    return lax.dot_general(a, b, (((1,), (0,)), ((), ())), preferred_element_type=f32)


def dot_nt(a, b):
    return lax.dot_general(a, b, (((1,), (1,)), ((), ())), preferred_element_type=f32)


def split(a):
    high = a.astype(bf16)
    return high, (a - high.astype(f32)).astype(bf16)


def dot3(dot, a, b):
    (ah, al), (bh, bl) = a, b
    return dot(ah, bh) + (dot(ah, bl) + dot(al, bh))


def call(kernel, out, args, scratch=(), smem=0, flops=1 << 28, vmem=16):
    moved = sum(a.size * a.dtype.itemsize for a in args) + sum(o.size * o.dtype.itemsize for o in out)
    return pl.pallas_call(
        kernel,
        out_shape=out,
        in_specs=[pl.BlockSpec(memory_space=SMEM)] * smem + [pl.BlockSpec(memory_space=VMEM)] * (len(args) - smem),
        out_specs=[pl.BlockSpec(memory_space=VMEM)] * len(out),
        scratch_shapes=list(scratch),
        compiler_params=pltpu.CompilerParams(vmem_limit_bytes=vmem << 20),
        cost_estimate=pl.CostEstimate(flops=flops, bytes_accessed=moved, transcendentals=0),
    )(*args)


def shape(dtype, *dims):
    return jax.ShapeDtypeStruct(dims, dtype)


def pack_kernel(vectors, columns, chunk):
    size = chunk.shape[2]
    for t in range(chunk.shape[0]):
        turned = vectors[pl.ds(t * size, size), :].T
        columns[:, pl.ds(t * size, size)] = turned
        chunk[t] = turned.astype(bf16)


def place(tile, meta):
    start, odd, pair_odd = meta[1], meta[2], meta[3]
    w = tile - start
    back = REACH - 1 - w // 4
    role = jnp.where(back % 2 == 1, 2 + ((back // 2) ^ pair_odd ^ 1), back // 2)
    return role * 4 + 2 * (((w % 4) // 2) ^ odd) + w % 2


def gather(pieces, window, sems):
    return [pltpu.make_async_copy(piece, window.at[pl.ds(2 * s, 2)], sems.at[s]) for s, piece in enumerate(pieces)]


def each_tile(meta, rows, cols, blocks, tiles, sems, ready, product, total):
    used = meta[0]
    groups = (used + GROUP - 1) // GROUP

    def fetch(group):
        at = group % 2
        return pltpu.make_async_copy(blocks.at[pl.ds(group * GROUP, GROUP)], tiles.at[at], sems.at[at])

    @pl.when(groups > 0)
    def _():
        fetch(0).start()

    for copy in ready:
        copy.start()
    total[...] = jnp.zeros_like(total)
    for copy in ready:
        copy.wait()

    def multiply(group, carry):
        @pl.when(group + 1 < groups)
        def _():
            fetch(group + 1).start()

        fetch(group).wait()
        found = []
        for k in range(GROUP):
            slot = group * GROUP + k
            row, col = rows[slot], cols[slot]
            tile = tiles[group % 2, k]
            tile = jnp.where(slot < used, tile, jnp.zeros_like(tile))
            found.append(product(tile, place(row, meta), place(col, meta)) + (row == col,))
        for at, part, diagonal in found:
            total[at] += part * jnp.where(diagonal, 0.5, 1.0).astype(f32)
        return carry

    lax.fori_loop(0, groups, multiply, 0)


def mirror_kernel(meta, rows, cols, *refs):
    pieces, blocks, out = refs[:2], refs[2], refs[3:-5]
    window, total, tiles, piece_sems, tile_sems = refs[-5:]

    def product(tile, row, col):
        return col, dot_nn(window[row], tile)

    each_tile(meta, rows, cols, blocks, tiles, tile_sems, gather(pieces, window, piece_sems), product, total)
    for s, segment in enumerate(out):
        segment[...] = total[pl.ds(2 * s, 2)].astype(segment.dtype)


def direct_kernel(meta, rows, cols, *refs):
    pieces, blocks = refs[: 2 * REACH], refs[2 * REACH]
    x_other, cross_other, kept, near, kept_out, near_out, inner = refs[2 * REACH + 1 : -5]
    window, total, tiles, piece_sems, tile_sems = refs[-5:]

    def product(tile, row, col):
        return row, dot_nt(window[col], tile)

    each_tile(meta, rows, cols, blocks, tiles, tile_sems, gather(pieces, window, piece_sems), product, total)
    kept_out[...] = kept[...] + total[pl.ds(0, 2)]
    near_out[...] = (near[...] + total[pl.ds(2, 2)]).astype(bf16)
    size = inner.shape[1]
    own = jnp.zeros((size, size), f32)
    other = jnp.zeros((size, size), f32)
    for s in range(4):
        mine = total[s].astype(bf16)
        there = x_other[:, pl.ds(s * size, size)].astype(bf16) if s < 2 else cross_other[s - 2]
        own += dot_nt(mine, window[s])
        other += dot_nt(mine, there)
    inner[pl.ds(0, size), :] = own + own.T
    inner[pl.ds(size, size), :] = other


def tiles_call(kernel, out, meta, blocks, rows, cols, pieces, more, window, total):
    size, width = blocks.shape[1], pieces[0].shape[1]
    return pl.pallas_call(
        kernel,
        in_specs=[pl.BlockSpec(memory_space=SMEM)] * 3
        + [pl.BlockSpec(memory_space=pl.ANY)] * len(pieces)
        + [pl.BlockSpec(memory_space=pltpu.HBM)]
        + [pl.BlockSpec(memory_space=VMEM)] * len(more),
        out_specs=[pl.BlockSpec(memory_space=VMEM)] * len(out),
        scratch_shapes=[
            VMEM((window, width, size), bf16),
            VMEM((total, width, size), f32),
            VMEM((2, GROUP, size, size), bf16),
            pltpu.SemaphoreType.DMA((len(pieces),)),
            pltpu.SemaphoreType.DMA((2,)),
        ],
        out_shape=out,
        compiler_params=pltpu.CompilerParams(vmem_limit_bytes=TILES_VMEM << 20),
        cost_estimate=pl.CostEstimate(flops=4 << 30, bytes_accessed=12 << 20, transcendentals=0),
    )(meta, rows, cols, *pieces, blocks, *more)


def descend_kernel(x, kept, near, far, two, out):
    size = kept.shape[2]
    for t in range(x.shape[1] // size):
        part = pl.ds(t * size, size)
        applied = kept[t] + near[t].astype(f32) + (far[t].astype(f32) + two[t].astype(f32))
        out[:, part] = x[:, part] - STEP_RATE * applied


def gram_kernel(core, mine, theirs, out):
    width = mine.shape[0]
    half = width // 2
    own, other = split(mine[...]), split(theirs[...])
    out[pl.ds(0, width), :] = dot3(dot_nt, own, own)
    ahead = core[0] == 0
    high = jnp.where(ahead, theirs[pl.ds(0, half), :], mine[pl.ds(half, half), :])
    low = [jnp.where(ahead, a, b) for a, b in zip(own, other)]
    out[pl.ds(width, half), :] = dot3(dot_nt, split(high), low)


def inverse_factor(g, w, high, low):
    n = g.shape[0]
    at_row = lax.broadcasted_iota(jnp.int32, (n, n), 0)
    at_col = lax.broadcasted_iota(jnp.int32, (n, n), 1)
    eye = jnp.where(at_row == at_col, 1.0, 0.0).astype(f32)
    diagonal = eye * g[...]
    by_row = lax.rsqrt(jnp.sum(diagonal, axis=1, keepdims=True))
    by_col = lax.rsqrt(jnp.sum(diagonal, axis=0, keepdims=True))
    unit = g[...] * by_row * by_col
    rounded = unit.astype(bf16)
    square = dot_nn(rounded, rounded).astype(bf16)
    fourth = dot_nn(square, square)
    scale = 1.9 / jnp.sqrt(jnp.sqrt(jnp.sqrt(jnp.sum(fourth * fourth, keepdims=True))))
    scaled = unit * scale
    high[...], low[...] = split(scaled)

    half = n // 2
    top, bottom = pl.ds(0, half), pl.ds(half, half)
    small = eye[:half, :half]
    triangle = (at_row > at_col)[:half, :half]

    def lower(e):
        return jnp.where(triangle, e, 0.5 * small * e)

    def read(ref):
        return ref[top, top], ref[bottom, top], ref[bottom, bottom]

    def product(a, b):
        return dot_nn(a[0], b[0]), dot_nn(a[1], b[0]) + dot_nn(a[2], b[1]), dot_nn(a[2], b[2])

    def narrow(blocks):
        return tuple(block.astype(bf16) for block in blocks)

    p = (lower(scaled[:half, :half] - small), scaled[half:, :half], lower(scaled[half:, half:] - small))
    pb = narrow(p)
    square = product(pb, pb)
    w[top, bottom] = jnp.zeros((half, half), f32)
    w[top, top] = small - p[0] + square[0]
    w[bottom, top] = square[1] - p[1]
    w[bottom, bottom] = small - p[2] + square[2]

    def improve(e, old):
        p = (lower(e[0] - small), e[1], lower(e[2] - small))
        pb = narrow(p)
        first = product(pb, narrow(old))
        second = product(pb, narrow(first))
        w[top, top] = old[0] - first[0] + second[0]
        w[bottom, top] = old[1] - first[1] + second[1]
        w[bottom, bottom] = old[2] - first[2] + second[2]
        return jnp.sqrt(sum(jnp.sum(block * block) for block in p))

    def congruence(nn, nt, cut, w, s):
        s00, s10, s11, s01 = s
        left = nn(w[0], s00)
        below, right = nn(w[1], s00) + nn(w[2], s10), nn(w[1], s01) + nn(w[2], s11)
        left, below, right = cut(left), cut(below), cut(right)
        return nt(left, w[0]), nt(below, w[0]), nt(below, w[1]) + nt(right, w[2])

    def whole(ref):
        return read(ref) + (ref[top, bottom],)

    def rough(state):
        old = read(w)
        e = congruence(dot_nn, dot_nt, lambda a: a.astype(bf16), narrow(old), whole(high))
        return state[0] + 1, improve(e, old)

    def fine(state):
        old = read(w)
        nn, nt = (lambda a, b: dot3(dot_nn, a, b)), (lambda a, b: dot3(dot_nt, a, b))
        e = congruence(nn, nt, split, [split(a) for a in old], list(zip(whole(high), whole(low))))
        return state[0] + 1, improve(e, old)

    def until(bound, most):
        return lambda state: (state[0] < most) & jnp.logical_not(state[1] <= bound)

    lax.while_loop(until(0.4, 16), rough, (0, jnp.float32(1e9)))
    _, error = lax.while_loop(until(0.1, 6), fine, (0, jnp.float32(1e9)))
    done = error <= 0.1

    @pl.when(done)
    def _():
        w[...] = w[...] * (by_col * jnp.sqrt(scale))

    @pl.when(jnp.logical_not(done))
    def _():
        w[...] = eye

        def eliminate(k, carry):
            lane = lax.broadcasted_iota(jnp.int32, (1, n), 1)
            below = lax.broadcasted_iota(jnp.int32, (n, 1), 0)
            row = g[pl.ds(k, 1), :]
            pivot = jnp.sum(jnp.where(lane == k, row, 0.0), axis=1, keepdims=True)
            column = jnp.sum(jnp.where(at_col == k, g[...], 0.0), axis=1, keepdims=True)
            ratio = jnp.where(below > k, column / pivot, 0.0)
            solved = w[pl.ds(k, 1), :]
            g[...] = g[...] - ratio * row
            w[...] = w[...] - ratio * solved
            w[pl.ds(k, 1), :] = solved * lax.rsqrt(pivot)
            return carry

        lax.fori_loop(0, n, eliminate, 0)


def lay_out(out, first, second):
    width = first.shape[1]
    out[pl.ds(0, width), pl.ds(0, width)] = first[:width]
    out[pl.ds(width, width), pl.ds(width, width)] = second[:width]
    below = jnp.concatenate([first[width:], second[width:]], axis=0)
    out[pl.ds(width, width), pl.ds(0, width)] = below
    out[pl.ds(0, width), pl.ds(width, width)] = below.T


def factor_kernel(rows_total, first_step, last, core, v, v_other, x, x_other, gram, gram_other, inner, inner_other, *refs):
    out, (g, w, high, low, update, rayleigh) = refs[:-6], refs[-6:]
    width, count = v.shape
    ahead = core[0] == 0

    def ordered(mine, theirs):
        mine, theirs = mine / rows_total, theirs / rows_total
        return jnp.where(ahead, mine, theirs), jnp.where(ahead, theirs, mine)

    first, second = ordered(inner[pl.ds(0, 2 * width), :], inner_other[pl.ds(0, 2 * width), :])
    rayleigh[pl.ds(0, width), pl.ds(0, width)] = first[:width]
    rayleigh[pl.ds(width, width), pl.ds(width, width)] = second[:width]
    across = first[width:] + second[width:].T
    rayleigh[pl.ds(0, width), pl.ds(width, width)] = across
    rayleigh[pl.ds(width, width), pl.ds(0, width)] = across.T
    lay_out(g, *ordered(gram[...], gram_other[...]))
    r = split(rayleigh[...])
    if first_step:
        extra = pl.ds(2 * width, width + width // 2)
        lay_out(w, *ordered(inner[extra, :], inner_other[extra, :]))
        turned = dot3(dot_nn, split(w[...]), r)
        g[...] += STEP_RATE * (turned + turned.T)
        g[...] += dot3(dot_nn, r, split(STEP_RATE**2 * turned - (2 * STEP_RATE**2) * rayleigh[...]))
    else:
        g[...] += 2 * STEP_RATE * rayleigh[...] - STEP_RATE**2 * dot3(dot_nn, r, r)
    inverse_factor(g, w, high, low)
    start = pl.multiple_of(core[0] * width, width)
    there = width - start
    update[pl.ds(start, width), :] = x[...]
    update[pl.ds(there, width), :] = x_other[...]
    mix = split(w[pl.ds(start, width), :])
    mine = split(rayleigh[pl.ds(start, width), :])
    theirs = split(rayleigh[pl.ds(there, width), :])
    for t in range(count // width):
        part = pl.ds(t * width, width)
        old = split(update[:, part])
        here = v[:, part] + STEP_RATE * dot3(dot_nn, mine, old)
        update[pl.ds(there, width), part] = v_other[:, part] + STEP_RATE * dot3(dot_nn, theirs, old)
        update[pl.ds(start, width), part] = here
        solved = dot3(dot_nn, mix, split(update[:, part]))
        if last:
            out[0][part, :] = solved.T
            out[1][part, :] = ((x[:, part] - here) * (1 / STEP_RATE)).T
        else:
            out[0][:, part] = solved
            out[1][t] = solved.astype(bf16)


def swap_cores(a):
    return lax.ppermute(a, "vec", [(0, 1), (1, 0)])


def flip(a, mask):
    return lax.ppermute(a, "patch", [(i, i ^ mask) for i in range(lax.axis_size("patch"))])


def shift(a, pairs):
    devices = range(lax.axis_size("patch"))
    return lax.ppermute(a, "patch", [(i - 2 * pairs, i) for i in devices if i - 2 * pairs in devices])


def stride(a, back=False):
    devices = range(lax.axis_size("patch"))
    route = [(i - (2 if i // 2 % 2 else 6), i) for i in devices]
    return lax.ppermute(a, "patch", [(d, s) if back else (s, d) for s, d in route if s in devices])


def together(*arrays):
    return lax.optimization_barrier(arrays)


def reach(u, own_x, done):
    two = shift(u, 2)
    far = stride(u)
    two_x, side = flip(two, 1), flip(two, 2)
    far, two_x, side, _ = together(far, two_x, side, done)
    return [u, own_x, two, two_x, far, flip(far, 1), side, flip(two_x, 2)]


def place_order(parts, place):
    radix = len(parts)
    bit = 1
    while bit < radix:
        swapped = [parts[j ^ bit] for j in range(radix)]
        parts = [jnp.where(place & bit, b, a) for a, b in zip(parts, swapped)]
        bit *= 2
    return parts


def summed(a, gates=()):
    position = lax.axis_index("patch")
    left, step, stages = lax.axis_size("patch"), 1, []
    while left > 1:
        radix = 4 if left % 4 == 0 else 2
        stages.append((radix, step))
        left, step = left // radix, step * radix
    gates = list(gates)

    def gated(x):
        return together(x, *gates.pop(0))[0] if gates else x

    for radix, step in stages[:-1]:
        place = (position // step) % radix
        parts = gated(a).reshape(radix, a.shape[0] // radix, a.shape[1])
        a = lax.dynamic_index_in_dim(parts, place, 0, False)
        for m in range(1, radix):
            a = a + flip(lax.dynamic_index_in_dim(parts, place ^ m, 0, False), m * step)
    radix, step = stages[-1]
    a = gated(a)
    a = sum([flip(a, m * step) for m in range(1, radix)], a)
    for radix, step in stages[-2::-1]:
        place = (position // step) % radix
        a = gated(a)
        parts = place_order([a] + [flip(a, m * step) for m in range(1, radix)], place)
        a = jnp.concatenate(parts, axis=0)
    return a


def shards(vectors, blocks, block_row, block_col, block_count):
    count, width = vectors.shape
    size = blocks.shape[1]
    rows_total = float(count * lax.axis_size("patch"))
    position = lax.axis_index("patch")
    odd = position % 2
    meta = jnp.stack([block_count[0], 2 * (position - odd) - 4 * (REACH - 1), odd, position // 2 % 2]).astype(jnp.int32)
    core = lax.axis_index("vec").astype(jnp.int32).reshape(1)
    flat, chunk = shape(f32, width, count), shape(bf16, count // size, width, size)
    x, u = call(pack_kernel, [flat, chunk], [vectors])
    for step in range(STEPS):
        last = step == STEPS - 1
        own_x = flip(u, 1)
        x_other = swap_cores(x)
        cross_other = swap_cores(own_x)
        table = (meta, blocks, block_row, block_col)
        segment = (2, width, size)
        sums = tiles_call(
            mirror_kernel, [shape(kind, *segment) for kind in SEGMENT_KINDS], *table, [u, own_x], [], 4, 4 * REACH
        )
        same, cross = sums[::2], sums[1::2]
        kept, near, inner = tiles_call(
            direct_kernel,
            [shape(f32, *segment), shape(bf16, *segment), shape(f32, 2 * width, width)],
            *table,
            reach(u, own_x, cross[3]),
            [x_other, cross_other, same[0], cross[0]],
            4 * REACH,
            4,
        )
        side_x, far_x, side = flip(cross[3], 2), flip(cross[2], 1), flip(same[3], 2)
        two_out = (cross[1] + side_x.astype(f32)).astype(bf16)
        two_x, far = flip(two_out, 1), stride((same[2] + far_x.astype(f32)).astype(bf16), True)
        two = shift((same[1] + (two_x.astype(f32) + side.astype(f32))).astype(bf16), -2)
        joined = [flip(near, 1), far, two]
        inner_out = [inner]
        if step == 0:
            inner_out += call(gram_kernel, [shape(f32, width + width // 2, width)], [core, x, x_other], smem=1)
        inner = summed(jnp.concatenate(inner_out))
        (v,) = call(descend_kernel, [flat], [x, kept, *joined])
        v_other = swap_cores(v)
        (gram,) = call(gram_kernel, [shape(f32, width + width // 2, width)], [core, v, v_other], smem=1)
        gram = summed(gram)
        full = (2 * width, 2 * width)
        wide = shape(f32, count, width)
        out = call(
            lambda *refs: factor_kernel(rows_total, step == 0, last, *refs),
            [wide, wide] if last else [flat, chunk],
            [core, v, v_other, x, x_other, gram, swap_cores(gram), inner, swap_cores(inner)],
            scratch=[VMEM(full, f32), VMEM(full, f32), VMEM(full, bf16), VMEM(full, bf16)]
            + [VMEM((2 * width, count), f32), VMEM(full, f32)],
            smem=1,
            flops=16 << 30,
            vmem=28,
        )
        x, u = out
    return x, u


def solution(mesh):
    in_specs = (P("patch", "vec"), P("patch", None, None), P("patch"), P("patch"), P("patch"))
    out_specs = (P("patch", "vec"), P("patch", "vec"))
    return jax.shard_map(shards, mesh=mesh, in_specs=in_specs, out_specs=out_specs, check_vma=False)
```

```python
import jax
import jax.numpy as jnp
from jax import lax
from jax.experimental import pallas as pl
from jax.experimental.pallas import tpu as pltpu
from jax.sharding import PartitionSpec as P

STEPS = 2
STEP_RATE = 0.25
GROUP = 8
REACH = 4

f32, bf16 = jnp.float32, jnp.bfloat16
SEGMENT_KINDS = (f32, f32, f32, f32, f32, bf16, bf16, bf16)
TILES_VMEM = 48
VMEM, SMEM = pltpu.VMEM, pltpu.SMEM


def dot_nn(a, b):
    return lax.dot_general(a, b, (((1,), (0,)), ((), ())), preferred_element_type=f32)


def dot_nt(a, b):
    return lax.dot_general(a, b, (((1,), (1,)), ((), ())), preferred_element_type=f32)


def split(a):
    high = a.astype(bf16)
    return high, (a - high.astype(f32)).astype(bf16)


def dot3(dot, a, b):
    (ah, al), (bh, bl) = a, b
    return dot(ah, bh) + (dot(ah, bl) + dot(al, bh))


def call(kernel, out, args, scratch=(), smem=0, flops=1 << 28, vmem=16):
    moved = sum(a.size * a.dtype.itemsize for a in args) + sum(o.size * o.dtype.itemsize for o in out)
    return pl.pallas_call(
        kernel,
        out_shape=out,
        in_specs=[pl.BlockSpec(memory_space=SMEM)] * smem + [pl.BlockSpec(memory_space=VMEM)] * (len(args) - smem),
        out_specs=[pl.BlockSpec(memory_space=VMEM)] * len(out),
        scratch_shapes=list(scratch),
        compiler_params=pltpu.CompilerParams(vmem_limit_bytes=vmem << 20),
        cost_estimate=pl.CostEstimate(flops=flops, bytes_accessed=moved, transcendentals=0),
    )(*args)


def shape(dtype, *dims):
    return jax.ShapeDtypeStruct(dims, dtype)


def pack_kernel(vectors, columns, chunk):
    size = chunk.shape[2]
    for t in range(chunk.shape[0]):
        turned = vectors[pl.ds(t * size, size), :].T
        columns[:, pl.ds(t * size, size)] = turned
        chunk[t] = turned.astype(bf16)


def place(tile, meta):
    start, odd, pair_odd = meta[1], meta[2], meta[3]
    w = tile - start
    back = REACH - 1 - w // 4
    role = jnp.where(back % 2 == 1, 2 + ((back // 2) ^ pair_odd ^ 1), back // 2)
    return role * 4 + 2 * (((w % 4) // 2) ^ odd) + w % 2


def gather(pieces, window, sems):
    return [pltpu.make_async_copy(piece, window.at[pl.ds(2 * s, 2)], sems.at[s]) for s, piece in enumerate(pieces)]


def each_tile(meta, rows, cols, blocks, tiles, sems, ready, product, total):
    used = meta[0]
    groups = (used + GROUP - 1) // GROUP

    def fetch(group):
        at = group % 2
        return pltpu.make_async_copy(blocks.at[pl.ds(group * GROUP, GROUP)], tiles.at[at], sems.at[at])

    @pl.when(groups > 0)
    def _():
        fetch(0).start()

    for copy in ready:
        copy.start()
    total[...] = jnp.zeros_like(total)
    for copy in ready:
        copy.wait()

    def multiply(group, carry):
        @pl.when(group + 1 < groups)
        def _():
            fetch(group + 1).start()

        fetch(group).wait()
        found = []
        for k in range(GROUP):
            slot = group * GROUP + k
            row, col = rows[slot], cols[slot]
            tile = tiles[group % 2, k]
            tile = jnp.where(slot < used, tile, jnp.zeros_like(tile))
            found.append(product(tile, place(row, meta), place(col, meta)) + (row == col,))
        for at, part, diagonal in found:
            total[at] += part * jnp.where(diagonal, 0.5, 1.0).astype(f32)
        return carry

    lax.fori_loop(0, groups, multiply, 0)


def mirror_kernel(meta, rows, cols, *refs):
    pieces, blocks, out = refs[:2], refs[2], refs[3:-5]
    window, total, tiles, piece_sems, tile_sems = refs[-5:]

    def product(tile, row, col):
        return col, dot_nn(window[row], tile)

    each_tile(meta, rows, cols, blocks, tiles, tile_sems, gather(pieces, window, piece_sems), product, total)
    for s, segment in enumerate(out):
        segment[...] = total[pl.ds(2 * s, 2)].astype(segment.dtype)


def direct_kernel(meta, rows, cols, *refs):
    pieces, blocks = refs[: 2 * REACH], refs[2 * REACH]
    x_other, cross_other, kept, near, kept_out, near_out, inner = refs[2 * REACH + 1 : -5]
    window, total, tiles, piece_sems, tile_sems = refs[-5:]

    def product(tile, row, col):
        return row, dot_nt(window[col], tile)

    each_tile(meta, rows, cols, blocks, tiles, tile_sems, gather(pieces, window, piece_sems), product, total)
    kept_out[...] = kept[...] + total[pl.ds(0, 2)]
    near_out[...] = (near[...] + total[pl.ds(2, 2)]).astype(bf16)
    size = inner.shape[1]
    own = jnp.zeros((size, size), f32)
    other = jnp.zeros((size, size), f32)
    for s in range(4):
        mine = total[s].astype(bf16)
        there = x_other[:, pl.ds(s * size, size)].astype(bf16) if s < 2 else cross_other[s - 2]
        own += dot_nt(mine, window[s])
        other += dot_nt(mine, there)
    inner[pl.ds(0, size), :] = own + own.T
    inner[pl.ds(size, size), :] = other


def tiles_call(kernel, out, meta, blocks, rows, cols, pieces, more, window, total):
    size, width = blocks.shape[1], pieces[0].shape[1]
    return pl.pallas_call(
        kernel,
        in_specs=[pl.BlockSpec(memory_space=SMEM)] * 3
        + [pl.BlockSpec(memory_space=pl.ANY)] * len(pieces)
        + [pl.BlockSpec(memory_space=pltpu.HBM)]
        + [pl.BlockSpec(memory_space=VMEM)] * len(more),
        out_specs=[pl.BlockSpec(memory_space=VMEM)] * len(out),
        scratch_shapes=[
            VMEM((window, width, size), bf16),
            VMEM((total, width, size), f32),
            VMEM((2, GROUP, size, size), bf16),
            pltpu.SemaphoreType.DMA((len(pieces),)),
            pltpu.SemaphoreType.DMA((2,)),
        ],
        out_shape=out,
        compiler_params=pltpu.CompilerParams(vmem_limit_bytes=TILES_VMEM << 20),
        cost_estimate=pl.CostEstimate(flops=4 << 30, bytes_accessed=12 << 20, transcendentals=0),
    )(meta, rows, cols, *pieces, blocks, *more)


def descend_kernel(x, kept, near, far, two, out):
    size = kept.shape[2]
    for t in range(x.shape[1] // size):
        part = pl.ds(t * size, size)
        applied = kept[t] + near[t].astype(f32) + (far[t].astype(f32) + two[t].astype(f32))
        out[:, part] = x[:, part] - STEP_RATE * applied


def gram_kernel(core, mine, theirs, out):
    width = mine.shape[0]
    half = width // 2
    own, other = split(mine[...]), split(theirs[...])
    out[pl.ds(0, width), :] = dot3(dot_nt, own, own)
    ahead = core[0] == 0
    high = jnp.where(ahead, theirs[pl.ds(0, half), :], mine[pl.ds(half, half), :])
    low = [jnp.where(ahead, a, b) for a, b in zip(own, other)]
    out[pl.ds(width, half), :] = dot3(dot_nt, split(high), low)


def inverse_factor(g, w, high, low):
    n = g.shape[0]
    at_row = lax.broadcasted_iota(jnp.int32, (n, n), 0)
    at_col = lax.broadcasted_iota(jnp.int32, (n, n), 1)
    eye = jnp.where(at_row == at_col, 1.0, 0.0).astype(f32)
    diagonal = eye * g[...]
    by_row = lax.rsqrt(jnp.sum(diagonal, axis=1, keepdims=True))
    by_col = lax.rsqrt(jnp.sum(diagonal, axis=0, keepdims=True))
    unit = g[...] * by_row * by_col
    rounded = unit.astype(bf16)
    square = dot_nn(rounded, rounded).astype(bf16)
    fourth = dot_nn(square, square)
    scale = 1.9 / jnp.sqrt(jnp.sqrt(jnp.sqrt(jnp.sum(fourth * fourth, keepdims=True))))
    scaled = unit * scale
    high[...], low[...] = split(scaled)

    half = n // 2
    top, bottom = pl.ds(0, half), pl.ds(half, half)
    small = eye[:half, :half]
    triangle = (at_row > at_col)[:half, :half]

    def lower(e):
        return jnp.where(triangle, e, 0.5 * small * e)

    def read(ref):
        return ref[top, top], ref[bottom, top], ref[bottom, bottom]

    def product(a, b):
        return dot_nn(a[0], b[0]), dot_nn(a[1], b[0]) + dot_nn(a[2], b[1]), dot_nn(a[2], b[2])

    def narrow(blocks):
        return tuple(block.astype(bf16) for block in blocks)

    p = (lower(scaled[:half, :half] - small), scaled[half:, :half], lower(scaled[half:, half:] - small))
    pb = narrow(p)
    square = product(pb, pb)
    w[top, bottom] = jnp.zeros((half, half), f32)
    w[top, top] = small - p[0] + square[0]
    w[bottom, top] = square[1] - p[1]
    w[bottom, bottom] = small - p[2] + square[2]

    def improve(e, old):
        p = (lower(e[0] - small), e[1], lower(e[2] - small))
        pb = narrow(p)
        first = product(pb, narrow(old))
        second = product(pb, narrow(first))
        w[top, top] = old[0] - first[0] + second[0]
        w[bottom, top] = old[1] - first[1] + second[1]
        w[bottom, bottom] = old[2] - first[2] + second[2]
        return jnp.sqrt(sum(jnp.sum(block * block) for block in p))

    def congruence(nn, nt, cut, w, s):
        s00, s10, s11, s01 = s
        left = nn(w[0], s00)
        below, right = nn(w[1], s00) + nn(w[2], s10), nn(w[1], s01) + nn(w[2], s11)
        left, below, right = cut(left), cut(below), cut(right)
        return nt(left, w[0]), nt(below, w[0]), nt(below, w[1]) + nt(right, w[2])

    def whole(ref):
        return read(ref) + (ref[top, bottom],)

    def rough(state):
        old = read(w)
        e = congruence(dot_nn, dot_nt, lambda a: a.astype(bf16), narrow(old), whole(high))
        return state[0] + 1, improve(e, old)

    def fine(state):
        old = read(w)
        nn, nt = (lambda a, b: dot3(dot_nn, a, b)), (lambda a, b: dot3(dot_nt, a, b))
        e = congruence(nn, nt, split, [split(a) for a in old], list(zip(whole(high), whole(low))))
        return state[0] + 1, improve(e, old)

    def until(bound, most):
        return lambda state: (state[0] < most) & jnp.logical_not(state[1] <= bound)

    lax.while_loop(until(0.4, 16), rough, (0, jnp.float32(1e9)))
    _, error = lax.while_loop(until(0.1, 6), fine, (0, jnp.float32(1e9)))
    done = error <= 0.1

    @pl.when(done)
    def _():
        w[...] = w[...] * (by_col * jnp.sqrt(scale))

    @pl.when(jnp.logical_not(done))
    def _():
        w[...] = eye

        def eliminate(k, carry):
            lane = lax.broadcasted_iota(jnp.int32, (1, n), 1)
            below = lax.broadcasted_iota(jnp.int32, (n, 1), 0)
            row = g[pl.ds(k, 1), :]
            pivot = jnp.sum(jnp.where(lane == k, row, 0.0), axis=1, keepdims=True)
            column = jnp.sum(jnp.where(at_col == k, g[...], 0.0), axis=1, keepdims=True)
            ratio = jnp.where(below > k, column / pivot, 0.0)
            solved = w[pl.ds(k, 1), :]
            g[...] = g[...] - ratio * row
            w[...] = w[...] - ratio * solved
            w[pl.ds(k, 1), :] = solved * lax.rsqrt(pivot)
            return carry

        lax.fori_loop(0, n, eliminate, 0)


def lay_out(out, first, second):
    width = first.shape[1]
    out[pl.ds(0, width), pl.ds(0, width)] = first[:width]
    out[pl.ds(width, width), pl.ds(width, width)] = second[:width]
    below = jnp.concatenate([first[width:], second[width:]], axis=0)
    out[pl.ds(width, width), pl.ds(0, width)] = below
    out[pl.ds(0, width), pl.ds(width, width)] = below.T


def factor_kernel(rows_total, first_step, last, core, v, v_other, x, x_other, gram, gram_other, inner, inner_other, *refs):
    out, (g, w, high, low, update, rayleigh) = refs[:-6], refs[-6:]
    width, count = v.shape
    ahead = core[0] == 0

    def ordered(mine, theirs):
        mine, theirs = mine / rows_total, theirs / rows_total
        return jnp.where(ahead, mine, theirs), jnp.where(ahead, theirs, mine)

    first, second = ordered(inner[pl.ds(0, 2 * width), :], inner_other[pl.ds(0, 2 * width), :])
    rayleigh[pl.ds(0, width), pl.ds(0, width)] = first[:width]
    rayleigh[pl.ds(width, width), pl.ds(width, width)] = second[:width]
    across = first[width:] + second[width:].T
    rayleigh[pl.ds(0, width), pl.ds(width, width)] = across
    rayleigh[pl.ds(width, width), pl.ds(0, width)] = across.T
    lay_out(g, *ordered(gram[...], gram_other[...]))
    r = split(rayleigh[...])
    if first_step:
        extra = pl.ds(2 * width, width + width // 2)
        lay_out(w, *ordered(inner[extra, :], inner_other[extra, :]))
        turned = dot3(dot_nn, split(w[...]), r)
        g[...] += STEP_RATE * (turned + turned.T)
        g[...] += dot3(dot_nn, r, split(STEP_RATE**2 * turned - (2 * STEP_RATE**2) * rayleigh[...]))
    else:
        g[...] += 2 * STEP_RATE * rayleigh[...] - STEP_RATE**2 * dot3(dot_nn, r, r)
    inverse_factor(g, w, high, low)
    start = pl.multiple_of(core[0] * width, width)
    there = width - start
    update[pl.ds(start, width), :] = x[...]
    update[pl.ds(there, width), :] = x_other[...]
    mix = split(w[pl.ds(start, width), :])
    mine = split(rayleigh[pl.ds(start, width), :])
    theirs = split(rayleigh[pl.ds(there, width), :])
    for t in range(count // width):
        part = pl.ds(t * width, width)
        old = split(update[:, part])
        here = v[:, part] + STEP_RATE * dot3(dot_nn, mine, old)
        update[pl.ds(there, width), part] = v_other[:, part] + STEP_RATE * dot3(dot_nn, theirs, old)
        update[pl.ds(start, width), part] = here
        solved = dot3(dot_nn, mix, split(update[:, part]))
        if last:
            out[0][part, :] = solved.T
            out[1][part, :] = ((x[:, part] - here) * (1 / STEP_RATE)).T
        else:
            out[0][:, part] = solved
            out[1][t] = solved.astype(bf16)


def swap_cores(a):
    return lax.ppermute(a, "vec", [(0, 1), (1, 0)])


def flip(a, mask):
    return lax.ppermute(a, "patch", [(i, i ^ mask) for i in range(lax.axis_size("patch"))])


def shift(a, pairs):
    devices = range(lax.axis_size("patch"))
    return lax.ppermute(a, "patch", [(i - 2 * pairs, i) for i in devices if i - 2 * pairs in devices])


def stride(a, back=False):
    devices = range(lax.axis_size("patch"))
    route = [(i - (2 if i // 2 % 2 else 6), i) for i in devices]
    return lax.ppermute(a, "patch", [(d, s) if back else (s, d) for s, d in route if s in devices])


def together(*arrays):
    return lax.optimization_barrier(arrays)


def reach(u):
    two, far = shift(u, 2), stride(u)
    return two, flip(two, 1), far, flip(two, 2)


def place_order(parts, place):
    radix = len(parts)
    bit = 1
    while bit < radix:
        swapped = [parts[j ^ bit] for j in range(radix)]
        parts = [jnp.where(place & bit, b, a) for a, b in zip(parts, swapped)]
        bit *= 2
    return parts


def stages_of():
    left, step, stages = lax.axis_size("patch"), 1, []
    while left > 1:
        radix = 4 if left % 4 == 0 else 2
        stages.append((radix, step))
        left, step = left // radix, step * radix
    return stages


def scatter(a, stage):
    radix, step = stage
    place = (lax.axis_index("patch") // step) % radix
    parts = a.reshape(radix, a.shape[0] // radix, a.shape[1])
    a = lax.dynamic_index_in_dim(parts, place, 0, False)
    for m in range(1, radix):
        a = a + flip(lax.dynamic_index_in_dim(parts, place ^ m, 0, False), m * step)
    return a


def finish(a, stages, done):
    for stage in stages[done:-1]:
        a = scatter(a, stage)
    radix, step = stages[-1]
    a = sum([flip(a, m * step) for m in range(1, radix)], a)
    for radix, step in stages[-2::-1]:
        place = (lax.axis_index("patch") // step) % radix
        a = jnp.concatenate(place_order([a] + [flip(a, m * step) for m in range(1, radix)], place), axis=0)
    return a


def shards(vectors, blocks, block_row, block_col, block_count):
    count, width = vectors.shape
    size = blocks.shape[1]
    rows_total = float(count * lax.axis_size("patch"))
    position = lax.axis_index("patch")
    odd = position % 2
    meta = jnp.stack([block_count[0], 2 * (position - odd) - 4 * (REACH - 1), odd, position // 2 % 2]).astype(jnp.int32)
    core = lax.axis_index("vec").astype(jnp.int32).reshape(1)
    stages = stages_of()
    flat, chunk = shape(f32, width, count), shape(bf16, count // size, width, size)
    x, u = call(pack_kernel, [flat, chunk], [vectors])
    for step in range(STEPS):
        last = step == STEPS - 1
        own_x = flip(u, 1)
        x_other = swap_cores(x)
        cross_other = swap_cores(own_x)
        table = (meta, blocks, block_row, block_col)
        segment = (2, width, size)
        sums = tiles_call(
            mirror_kernel, [shape(kind, *segment) for kind in SEGMENT_KINDS], *table, [u, own_x], [], 4, 4 * REACH
        )
        same, cross = sums[::2], sums[1::2]
        two, two_x, far, side = reach(u)
        far, two_x, side, out_side_x, out_far, out_side = together(far, two_x, side, cross[3], cross[2], same[3])
        pieces = [u, own_x, two, two_x, far, flip(far, 1), side, flip(two_x, 2)]
        kept, near, inner = tiles_call(
            direct_kernel,
            [shape(f32, *segment), shape(bf16, *segment), shape(f32, 2 * width, width)],
            *table,
            pieces,
            [x_other, cross_other, same[0], cross[0]],
            4 * REACH,
            4,
        )
        side_x, far_x, side = flip(out_side_x, 2), flip(out_far, 1), flip(out_side, 2)
        two_out = (cross[1] + side_x.astype(f32)).astype(bf16)
        two_x, far = flip(two_out, 1), stride((same[2] + far_x.astype(f32)).astype(bf16), True)
        two = shift((same[1] + (two_x.astype(f32) + side.astype(f32))).astype(bf16), -2)
        inner_out = [inner]
        if step == 0:
            inner_out += call(gram_kernel, [shape(f32, width + width // 2, width)], [core, x, x_other], smem=1)
        inner = scatter(jnp.concatenate(inner_out), stages[0])
        inner, *joined = together(inner, flip(near, 1), far, two)
        (v,) = call(descend_kernel, [flat], [x, kept, *joined])
        v_other = swap_cores(v)
        (gram,) = call(gram_kernel, [shape(f32, width + width // 2, width)], [core, v, v_other], smem=1)
        inner, gram = together(inner, gram)
        inner, gram = finish(inner, stages, 1), finish(gram, stages, 0)
        full = (2 * width, 2 * width)
        wide = shape(f32, count, width)
        out = call(
            lambda *refs: factor_kernel(rows_total, step == 0, last, *refs),
            [wide, wide] if last else [flat, chunk],
            [core, v, v_other, x, x_other, gram, swap_cores(gram), inner, swap_cores(inner)],
            scratch=[VMEM(full, f32), VMEM(full, f32), VMEM(full, bf16), VMEM(full, bf16)]
            + [VMEM((2 * width, count), f32), VMEM(full, f32)],
            smem=1,
            flops=16 << 30,
            vmem=28,
        )
        x, u = out
    return x, u


def solution(mesh):
    in_specs = (P("patch", "vec"), P("patch", None, None), P("patch"), P("patch"), P("patch"))
    out_specs = (P("patch", "vec"), P("patch", "vec"))
    return jax.shard_map(shards, mesh=mesh, in_specs=in_specs, out_specs=out_specs, check_vma=False)
```

```python
import jax
import jax.numpy as jnp
from jax import lax
from jax.experimental import pallas as pl
from jax.experimental.pallas import tpu as pltpu
from jax.sharding import PartitionSpec as P

STEPS = 2
STEP_RATE = 0.25
GROUP = 8
REACH = 4

f32, bf16 = jnp.float32, jnp.bfloat16
SEGMENT_KINDS = (f32, f32, f32, f32, f32, bf16, bf16, bf16)
TILES_VMEM = 48
VMEM, SMEM = pltpu.VMEM, pltpu.SMEM


def dot_nn(a, b):
    return lax.dot_general(a, b, (((1,), (0,)), ((), ())), preferred_element_type=f32)


def dot_nt(a, b):
    return lax.dot_general(a, b, (((1,), (1,)), ((), ())), preferred_element_type=f32)


def split(a):
    high = a.astype(bf16)
    return high, (a - high.astype(f32)).astype(bf16)


def dot3(dot, a, b):
    (ah, al), (bh, bl) = a, b
    return dot(ah, bh) + (dot(ah, bl) + dot(al, bh))


def call(kernel, out, args, scratch=(), smem=0, flops=1 << 28, vmem=16):
    moved = sum(a.size * a.dtype.itemsize for a in args) + sum(o.size * o.dtype.itemsize for o in out)
    return pl.pallas_call(
        kernel,
        out_shape=out,
        in_specs=[pl.BlockSpec(memory_space=SMEM)] * smem + [pl.BlockSpec(memory_space=VMEM)] * (len(args) - smem),
        out_specs=[pl.BlockSpec(memory_space=VMEM)] * len(out),
        scratch_shapes=list(scratch),
        compiler_params=pltpu.CompilerParams(vmem_limit_bytes=vmem << 20),
        cost_estimate=pl.CostEstimate(flops=flops, bytes_accessed=moved, transcendentals=0),
    )(*args)


def shape(dtype, *dims):
    return jax.ShapeDtypeStruct(dims, dtype)


def pack_kernel(vectors, columns, chunk):
    size = chunk.shape[2]
    for t in range(chunk.shape[0]):
        turned = vectors[pl.ds(t * size, size), :].T
        columns[:, pl.ds(t * size, size)] = turned
        chunk[t] = turned.astype(bf16)


def place(tile, meta):
    start, odd, pair_odd = meta[1], meta[2], meta[3]
    w = tile - start
    back = REACH - 1 - w // 4
    role = jnp.where(back % 2 == 1, 2 + ((back // 2) ^ pair_odd ^ 1), back // 2)
    return role * 4 + 2 * (((w % 4) // 2) ^ odd) + w % 2


def gather(pieces, window, sems):
    return [pltpu.make_async_copy(piece, window.at[pl.ds(2 * s, 2)], sems.at[s]) for s, piece in enumerate(pieces)]


def each_tile(meta, rows, cols, blocks, tiles, sems, ready, product, total):
    used = meta[0]
    groups = (used + GROUP - 1) // GROUP

    def fetch(group):
        part = pl.ds(group * GROUP, GROUP)
        return pltpu.make_async_copy(blocks.at[part], tiles.at[part], sems.at[group])

    for group in range(tiles.shape[0] // GROUP):

        @pl.when(group < groups)
        def _():
            fetch(group).start()

    for copy in ready:
        copy.start()
    total[...] = jnp.zeros_like(total)
    for copy in ready:
        copy.wait()

    def multiply(group, carry):
        fetch(group).wait()
        found = []
        for k in range(GROUP):
            slot = group * GROUP + k
            row, col = rows[slot], cols[slot]
            tile = tiles[slot]
            tile = jnp.where(slot < used, tile, jnp.zeros_like(tile))
            found.append(product(tile, place(row, meta), place(col, meta)) + (row == col,))
        for at, part, diagonal in found:
            total[at] += part * jnp.where(diagonal, 0.5, 1.0).astype(f32)
        return carry

    lax.fori_loop(0, groups, multiply, 0)


def mirror_kernel(meta, rows, cols, *refs):
    pieces, blocks, out = refs[:2], refs[2], refs[3:-5]
    window, total, tiles, piece_sems, tile_sems = refs[-5:]

    def product(tile, row, col):
        return col, dot_nn(window[row], tile)

    each_tile(meta, rows, cols, blocks, tiles, tile_sems, gather(pieces, window, piece_sems), product, total)
    for s, segment in enumerate(out):
        segment[...] = total[pl.ds(2 * s, 2)].astype(segment.dtype)


def direct_kernel(meta, rows, cols, *refs):
    pieces, blocks = refs[: 2 * REACH], refs[2 * REACH]
    x_other, cross_other, kept, near, kept_out, near_out, inner = refs[2 * REACH + 1 : -5]
    window, total, tiles, piece_sems, tile_sems = refs[-5:]

    def product(tile, row, col):
        return row, dot_nt(window[col], tile)

    each_tile(meta, rows, cols, blocks, tiles, tile_sems, gather(pieces, window, piece_sems), product, total)
    kept_out[...] = kept[...] + total[pl.ds(0, 2)]
    near_out[...] = (near[...] + total[pl.ds(2, 2)]).astype(bf16)
    size = inner.shape[1]
    own = jnp.zeros((size, size), f32)
    other = jnp.zeros((size, size), f32)
    for s in range(4):
        mine = total[s].astype(bf16)
        there = x_other[:, pl.ds(s * size, size)].astype(bf16) if s < 2 else cross_other[s - 2]
        own += dot_nt(mine, window[s])
        other += dot_nt(mine, there)
    inner[pl.ds(0, size), :] = own + own.T
    inner[pl.ds(size, size), :] = other


def tiles_call(kernel, out, meta, blocks, rows, cols, pieces, more, window, total):
    size, width = blocks.shape[1], pieces[0].shape[1]
    return pl.pallas_call(
        kernel,
        in_specs=[pl.BlockSpec(memory_space=SMEM)] * 3
        + [pl.BlockSpec(memory_space=pl.ANY)] * len(pieces)
        + [pl.BlockSpec(memory_space=pltpu.HBM)]
        + [pl.BlockSpec(memory_space=VMEM)] * len(more),
        out_specs=[pl.BlockSpec(memory_space=VMEM)] * len(out),
        scratch_shapes=[
            VMEM((window, width, size), bf16),
            VMEM((total, width, size), f32),
            VMEM(blocks.shape, bf16),
            pltpu.SemaphoreType.DMA((len(pieces),)),
            pltpu.SemaphoreType.DMA((blocks.shape[0] // GROUP,)),
        ],
        out_shape=out,
        compiler_params=pltpu.CompilerParams(vmem_limit_bytes=TILES_VMEM << 20),
        cost_estimate=pl.CostEstimate(flops=4 << 30, bytes_accessed=12 << 20, transcendentals=0),
    )(meta, rows, cols, *pieces, blocks, *more)


def descend_kernel(x, kept, near, far, two, out):
    size = kept.shape[2]
    for t in range(x.shape[1] // size):
        part = pl.ds(t * size, size)
        applied = kept[t] + near[t].astype(f32) + (far[t].astype(f32) + two[t].astype(f32))
        out[:, part] = x[:, part] - STEP_RATE * applied


def gram_kernel(core, mine, theirs, out):
    width = mine.shape[0]
    half = width // 2
    own, other = split(mine[...]), split(theirs[...])
    out[pl.ds(0, width), :] = dot3(dot_nt, own, own)
    ahead = core[0] == 0
    high = jnp.where(ahead, theirs[pl.ds(0, half), :], mine[pl.ds(half, half), :])
    low = [jnp.where(ahead, a, b) for a, b in zip(own, other)]
    out[pl.ds(width, half), :] = dot3(dot_nt, split(high), low)


def inverse_factor(g, w, high, low):
    n = g.shape[0]
    at_row = lax.broadcasted_iota(jnp.int32, (n, n), 0)
    at_col = lax.broadcasted_iota(jnp.int32, (n, n), 1)
    eye = jnp.where(at_row == at_col, 1.0, 0.0).astype(f32)
    diagonal = eye * g[...]
    by_row = lax.rsqrt(jnp.sum(diagonal, axis=1, keepdims=True))
    by_col = lax.rsqrt(jnp.sum(diagonal, axis=0, keepdims=True))
    unit = g[...] * by_row * by_col
    rounded = unit.astype(bf16)
    square = dot_nn(rounded, rounded).astype(bf16)
    fourth = dot_nn(square, square)
    scale = 1.9 / jnp.sqrt(jnp.sqrt(jnp.sqrt(jnp.sum(fourth * fourth, keepdims=True))))
    scaled = unit * scale
    high[...], low[...] = split(scaled)

    half = n // 2
    top, bottom = pl.ds(0, half), pl.ds(half, half)
    small = eye[:half, :half]
    triangle = (at_row > at_col)[:half, :half]

    def lower(e):
        return jnp.where(triangle, e, 0.5 * small * e)

    def read(ref):
        return ref[top, top], ref[bottom, top], ref[bottom, bottom]

    def product(a, b):
        return dot_nn(a[0], b[0]), dot_nn(a[1], b[0]) + dot_nn(a[2], b[1]), dot_nn(a[2], b[2])

    def narrow(blocks):
        return tuple(block.astype(bf16) for block in blocks)

    p = (lower(scaled[:half, :half] - small), scaled[half:, :half], lower(scaled[half:, half:] - small))
    pb = narrow(p)
    square = product(pb, pb)
    w[top, bottom] = jnp.zeros((half, half), f32)
    w[top, top] = small - p[0] + square[0]
    w[bottom, top] = square[1] - p[1]
    w[bottom, bottom] = small - p[2] + square[2]

    def improve(e, old):
        p = (lower(e[0] - small), e[1], lower(e[2] - small))
        pb = narrow(p)
        first = product(pb, narrow(old))
        second = product(pb, narrow(first))
        w[top, top] = old[0] - first[0] + second[0]
        w[bottom, top] = old[1] - first[1] + second[1]
        w[bottom, bottom] = old[2] - first[2] + second[2]
        return jnp.sqrt(sum(jnp.sum(block * block) for block in p))

    def congruence(nn, nt, cut, w, s):
        s00, s10, s11, s01 = s
        left = nn(w[0], s00)
        below, right = nn(w[1], s00) + nn(w[2], s10), nn(w[1], s01) + nn(w[2], s11)
        left, below, right = cut(left), cut(below), cut(right)
        return nt(left, w[0]), nt(below, w[0]), nt(below, w[1]) + nt(right, w[2])

    def whole(ref):
        return read(ref) + (ref[top, bottom],)

    def rough(state):
        old = read(w)
        e = congruence(dot_nn, dot_nt, lambda a: a.astype(bf16), narrow(old), whole(high))
        return state[0] + 1, improve(e, old)

    def fine(state):
        old = read(w)
        nn, nt = (lambda a, b: dot3(dot_nn, a, b)), (lambda a, b: dot3(dot_nt, a, b))
        e = congruence(nn, nt, split, [split(a) for a in old], list(zip(whole(high), whole(low))))
        return state[0] + 1, improve(e, old)

    def until(bound, most):
        return lambda state: (state[0] < most) & jnp.logical_not(state[1] <= bound)

    lax.while_loop(until(0.4, 16), rough, (0, jnp.float32(1e9)))
    _, error = lax.while_loop(until(0.1, 6), fine, (0, jnp.float32(1e9)))
    done = error <= 0.1

    @pl.when(done)
    def _():
        w[...] = w[...] * (by_col * jnp.sqrt(scale))

    @pl.when(jnp.logical_not(done))
    def _():
        w[...] = eye

        def eliminate(k, carry):
            lane = lax.broadcasted_iota(jnp.int32, (1, n), 1)
            below = lax.broadcasted_iota(jnp.int32, (n, 1), 0)
            row = g[pl.ds(k, 1), :]
            pivot = jnp.sum(jnp.where(lane == k, row, 0.0), axis=1, keepdims=True)
            column = jnp.sum(jnp.where(at_col == k, g[...], 0.0), axis=1, keepdims=True)
            ratio = jnp.where(below > k, column / pivot, 0.0)
            solved = w[pl.ds(k, 1), :]
            g[...] = g[...] - ratio * row
            w[...] = w[...] - ratio * solved
            w[pl.ds(k, 1), :] = solved * lax.rsqrt(pivot)
            return carry

        lax.fori_loop(0, n, eliminate, 0)


def lay_out(out, first, second):
    width = first.shape[1]
    out[pl.ds(0, width), pl.ds(0, width)] = first[:width]
    out[pl.ds(width, width), pl.ds(width, width)] = second[:width]
    below = jnp.concatenate([first[width:], second[width:]], axis=0)
    out[pl.ds(width, width), pl.ds(0, width)] = below
    out[pl.ds(0, width), pl.ds(width, width)] = below.T


def factor_kernel(rows_total, first_step, last, core, v, v_other, x, x_other, gram, gram_other, inner, inner_other, *refs):
    out, (g, w, high, low, update, rayleigh) = refs[:-6], refs[-6:]
    width, count = v.shape
    ahead = core[0] == 0

    def ordered(mine, theirs):
        mine, theirs = mine / rows_total, theirs / rows_total
        return jnp.where(ahead, mine, theirs), jnp.where(ahead, theirs, mine)

    first, second = ordered(inner[pl.ds(0, 2 * width), :], inner_other[pl.ds(0, 2 * width), :])
    rayleigh[pl.ds(0, width), pl.ds(0, width)] = first[:width]
    rayleigh[pl.ds(width, width), pl.ds(width, width)] = second[:width]
    across = first[width:] + second[width:].T
    rayleigh[pl.ds(0, width), pl.ds(width, width)] = across
    rayleigh[pl.ds(width, width), pl.ds(0, width)] = across.T
    lay_out(g, *ordered(gram[...], gram_other[...]))
    r = split(rayleigh[...])
    if first_step:
        extra = pl.ds(2 * width, width + width // 2)
        lay_out(w, *ordered(inner[extra, :], inner_other[extra, :]))
        turned = dot3(dot_nn, split(w[...]), r)
        g[...] += STEP_RATE * (turned + turned.T)
        g[...] += dot3(dot_nn, r, split(STEP_RATE**2 * turned - (2 * STEP_RATE**2) * rayleigh[...]))
    else:
        g[...] += 2 * STEP_RATE * rayleigh[...] - STEP_RATE**2 * dot3(dot_nn, r, r)
    inverse_factor(g, w, high, low)
    start = pl.multiple_of(core[0] * width, width)
    there = width - start
    update[pl.ds(start, width), :] = x[...]
    update[pl.ds(there, width), :] = x_other[...]
    mix = split(w[pl.ds(start, width), :])
    mine = split(rayleigh[pl.ds(start, width), :])
    theirs = split(rayleigh[pl.ds(there, width), :])
    for t in range(count // width):
        part = pl.ds(t * width, width)
        old = split(update[:, part])
        here = v[:, part] + STEP_RATE * dot3(dot_nn, mine, old)
        update[pl.ds(there, width), part] = v_other[:, part] + STEP_RATE * dot3(dot_nn, theirs, old)
        update[pl.ds(start, width), part] = here
        solved = dot3(dot_nn, mix, split(update[:, part]))
        if last:
            out[0][part, :] = solved.T
            out[1][part, :] = ((x[:, part] - here) * (1 / STEP_RATE)).T
        else:
            out[0][:, part] = solved
            out[1][t] = solved.astype(bf16)


def swap_cores(a):
    return lax.ppermute(a, "vec", [(0, 1), (1, 0)])


def flip(a, mask):
    return lax.ppermute(a, "patch", [(i, i ^ mask) for i in range(lax.axis_size("patch"))])


def shift(a, pairs):
    devices = range(lax.axis_size("patch"))
    return lax.ppermute(a, "patch", [(i - 2 * pairs, i) for i in devices if i - 2 * pairs in devices])


def stride(a, back=False):
    devices = range(lax.axis_size("patch"))
    route = [(i - (2 if i // 2 % 2 else 6), i) for i in devices]
    return lax.ppermute(a, "patch", [(d, s) if back else (s, d) for s, d in route if s in devices])


def together(*arrays):
    return lax.optimization_barrier(arrays)


def reach(u, own_x):
    two, far = shift(u, 2), stride(together(u, own_x)[0])
    return two, flip(two, 1), far, flip(two, 2)


def place_order(parts, place):
    radix = len(parts)
    bit = 1
    while bit < radix:
        swapped = [parts[j ^ bit] for j in range(radix)]
        parts = [jnp.where(place & bit, b, a) for a, b in zip(parts, swapped)]
        bit *= 2
    return parts


def stages_of():
    left, step, stages = lax.axis_size("patch"), 1, []
    while left > 1:
        radix = 4 if left % 4 == 0 else 2
        stages.append((radix, step))
        left, step = left // radix, step * radix
    return stages


def scatter(a, stage):
    radix, step = stage
    place = (lax.axis_index("patch") // step) % radix
    parts = a.reshape(radix, a.shape[0] // radix, a.shape[1])
    a = lax.dynamic_index_in_dim(parts, place, 0, False)
    for m in range(1, radix):
        a = a + flip(lax.dynamic_index_in_dim(parts, place ^ m, 0, False), m * step)
    return a


def exchange(a, stage):
    radix, step = stage
    return sum([flip(a, m * step) for m in range(1, radix)], a)


def collect(a, stage):
    radix, step = stage
    place = (lax.axis_index("patch") // step) % radix
    return jnp.concatenate(place_order([a] + [flip(a, m * step) for m in range(1, radix)], place), axis=0)


def sum_both(a, b, stages):
    steps_a = [(scatter, stage) for stage in stages[1:]] + [(collect, stage) for stage in stages[::-1]]
    steps_b = [(scatter, stage) for stage in stages[:-1]] + [(exchange, stages[-1])]
    steps_b += [(collect, stage) for stage in stages[-2::-1]]
    for (go_a, stage_a), (go_b, stage_b) in zip(steps_a, steps_b, strict=True):
        a, b = together(go_a(a, stage_a), go_b(b, stage_b))
    return a, b


def shards(vectors, blocks, block_row, block_col, block_count):
    count, width = vectors.shape
    size = blocks.shape[1]
    rows_total = float(count * lax.axis_size("patch"))
    position = lax.axis_index("patch")
    odd = position % 2
    meta = jnp.stack([block_count[0], 2 * (position - odd) - 4 * (REACH - 1), odd, position // 2 % 2]).astype(jnp.int32)
    core = lax.axis_index("vec").astype(jnp.int32).reshape(1)
    stages = stages_of()
    flat, chunk = shape(f32, width, count), shape(bf16, count // size, width, size)
    x, u = call(pack_kernel, [flat, chunk], [vectors])
    for step in range(STEPS):
        last = step == STEPS - 1
        own_x = flip(u, 1)
        x_other = swap_cores(x)
        cross_other = swap_cores(own_x)
        table = (meta, blocks, block_row, block_col)
        segment = (2, width, size)
        sums = tiles_call(
            mirror_kernel, [shape(kind, *segment) for kind in SEGMENT_KINDS], *table, [u, own_x], [], 4, 4 * REACH
        )
        same, cross = sums[::2], sums[1::2]
        two, two_x, far, side = reach(u, own_x)
        out_side_x, out_far, out_side = together(cross[3], cross[2], same[3], far, two_x, side)[:3]
        pieces = [u, own_x, two, two_x, far, flip(far, 1), side, flip(two_x, 2)]
        kept, near, inner = tiles_call(
            direct_kernel,
            [shape(f32, *segment), shape(bf16, *segment), shape(f32, 2 * width, width)],
            *table,
            pieces,
            [x_other, cross_other, same[0], cross[0]],
            4 * REACH,
            4,
        )
        side_x, far_x, side = flip(out_side_x, 2), flip(out_far, 1), flip(out_side, 2)
        two_out = (cross[1] + side_x.astype(f32)).astype(bf16)
        two_x, far = flip(two_out, 1), stride((same[2] + far_x.astype(f32)).astype(bf16), True)
        two = shift((same[1] + (two_x.astype(f32) + side.astype(f32))).astype(bf16), -2)
        inner_out = [inner]
        if step == 0:
            inner_out += call(gram_kernel, [shape(f32, width + width // 2, width)], [core, x, x_other], smem=1)
        inner = scatter(jnp.concatenate(inner_out), stages[0])
        inner, *joined = together(inner, flip(near, 1), far, two)
        (v,) = call(descend_kernel, [flat], [x, kept, *joined])
        v_other = swap_cores(v)
        (gram,) = call(gram_kernel, [shape(f32, width + width // 2, width)], [core, v, v_other], smem=1)
        inner, gram = together(inner, gram)
        inner, gram = sum_both(inner, gram, stages)
        full = (2 * width, 2 * width)
        wide = shape(f32, count, width)
        out = call(
            lambda *refs: factor_kernel(rows_total, step == 0, last, *refs),
            [wide, wide] if last else [flat, chunk],
            [core, v, v_other, x, x_other, gram, swap_cores(gram), inner, swap_cores(inner)],
            scratch=[VMEM(full, f32), VMEM(full, f32), VMEM(full, bf16), VMEM(full, bf16)]
            + [VMEM((2 * width, count), f32), VMEM(full, f32)],
            smem=1,
            flops=16 << 30,
            vmem=28,
        )
        x, u = out
    return x, u


def solution(mesh):
    in_specs = (P("patch", "vec"), P("patch", None, None), P("patch"), P("patch"), P("patch"))
    out_specs = (P("patch", "vec"), P("patch", "vec"))
    return jax.shard_map(shards, mesh=mesh, in_specs=in_specs, out_specs=out_specs, check_vma=False)
```

```python
import jax
import jax.numpy as jnp
from jax import lax
from jax.experimental import pallas as pl
from jax.experimental.pallas import tpu as pltpu
from jax.sharding import PartitionSpec as P

STEPS = 2
STEP_RATE = 0.25
GROUP = 8
REACH = 4

f32, bf16 = jnp.float32, jnp.bfloat16
SEGMENT_KINDS = (f32, f32, f32, f32, f32, bf16, bf16, bf16)
TILES_VMEM = 48
VMEM, SMEM = pltpu.VMEM, pltpu.SMEM


def dot_nn(a, b):
    return lax.dot_general(a, b, (((1,), (0,)), ((), ())), preferred_element_type=f32)


def dot_nt(a, b):
    return lax.dot_general(a, b, (((1,), (1,)), ((), ())), preferred_element_type=f32)


def split(a):
    high = a.astype(bf16)
    return high, (a - high.astype(f32)).astype(bf16)


def dot3(dot, a, b):
    (ah, al), (bh, bl) = a, b
    return dot(ah, bh) + (dot(ah, bl) + dot(al, bh))


def call(kernel, out, args, scratch=(), smem=0, flops=1 << 28, vmem=16):
    moved = sum(a.size * a.dtype.itemsize for a in args) + sum(o.size * o.dtype.itemsize for o in out)
    return pl.pallas_call(
        kernel,
        out_shape=out,
        in_specs=[pl.BlockSpec(memory_space=SMEM)] * smem + [pl.BlockSpec(memory_space=VMEM)] * (len(args) - smem),
        out_specs=[pl.BlockSpec(memory_space=VMEM)] * len(out),
        scratch_shapes=list(scratch),
        compiler_params=pltpu.CompilerParams(vmem_limit_bytes=vmem << 20),
        cost_estimate=pl.CostEstimate(flops=flops, bytes_accessed=moved, transcendentals=0),
    )(*args)


def shape(dtype, *dims):
    return jax.ShapeDtypeStruct(dims, dtype)


def pack_kernel(vectors, columns, chunk):
    size = chunk.shape[2]
    for t in range(chunk.shape[0]):
        turned = vectors[pl.ds(t * size, size), :].T
        columns[:, pl.ds(t * size, size)] = turned
        chunk[t] = turned.astype(bf16)


def place(tile, meta):
    start, odd, pair_odd = meta[1], meta[2], meta[3]
    w = tile - start
    back = REACH - 1 - w // 4
    role = jnp.where(back % 2 == 1, 2 + ((back // 2) ^ pair_odd ^ 1), back // 2)
    return role * 4 + 2 * (((w % 4) // 2) ^ odd) + w % 2


def gather(pieces, window, sems):
    return [pltpu.make_async_copy(piece, window.at[pl.ds(2 * s, 2)], sems.at[s]) for s, piece in enumerate(pieces)]


def each_tile(meta, rows, cols, blocks, tiles, sems, ready, product, total):
    used = meta[0]
    groups = (used + GROUP - 1) // GROUP

    def fetch(group):
        part = pl.ds(group * GROUP, GROUP)
        return pltpu.make_async_copy(blocks.at[part], tiles.at[part], sems.at[group])

    for group in range(tiles.shape[0] // GROUP):

        @pl.when(group < groups)
        def _():
            fetch(group).start()

    for copy in ready:
        copy.start()
    total[...] = jnp.zeros_like(total)
    for copy in ready:
        copy.wait()

    def multiply(group, carry):
        fetch(group).wait()
        found = []
        for k in range(GROUP):
            slot = group * GROUP + k
            row, col = rows[slot], cols[slot]
            tile = tiles[slot]
            tile = jnp.where(slot < used, tile, jnp.zeros_like(tile))
            found.append(product(tile, place(row, meta), place(col, meta)) + (row == col,))
        for at, part, diagonal in found:
            total[at] += part * jnp.where(diagonal, 0.5, 1.0).astype(f32)
        return carry

    lax.fori_loop(0, groups, multiply, 0)


def mirror_kernel(meta, rows, cols, *refs):
    pieces, blocks, out = refs[:2], refs[2], refs[3:-5]
    window, total, tiles, piece_sems, tile_sems = refs[-5:]

    def product(tile, row, col):
        return col, dot_nn(window[row], tile)

    each_tile(meta, rows, cols, blocks, tiles, tile_sems, gather(pieces, window, piece_sems), product, total)
    for s, segment in enumerate(out):
        segment[...] = total[pl.ds(2 * s, 2)].astype(segment.dtype)


def direct_kernel(meta, rows, cols, *refs):
    pieces, blocks = refs[: 2 * REACH], refs[2 * REACH]
    x_other, cross_other, kept, near, kept_out, near_out, inner = refs[2 * REACH + 1 : -5]
    window, total, tiles, piece_sems, tile_sems = refs[-5:]

    def product(tile, row, col):
        return row, dot_nt(window[col], tile)

    each_tile(meta, rows, cols, blocks, tiles, tile_sems, gather(pieces, window, piece_sems), product, total)
    kept_out[...] = kept[...] + total[pl.ds(0, 2)]
    near_out[...] = (near[...] + total[pl.ds(2, 2)]).astype(bf16)
    size = inner.shape[1]
    own = jnp.zeros((size, size), f32)
    other = jnp.zeros((size, size), f32)
    for s in range(4):
        mine = total[s].astype(bf16)
        there = x_other[:, pl.ds(s * size, size)].astype(bf16) if s < 2 else cross_other[s - 2]
        own += dot_nt(mine, window[s])
        other += dot_nt(mine, there)
    inner[pl.ds(0, size), :] = own + own.T
    inner[pl.ds(size, size), :] = other


def tiles_call(kernel, out, meta, blocks, rows, cols, pieces, more, window, total):
    size, width = blocks.shape[1], pieces[0].shape[1]
    return pl.pallas_call(
        kernel,
        in_specs=[pl.BlockSpec(memory_space=SMEM)] * 3
        + [pl.BlockSpec(memory_space=pl.ANY)] * len(pieces)
        + [pl.BlockSpec(memory_space=pltpu.HBM)]
        + [pl.BlockSpec(memory_space=VMEM)] * len(more),
        out_specs=[pl.BlockSpec(memory_space=VMEM)] * len(out),
        scratch_shapes=[
            VMEM((window, width, size), bf16),
            VMEM((total, width, size), f32),
            VMEM(blocks.shape, bf16),
            pltpu.SemaphoreType.DMA((len(pieces),)),
            pltpu.SemaphoreType.DMA((blocks.shape[0] // GROUP,)),
        ],
        out_shape=out,
        compiler_params=pltpu.CompilerParams(vmem_limit_bytes=TILES_VMEM << 20),
        cost_estimate=pl.CostEstimate(flops=4 << 30, bytes_accessed=12 << 20, transcendentals=0),
    )(meta, rows, cols, *pieces, blocks, *more)


def descend_kernel(x, kept, near, far, two, out):
    size = kept.shape[2]
    for t in range(x.shape[1] // size):
        part = pl.ds(t * size, size)
        applied = kept[t] + near[t].astype(f32) + (far[t].astype(f32) + two[t].astype(f32))
        out[:, part] = x[:, part] - STEP_RATE * applied


def gram_kernel(core, mine, theirs, out):
    width = mine.shape[0]
    half = width // 2
    own, other = split(mine[...]), split(theirs[...])
    out[pl.ds(0, width), :] = dot3(dot_nt, own, own)
    ahead = core[0] == 0
    high = jnp.where(ahead, theirs[pl.ds(0, half), :], mine[pl.ds(half, half), :])
    low = [jnp.where(ahead, a, b) for a, b in zip(own, other)]
    out[pl.ds(width, half), :] = dot3(dot_nt, split(high), low)


def inverse_factor(g, w, high, low):
    n = g.shape[0]
    at_row = lax.broadcasted_iota(jnp.int32, (n, n), 0)
    at_col = lax.broadcasted_iota(jnp.int32, (n, n), 1)
    eye = jnp.where(at_row == at_col, 1.0, 0.0).astype(f32)
    diagonal = eye * g[...]
    by_row = lax.rsqrt(jnp.sum(diagonal, axis=1, keepdims=True))
    by_col = lax.rsqrt(jnp.sum(diagonal, axis=0, keepdims=True))
    unit = g[...] * by_row * by_col
    rounded = unit.astype(bf16)
    square = dot_nn(rounded, rounded).astype(bf16)
    fourth = dot_nn(square, square)
    scale = 1.9 / jnp.sqrt(jnp.sqrt(jnp.sqrt(jnp.sum(fourth * fourth, keepdims=True))))
    scaled = unit * scale
    high[...], low[...] = split(scaled)

    half = n // 2
    top, bottom = pl.ds(0, half), pl.ds(half, half)
    small = eye[:half, :half]
    triangle = (at_row > at_col)[:half, :half]

    def lower(e):
        return jnp.where(triangle, e, 0.5 * small * e)

    def read(ref):
        return ref[top, top], ref[bottom, top], ref[bottom, bottom]

    def product(a, b):
        return dot_nn(a[0], b[0]), dot_nn(a[1], b[0]) + dot_nn(a[2], b[1]), dot_nn(a[2], b[2])

    def narrow(blocks):
        return tuple(block.astype(bf16) for block in blocks)

    p = (lower(scaled[:half, :half] - small), scaled[half:, :half], lower(scaled[half:, half:] - small))
    pb = narrow(p)
    square = product(pb, pb)
    w[top, bottom] = jnp.zeros((half, half), f32)
    w[top, top] = small - p[0] + square[0]
    w[bottom, top] = square[1] - p[1]
    w[bottom, bottom] = small - p[2] + square[2]

    def improve(e, old):
        p = (lower(e[0] - small), e[1], lower(e[2] - small))
        pb = narrow(p)
        first = product(pb, narrow(old))
        second = product(pb, narrow(first))
        w[top, top] = old[0] - first[0] + second[0]
        w[bottom, top] = old[1] - first[1] + second[1]
        w[bottom, bottom] = old[2] - first[2] + second[2]
        return jnp.sqrt(sum(jnp.sum(block * block) for block in p))

    def congruence(nn, nt, cut, w, s):
        s00, s10, s11, s01 = s
        left = nn(w[0], s00)
        below, right = nn(w[1], s00) + nn(w[2], s10), nn(w[1], s01) + nn(w[2], s11)
        left, below, right = cut(left), cut(below), cut(right)
        return nt(left, w[0]), nt(below, w[0]), nt(below, w[1]) + nt(right, w[2])

    def whole(ref):
        return read(ref) + (ref[top, bottom],)

    def rough(state):
        old = read(w)
        e = congruence(dot_nn, dot_nt, lambda a: a.astype(bf16), narrow(old), whole(high))
        return state[0] + 1, improve(e, old)

    def fine(state):
        old = read(w)
        nn, nt = (lambda a, b: dot3(dot_nn, a, b)), (lambda a, b: dot3(dot_nt, a, b))
        e = congruence(nn, nt, split, [split(a) for a in old], list(zip(whole(high), whole(low))))
        return state[0] + 1, improve(e, old)

    def until(bound, most):
        return lambda state: (state[0] < most) & jnp.logical_not(state[1] <= bound)

    lax.while_loop(until(0.4, 16), rough, (0, jnp.float32(1e9)))
    _, error = lax.while_loop(until(0.1, 6), fine, (0, jnp.float32(1e9)))
    done = error <= 0.1

    @pl.when(done)
    def _():
        w[...] = w[...] * (by_col * jnp.sqrt(scale))

    @pl.when(jnp.logical_not(done))
    def _():
        w[...] = eye

        def eliminate(k, carry):
            lane = lax.broadcasted_iota(jnp.int32, (1, n), 1)
            below = lax.broadcasted_iota(jnp.int32, (n, 1), 0)
            row = g[pl.ds(k, 1), :]
            pivot = jnp.sum(jnp.where(lane == k, row, 0.0), axis=1, keepdims=True)
            column = jnp.sum(jnp.where(at_col == k, g[...], 0.0), axis=1, keepdims=True)
            ratio = jnp.where(below > k, column / pivot, 0.0)
            solved = w[pl.ds(k, 1), :]
            g[...] = g[...] - ratio * row
            w[...] = w[...] - ratio * solved
            w[pl.ds(k, 1), :] = solved * lax.rsqrt(pivot)
            return carry

        lax.fori_loop(0, n, eliminate, 0)


def lay_out(out, first, second):
    width = first.shape[1]
    out[pl.ds(0, width), pl.ds(0, width)] = first[:width]
    out[pl.ds(width, width), pl.ds(width, width)] = second[:width]
    below = jnp.concatenate([first[width:], second[width:]], axis=0)
    out[pl.ds(width, width), pl.ds(0, width)] = below
    out[pl.ds(0, width), pl.ds(width, width)] = below.T


def factor_kernel(rows_total, first_step, last, core, v, v_other, x, x_other, sums, sums_other, *refs):
    out, (g, w, high, low, update, rayleigh) = refs[:-6], refs[-6:]
    width, count = v.shape
    ahead = core[0] == 0

    def ordered(mine, theirs):
        mine, theirs = mine / rows_total, theirs / rows_total
        return jnp.where(ahead, mine, theirs), jnp.where(ahead, theirs, mine)

    blocks, rows, _ = sums.shape
    cut = rows - (width + width // 2) // blocks

    def joined(ref, low, high):
        return jnp.concatenate([ref[block, pl.ds(low, high - low), :] for block in range(blocks)], axis=0)

    inner, inner_other = joined(sums, 0, cut), joined(sums_other, 0, cut)
    first, second = ordered(inner[: 2 * width], inner_other[: 2 * width])
    rayleigh[pl.ds(0, width), pl.ds(0, width)] = first[:width]
    rayleigh[pl.ds(width, width), pl.ds(width, width)] = second[:width]
    across = first[width:] + second[width:].T
    rayleigh[pl.ds(0, width), pl.ds(width, width)] = across
    rayleigh[pl.ds(width, width), pl.ds(0, width)] = across.T
    lay_out(g, *ordered(joined(sums, cut, rows), joined(sums_other, cut, rows)))
    r = split(rayleigh[...])
    if first_step:
        lay_out(w, *ordered(inner[2 * width :], inner_other[2 * width :]))
        turned = dot3(dot_nn, split(w[...]), r)
        g[...] += STEP_RATE * (turned + turned.T)
        g[...] += dot3(dot_nn, r, split(STEP_RATE**2 * turned - (2 * STEP_RATE**2) * rayleigh[...]))
    else:
        g[...] += 2 * STEP_RATE * rayleigh[...] - STEP_RATE**2 * dot3(dot_nn, r, r)
    inverse_factor(g, w, high, low)
    start = pl.multiple_of(core[0] * width, width)
    there = width - start
    update[pl.ds(start, width), :] = x[...]
    update[pl.ds(there, width), :] = x_other[...]
    mix = split(w[pl.ds(start, width), :])
    mine = split(rayleigh[pl.ds(start, width), :])
    theirs = split(rayleigh[pl.ds(there, width), :])
    for t in range(count // width):
        part = pl.ds(t * width, width)
        old = split(update[:, part])
        here = v[:, part] + STEP_RATE * dot3(dot_nn, mine, old)
        update[pl.ds(there, width), part] = v_other[:, part] + STEP_RATE * dot3(dot_nn, theirs, old)
        update[pl.ds(start, width), part] = here
        solved = dot3(dot_nn, mix, split(update[:, part]))
        if last:
            out[0][part, :] = solved.T
            out[1][part, :] = ((x[:, part] - here) * (1 / STEP_RATE)).T
        else:
            out[0][:, part] = solved
            out[1][t] = solved.astype(bf16)


def swap_cores(a):
    return lax.ppermute(a, "vec", [(0, 1), (1, 0)])


def flip(a, mask):
    return lax.ppermute(a, "patch", [(i, i ^ mask) for i in range(lax.axis_size("patch"))])


def shift(a, pairs):
    devices = range(lax.axis_size("patch"))
    return lax.ppermute(a, "patch", [(i - 2 * pairs, i) for i in devices if i - 2 * pairs in devices])


def stride(a, back=False):
    devices = range(lax.axis_size("patch"))
    route = [(i - (2 if i // 2 % 2 else 6), i) for i in devices]
    return lax.ppermute(a, "patch", [(d, s) if back else (s, d) for s, d in route if s in devices])


def together(*arrays):
    return lax.optimization_barrier(arrays)


def reach(u, own_x):
    two, far = shift(u, 2), stride(together(u, own_x)[0])
    return two, flip(two, 1), far, flip(two, 2)


def place_order(parts, place):
    radix = len(parts)
    bit = 1
    while bit < radix:
        swapped = [parts[j ^ bit] for j in range(radix)]
        parts = [jnp.where(place & bit, b, a) for a, b in zip(parts, swapped)]
        bit *= 2
    return parts


def stages_of():
    left, step, stages = lax.axis_size("patch"), 1, []
    while left > 1:
        radix = 4 if left % 4 == 0 else 2
        stages.append((radix, step))
        left, step = left // radix, step * radix
    return stages


def scatter(a, stage):
    radix, step = stage
    place = (lax.axis_index("patch") // step) % radix
    parts = a.reshape(radix, a.shape[0] // radix, a.shape[1])
    a = lax.dynamic_index_in_dim(parts, place, 0, False)
    for m in range(1, radix):
        a = a + flip(lax.dynamic_index_in_dim(parts, place ^ m, 0, False), m * step)
    return a


def shared(a, stage):
    radix, step = stage
    return [a] + [flip(a, m * step) for m in range(1, radix)]


def in_order(parts, stage):
    radix, step = stage
    return jnp.concatenate(place_order(parts, (lax.axis_index("patch") // step) % radix), axis=0)


def sum_both(a, b, stages):
    for stage_a, stage_b in zip(stages[1:], stages[:-1], strict=True):
        a, b = together(scatter(a, stage_a), scatter(b, stage_b))
    cut = a.shape[0]
    parts = shared(jnp.concatenate([a, b]), stages[-1])
    joined = jnp.concatenate([in_order([part[:cut] for part in parts], stages[-1]), sum(part[cut:] for part in parts)])
    blocks = 1
    for stage in stages[-2::-1]:
        joined = in_order(shared(joined, stage), stage)
        blocks *= stage[0]
    return joined.reshape(blocks, joined.shape[0] // blocks, joined.shape[1])


def shards(vectors, blocks, block_row, block_col, block_count):
    count, width = vectors.shape
    size = blocks.shape[1]
    rows_total = float(count * lax.axis_size("patch"))
    position = lax.axis_index("patch")
    odd = position % 2
    meta = jnp.stack([block_count[0], 2 * (position - odd) - 4 * (REACH - 1), odd, position // 2 % 2]).astype(jnp.int32)
    core = lax.axis_index("vec").astype(jnp.int32).reshape(1)
    stages = stages_of()
    flat, chunk = shape(f32, width, count), shape(bf16, count // size, width, size)
    x, u = call(pack_kernel, [flat, chunk], [vectors])
    for step in range(STEPS):
        last = step == STEPS - 1
        own_x = flip(u, 1)
        x_other = swap_cores(x)
        cross_other = swap_cores(own_x)
        table = (meta, blocks, block_row, block_col)
        segment = (2, width, size)
        sums = tiles_call(
            mirror_kernel, [shape(kind, *segment) for kind in SEGMENT_KINDS], *table, [u, own_x], [], 4, 4 * REACH
        )
        same, cross = sums[::2], sums[1::2]
        two, two_x, far, side = reach(u, own_x)
        pieces = [u, own_x, two, two_x, far, flip(far, 1), side, flip(two_x, 2)]
        out_side_x, out_side = together(cross[3], same[3], pieces[7])[:2]
        out_far = together(cross[2], side, two_x)[0]
        kept, near, inner = tiles_call(
            direct_kernel,
            [shape(f32, *segment), shape(bf16, *segment), shape(f32, 2 * width, width)],
            *table,
            pieces,
            [x_other, cross_other, same[0], cross[0]],
            4 * REACH,
            4,
        )
        side_x, far_x, side = flip(out_side_x, 2), flip(out_far, 1), flip(out_side, 2)
        two_out = (cross[1] + side_x.astype(f32)).astype(bf16)
        two_x, far = flip(two_out, 1), stride((same[2] + far_x.astype(f32)).astype(bf16), True)
        two = shift((same[1] + (two_x.astype(f32) + side.astype(f32))).astype(bf16), -2)
        inner_out = [inner]
        if step == 0:
            inner_out += call(gram_kernel, [shape(f32, width + width // 2, width)], [core, x, x_other], smem=1)
        inner = scatter(jnp.concatenate(inner_out), stages[0])
        inner, *joined = together(inner, flip(near, 1), far, two)
        (v,) = call(descend_kernel, [flat], [x, kept, *joined])
        v_other = swap_cores(v)
        (gram,) = call(gram_kernel, [shape(f32, width + width // 2, width)], [core, v, v_other], smem=1)
        inner, gram = together(inner, gram)
        sums = sum_both(inner, gram, stages)
        full = (2 * width, 2 * width)
        wide = shape(f32, count, width)
        out = call(
            lambda *refs: factor_kernel(rows_total, step == 0, last, *refs),
            [wide, wide] if last else [flat, chunk],
            [core, v, v_other, x, x_other, sums, swap_cores(sums)],
            scratch=[VMEM(full, f32), VMEM(full, f32), VMEM(full, bf16), VMEM(full, bf16)]
            + [VMEM((2 * width, count), f32), VMEM(full, f32)],
            smem=1,
            flops=16 << 30,
            vmem=28,
        )
        x, u = out
    return x, u


def solution(mesh):
    in_specs = (P("patch", "vec"), P("patch", None, None), P("patch"), P("patch"), P("patch"))
    out_specs = (P("patch", "vec"), P("patch", "vec"))
    return jax.shard_map(shards, mesh=mesh, in_specs=in_specs, out_specs=out_specs, check_vma=False)
```

```python
import jax
import jax.numpy as jnp
from jax import lax
from jax.experimental import pallas as pl
from jax.experimental.pallas import tpu as pltpu
from jax.sharding import PartitionSpec as P

STEPS = 2
STEP_RATE = 0.25
GROUP = 8
REACH = 4

f32, bf16 = jnp.float32, jnp.bfloat16
SEGMENT_KINDS = (f32, f32, f32, f32, f32, bf16, bf16, bf16)
TILES_VMEM = 48
VMEM, SMEM = pltpu.VMEM, pltpu.SMEM


def dot_nn(a, b):
    return lax.dot_general(a, b, (((1,), (0,)), ((), ())), preferred_element_type=f32)


def dot_nt(a, b):
    return lax.dot_general(a, b, (((1,), (1,)), ((), ())), preferred_element_type=f32)


def split(a):
    high = a.astype(bf16)
    return high, (a - high.astype(f32)).astype(bf16)


def dot3(dot, a, b):
    (ah, al), (bh, bl) = a, b
    return dot(ah, bh) + (dot(ah, bl) + dot(al, bh))


def call(kernel, out, args, scratch=(), smem=0, flops=1 << 28, vmem=16):
    moved = sum(a.size * a.dtype.itemsize for a in args) + sum(o.size * o.dtype.itemsize for o in out)
    return pl.pallas_call(
        kernel,
        out_shape=out,
        in_specs=[pl.BlockSpec(memory_space=SMEM)] * smem + [pl.BlockSpec(memory_space=VMEM)] * (len(args) - smem),
        out_specs=[pl.BlockSpec(memory_space=VMEM)] * len(out),
        scratch_shapes=list(scratch),
        compiler_params=pltpu.CompilerParams(vmem_limit_bytes=vmem << 20),
        cost_estimate=pl.CostEstimate(flops=flops, bytes_accessed=moved, transcendentals=0),
    )(*args)


def shape(dtype, *dims):
    return jax.ShapeDtypeStruct(dims, dtype)


def pack_kernel(vectors, columns, chunk):
    size = chunk.shape[2]
    for t in range(chunk.shape[0]):
        turned = vectors[pl.ds(t * size, size), :].T
        columns[:, pl.ds(t * size, size)] = turned
        chunk[t] = turned.astype(bf16)


def place(tile, meta):
    start, odd, pair_odd = meta[1], meta[2], meta[3]
    w = tile - start
    back = REACH - 1 - w // 4
    role = jnp.where(back % 2 == 1, 2 + ((back // 2) ^ pair_odd ^ 1), back // 2)
    return role * 4 + 2 * (((w % 4) // 2) ^ odd) + w % 2


def gather(pieces, window, sems):
    return [pltpu.make_async_copy(piece, window.at[pl.ds(2 * s, 2)], sems.at[s]) for s, piece in enumerate(pieces)]


def each_tile(meta, rows, cols, blocks, tiles, sems, ready, product, total):
    used = meta[0]
    groups = (used + GROUP - 1) // GROUP

    def fetch(group):
        part = pl.ds(group * GROUP, GROUP)
        return pltpu.make_async_copy(blocks.at[part], tiles.at[part], sems.at[group])

    for group in range(tiles.shape[0] // GROUP):

        @pl.when(group < groups)
        def _():
            fetch(group).start()

    for copy in ready:
        copy.start()
    total[...] = jnp.zeros_like(total)
    for copy in ready:
        copy.wait()

    def multiply(group, carry):
        fetch(group).wait()
        found = []
        for k in range(GROUP):
            slot = group * GROUP + k
            row, col = rows[slot], cols[slot]
            weight = jnp.where(slot < used, jnp.where(row == col, 0.5, 1.0), 0.0).astype(f32)
            found.append(product(tiles[slot], place(row, meta), place(col, meta)) + (weight,))
        for at, part, weight in found:
            total[at] += part * weight
        return carry

    lax.fori_loop(0, groups, multiply, 0)


def mirror_kernel(meta, rows, cols, *refs):
    pieces, blocks, out = refs[:2], refs[2], refs[3:-5]
    window, total, tiles, piece_sems, tile_sems = refs[-5:]

    def product(tile, row, col):
        return col, dot_nn(window[row], tile)

    each_tile(meta, rows, cols, blocks, tiles, tile_sems, gather(pieces, window, piece_sems), product, total)
    for s, segment in enumerate(out):
        segment[...] = total[pl.ds(2 * s, 2)].astype(segment.dtype)


def direct_kernel(meta, rows, cols, *refs):
    pieces, blocks = refs[: 2 * REACH], refs[2 * REACH]
    x_other, cross_other, kept, near, kept_out, near_out, inner = refs[2 * REACH + 1 : -5]
    window, total, tiles, piece_sems, tile_sems = refs[-5:]

    def product(tile, row, col):
        return row, dot_nt(window[col], tile)

    each_tile(meta, rows, cols, blocks, tiles, tile_sems, gather(pieces, window, piece_sems), product, total)
    kept_out[...] = kept[...] + total[pl.ds(0, 2)]
    near_out[...] = (near[...] + total[pl.ds(2, 2)]).astype(bf16)
    size = inner.shape[1]
    own = jnp.zeros((size, size), f32)
    other = jnp.zeros((size, size), f32)
    for s in range(4):
        mine = total[s].astype(bf16)
        there = x_other[:, pl.ds(s * size, size)].astype(bf16) if s < 2 else cross_other[s - 2]
        own += dot_nt(mine, window[s])
        other += dot_nt(mine, there)
    inner[pl.ds(0, size), :] = own + own.T
    inner[pl.ds(size, size), :] = other


def tiles_call(kernel, out, meta, blocks, rows, cols, pieces, more, window, total):
    size, width = blocks.shape[1], pieces[0].shape[1]
    return pl.pallas_call(
        kernel,
        in_specs=[pl.BlockSpec(memory_space=SMEM)] * 3
        + [pl.BlockSpec(memory_space=pl.ANY)] * len(pieces)
        + [pl.BlockSpec(memory_space=pltpu.HBM)]
        + [pl.BlockSpec(memory_space=VMEM)] * len(more),
        out_specs=[pl.BlockSpec(memory_space=VMEM)] * len(out),
        scratch_shapes=[
            VMEM((window, width, size), bf16),
            VMEM((total, width, size), f32),
            VMEM(blocks.shape, bf16),
            pltpu.SemaphoreType.DMA((len(pieces),)),
            pltpu.SemaphoreType.DMA((blocks.shape[0] // GROUP,)),
        ],
        out_shape=out,
        compiler_params=pltpu.CompilerParams(vmem_limit_bytes=TILES_VMEM << 20),
        cost_estimate=pl.CostEstimate(flops=4 << 30, bytes_accessed=12 << 20, transcendentals=0),
    )(meta, rows, cols, *pieces, blocks, *more)


def descend_kernel(x, kept, near, far, two, out):
    size = kept.shape[2]
    for t in range(x.shape[1] // size):
        part = pl.ds(t * size, size)
        applied = kept[t] + near[t].astype(f32) + (far[t].astype(f32) + two[t].astype(f32))
        out[:, part] = x[:, part] - STEP_RATE * applied


def gram_kernel(core, mine, theirs, out):
    width = mine.shape[0]
    half = width // 2
    own, other = split(mine[...]), split(theirs[...])
    out[pl.ds(0, width), :] = dot3(dot_nt, own, own)
    ahead = core[0] == 0
    high = jnp.where(ahead, theirs[pl.ds(0, half), :], mine[pl.ds(half, half), :])
    low = [jnp.where(ahead, a, b) for a, b in zip(own, other)]
    out[pl.ds(width, half), :] = dot3(dot_nt, split(high), low)


def inverse_factor(g, w, high, low):
    n = g.shape[0]
    at_row = lax.broadcasted_iota(jnp.int32, (n, n), 0)
    at_col = lax.broadcasted_iota(jnp.int32, (n, n), 1)
    eye = jnp.where(at_row == at_col, 1.0, 0.0).astype(f32)
    diagonal = eye * g[...]
    by_row = lax.rsqrt(jnp.sum(diagonal, axis=1, keepdims=True))
    by_col = lax.rsqrt(jnp.sum(diagonal, axis=0, keepdims=True))
    unit = g[...] * by_row * by_col
    rounded = unit.astype(bf16)
    square = dot_nn(rounded, rounded).astype(bf16)
    fourth = dot_nn(square, square)
    scale = 1.9 / jnp.sqrt(jnp.sqrt(jnp.sqrt(jnp.sum(fourth * fourth, keepdims=True))))
    scaled = unit * scale
    high[...], low[...] = split(scaled)

    half = n // 2
    top, bottom = pl.ds(0, half), pl.ds(half, half)
    small = eye[:half, :half]
    triangle = (at_row > at_col)[:half, :half]

    def lower(e):
        return jnp.where(triangle, e, 0.5 * small * e)

    def read(ref):
        return ref[top, top], ref[bottom, top], ref[bottom, bottom]

    def product(a, b):
        return dot_nn(a[0], b[0]), dot_nn(a[1], b[0]) + dot_nn(a[2], b[1]), dot_nn(a[2], b[2])

    def narrow(blocks):
        return tuple(block.astype(bf16) for block in blocks)

    p = (lower(scaled[:half, :half] - small), scaled[half:, :half], lower(scaled[half:, half:] - small))
    pb = narrow(p)
    square = product(pb, pb)
    w[top, bottom] = jnp.zeros((half, half), f32)
    w[top, top] = small - p[0] + square[0]
    w[bottom, top] = square[1] - p[1]
    w[bottom, bottom] = small - p[2] + square[2]

    def improve(e, old):
        p = (lower(e[0] - small), e[1], lower(e[2] - small))
        pb = narrow(p)
        first = product(pb, narrow(old))
        second = product(pb, narrow(first))
        w[top, top] = old[0] - first[0] + second[0]
        w[bottom, top] = old[1] - first[1] + second[1]
        w[bottom, bottom] = old[2] - first[2] + second[2]
        return jnp.sqrt(sum(jnp.sum(block * block) for block in p))

    def congruence(nn, nt, cut, w, s):
        s00, s10, s11, s01 = s
        left = nn(w[0], s00)
        below, right = nn(w[1], s00) + nn(w[2], s10), nn(w[1], s01) + nn(w[2], s11)
        left, below, right = cut(left), cut(below), cut(right)
        return nt(left, w[0]), nt(below, w[0]), nt(below, w[1]) + nt(right, w[2])

    def whole(ref):
        return read(ref) + (ref[top, bottom],)

    def rough(state):
        old = read(w)
        e = congruence(dot_nn, dot_nt, lambda a: a.astype(bf16), narrow(old), whole(high))
        return state[0] + 1, improve(e, old)

    def fine(state):
        old = read(w)
        nn, nt = (lambda a, b: dot3(dot_nn, a, b)), (lambda a, b: dot3(dot_nt, a, b))
        e = congruence(nn, nt, split, [split(a) for a in old], list(zip(whole(high), whole(low))))
        return state[0] + 1, improve(e, old)

    def until(bound, most):
        return lambda state: (state[0] < most) & jnp.logical_not(state[1] <= bound)

    lax.while_loop(until(0.4, 16), rough, (0, jnp.float32(1e9)))
    _, error = lax.while_loop(until(0.1, 6), fine, (0, jnp.float32(1e9)))
    done = error <= 0.1

    @pl.when(done)
    def _():
        w[...] = w[...] * (by_col * jnp.sqrt(scale))

    @pl.when(jnp.logical_not(done))
    def _():
        w[...] = eye

        def eliminate(k, carry):
            lane = lax.broadcasted_iota(jnp.int32, (1, n), 1)
            below = lax.broadcasted_iota(jnp.int32, (n, 1), 0)
            row = g[pl.ds(k, 1), :]
            pivot = jnp.sum(jnp.where(lane == k, row, 0.0), axis=1, keepdims=True)
            column = jnp.sum(jnp.where(at_col == k, g[...], 0.0), axis=1, keepdims=True)
            ratio = jnp.where(below > k, column / pivot, 0.0)
            solved = w[pl.ds(k, 1), :]
            g[...] = g[...] - ratio * row
            w[...] = w[...] - ratio * solved
            w[pl.ds(k, 1), :] = solved * lax.rsqrt(pivot)
            return carry

        lax.fori_loop(0, n, eliminate, 0)


def lay_out(out, first, second):
    width = first.shape[1]
    out[pl.ds(0, width), pl.ds(0, width)] = first[:width]
    out[pl.ds(width, width), pl.ds(width, width)] = second[:width]
    below = jnp.concatenate([first[width:], second[width:]], axis=0)
    out[pl.ds(width, width), pl.ds(0, width)] = below
    out[pl.ds(0, width), pl.ds(width, width)] = below.T


def factor_kernel(rows_total, first_step, last, core, v, v_other, x, x_other, sums, sums_other, *refs):
    out, (g, w, high, low, update, rayleigh) = refs[:-6], refs[-6:]
    width, count = v.shape
    ahead = core[0] == 0

    def ordered(mine, theirs):
        mine, theirs = mine / rows_total, theirs / rows_total
        return jnp.where(ahead, mine, theirs), jnp.where(ahead, theirs, mine)

    blocks, rows, _ = sums.shape
    cut = rows - (width + width // 2) // blocks

    def joined(ref, low, high):
        return jnp.concatenate([ref[block, pl.ds(low, high - low), :] for block in range(blocks)], axis=0)

    inner, inner_other = joined(sums, 0, cut), joined(sums_other, 0, cut)
    first, second = ordered(inner[: 2 * width], inner_other[: 2 * width])
    rayleigh[pl.ds(0, width), pl.ds(0, width)] = first[:width]
    rayleigh[pl.ds(width, width), pl.ds(width, width)] = second[:width]
    across = first[width:] + second[width:].T
    rayleigh[pl.ds(0, width), pl.ds(width, width)] = across
    rayleigh[pl.ds(width, width), pl.ds(0, width)] = across.T
    lay_out(g, *ordered(joined(sums, cut, rows), joined(sums_other, cut, rows)))
    r = split(rayleigh[...])
    if first_step:
        lay_out(w, *ordered(inner[2 * width :], inner_other[2 * width :]))
        turned = dot3(dot_nn, split(w[...]), r)
        g[...] += STEP_RATE * (turned + turned.T)
        g[...] += dot3(dot_nn, r, split(STEP_RATE**2 * turned - (2 * STEP_RATE**2) * rayleigh[...]))
    else:
        g[...] += 2 * STEP_RATE * rayleigh[...] - STEP_RATE**2 * dot3(dot_nn, r, r)
    inverse_factor(g, w, high, low)
    start = pl.multiple_of(core[0] * width, width)
    there = width - start
    update[pl.ds(start, width), :] = x[...]
    update[pl.ds(there, width), :] = x_other[...]
    mix = split(w[pl.ds(start, width), :])
    mine = split(rayleigh[pl.ds(start, width), :])
    theirs = split(rayleigh[pl.ds(there, width), :])
    for t in range(count // width):
        part = pl.ds(t * width, width)
        old = split(update[:, part])
        here = v[:, part] + STEP_RATE * dot3(dot_nn, mine, old)
        update[pl.ds(there, width), part] = v_other[:, part] + STEP_RATE * dot3(dot_nn, theirs, old)
        update[pl.ds(start, width), part] = here
        solved = dot3(dot_nn, mix, split(update[:, part]))
        if last:
            out[0][part, :] = solved.T
            out[1][part, :] = ((x[:, part] - here) * (1 / STEP_RATE)).T
        else:
            out[0][:, part] = solved
            out[1][t] = solved.astype(bf16)


def swap_cores(a):
    return lax.ppermute(a, "vec", [(0, 1), (1, 0)])


def flip(a, mask):
    return lax.ppermute(a, "patch", [(i, i ^ mask) for i in range(lax.axis_size("patch"))])


def shift(a, pairs):
    devices = range(lax.axis_size("patch"))
    return lax.ppermute(a, "patch", [(i - 2 * pairs, i) for i in devices if i - 2 * pairs in devices])


def stride(a, back=False):
    devices = range(lax.axis_size("patch"))
    route = [(i - (2 if i // 2 % 2 else 6), i) for i in devices]
    return lax.ppermute(a, "patch", [(d, s) if back else (s, d) for s, d in route if s in devices])


def together(*arrays):
    return lax.optimization_barrier(arrays)


def reach(u, own_x):
    two, far = shift(u, 2), stride(together(u, own_x)[0])
    return two, flip(two, 1), far, flip(two, 2)


def place_order(parts, place):
    radix = len(parts)
    bit = 1
    while bit < radix:
        swapped = [parts[j ^ bit] for j in range(radix)]
        parts = [jnp.where(place & bit, b, a) for a, b in zip(parts, swapped)]
        bit *= 2
    return parts


def stages_of():
    left, step, stages = lax.axis_size("patch"), 1, []
    while left > 1:
        radix = 4 if left % 4 == 0 else 2
        stages.append((radix, step))
        left, step = left // radix, step * radix
    return stages


def scatter(a, stage):
    radix, step = stage
    place = (lax.axis_index("patch") // step) % radix
    parts = a.reshape(radix, a.shape[0] // radix, a.shape[1])
    a = lax.dynamic_index_in_dim(parts, place, 0, False)
    for m in range(1, radix):
        a = a + flip(lax.dynamic_index_in_dim(parts, place ^ m, 0, False), m * step)
    return a


def shared(a, stage):
    radix, step = stage
    return [a] + [flip(a, m * step) for m in range(1, radix)]


def in_order(parts, stage):
    radix, step = stage
    return jnp.concatenate(place_order(parts, (lax.axis_index("patch") // step) % radix), axis=0)


def sum_both(a, b, stages):
    for stage_a, stage_b in zip(stages[1:], stages[:-1], strict=True):
        a, b = together(scatter(a, stage_a), scatter(b, stage_b))
    cut = a.shape[0]
    parts = shared(jnp.concatenate([a, b]), stages[-1])
    joined = jnp.concatenate([in_order([part[:cut] for part in parts], stages[-1]), sum(part[cut:] for part in parts)])
    blocks = 1
    for stage in stages[-2::-1]:
        joined = in_order(shared(joined, stage), stage)
        blocks *= stage[0]
    return joined.reshape(blocks, joined.shape[0] // blocks, joined.shape[1])


def shards(vectors, blocks, block_row, block_col, block_count):
    count, width = vectors.shape
    size = blocks.shape[1]
    rows_total = float(count * lax.axis_size("patch"))
    position = lax.axis_index("patch")
    odd = position % 2
    meta = jnp.stack([block_count[0], 2 * (position - odd) - 4 * (REACH - 1), odd, position // 2 % 2]).astype(jnp.int32)
    core = lax.axis_index("vec").astype(jnp.int32).reshape(1)
    stages = stages_of()
    flat, chunk = shape(f32, width, count), shape(bf16, count // size, width, size)
    x, u = call(pack_kernel, [flat, chunk], [vectors])
    for step in range(STEPS):
        last = step == STEPS - 1
        own_x = flip(u, 1)
        x_other = swap_cores(x)
        cross_other = swap_cores(own_x)
        table = (meta, blocks, block_row, block_col)
        segment = (2, width, size)
        sums = tiles_call(
            mirror_kernel, [shape(kind, *segment) for kind in SEGMENT_KINDS], *table, [u, own_x], [], 4, 4 * REACH
        )
        same, cross = sums[::2], sums[1::2]
        two, two_x, far, side = reach(u, own_x)
        out_side_x, out_far, out_side = together(cross[3], cross[2], same[3], far, two_x, side)[:3]
        pieces = [u, own_x, two, two_x, far, flip(far, 1), side, flip(two_x, 2)]
        kept, near, inner = tiles_call(
            direct_kernel,
            [shape(f32, *segment), shape(bf16, *segment), shape(f32, 2 * width, width)],
            *table,
            pieces,
            [x_other, cross_other, same[0], cross[0]],
            4 * REACH,
            4,
        )
        side_x, far_x, side = flip(out_side_x, 2), flip(out_far, 1), flip(out_side, 2)
        two_out = (cross[1] + side_x.astype(f32)).astype(bf16)
        two_x, far = flip(two_out, 1), stride((same[2] + far_x.astype(f32)).astype(bf16), True)
        two = shift((same[1] + (two_x.astype(f32) + side.astype(f32))).astype(bf16), -2)
        inner_out = [inner]
        if step == 0:
            inner_out += call(gram_kernel, [shape(f32, width + width // 2, width)], [core, x, x_other], smem=1)
        inner = scatter(jnp.concatenate(inner_out), stages[0])
        inner, *joined = together(inner, flip(near, 1), far, two)
        (v,) = call(descend_kernel, [flat], [x, kept, *joined])
        v_other = swap_cores(v)
        (gram,) = call(gram_kernel, [shape(f32, width + width // 2, width)], [core, v, v_other], smem=1)
        inner, gram = together(inner, gram)
        sums = sum_both(inner, gram, stages)
        full = (2 * width, 2 * width)
        wide = shape(f32, count, width)
        out = call(
            lambda *refs: factor_kernel(rows_total, step == 0, last, *refs),
            [wide, wide] if last else [flat, chunk],
            [core, v, v_other, x, x_other, sums, swap_cores(sums)],
            scratch=[VMEM(full, f32), VMEM(full, f32), VMEM(full, bf16), VMEM(full, bf16)]
            + [VMEM((2 * width, count), f32), VMEM(full, f32)],
            smem=1,
            flops=16 << 30,
            vmem=28,
        )
        x, u = out
    return x, u


def solution(mesh):
    in_specs = (P("patch", "vec"), P("patch", None, None), P("patch"), P("patch"), P("patch"))
    out_specs = (P("patch", "vec"), P("patch", "vec"))
    return jax.shard_map(shards, mesh=mesh, in_specs=in_specs, out_specs=out_specs, check_vma=False)
```

```python
import jax
import jax.numpy as jnp
from jax import lax
from jax.experimental import pallas as pl
from jax.experimental.pallas import tpu as pltpu
from jax.sharding import PartitionSpec as P

STEPS = 2
STEP_RATE = 0.25
GROUP = 8
REACH = 4

f32, bf16 = jnp.float32, jnp.bfloat16
SEGMENT_KINDS = (f32, f32, f32, f32, f32, bf16, bf16, bf16)
TILES_VMEM = 48
SCALARS = 4
VMEM, SMEM = pltpu.VMEM, pltpu.SMEM


def dot_nn(a, b):
    return lax.dot_general(a, b, (((1,), (0,)), ((), ())), preferred_element_type=f32)


def dot_nt(a, b):
    return lax.dot_general(a, b, (((1,), (1,)), ((), ())), preferred_element_type=f32)


def split(a):
    high = a.astype(bf16)
    return high, (a - high.astype(f32)).astype(bf16)


def dot3(dot, a, b):
    (ah, al), (bh, bl) = a, b
    return dot(ah, bh) + (dot(ah, bl) + dot(al, bh))


def call(kernel, out, args, scratch=(), smem=0, flops=1 << 28, vmem=16):
    moved = sum(a.size * a.dtype.itemsize for a in args) + sum(o.size * o.dtype.itemsize for o in out)
    return pl.pallas_call(
        kernel,
        out_shape=out,
        in_specs=[pl.BlockSpec(memory_space=SMEM)] * smem + [pl.BlockSpec(memory_space=VMEM)] * (len(args) - smem),
        out_specs=[pl.BlockSpec(memory_space=VMEM)] * len(out),
        scratch_shapes=list(scratch),
        compiler_params=pltpu.CompilerParams(vmem_limit_bytes=vmem << 20),
        cost_estimate=pl.CostEstimate(flops=flops, bytes_accessed=moved, transcendentals=0),
    )(*args)


def shape(dtype, *dims):
    return jax.ShapeDtypeStruct(dims, dtype)


def fold(a):
    half, quarter = a.shape[0] // 2, a.shape[0] // 4
    below = a[half:, :half]
    return jnp.concatenate(
        [
            jnp.concatenate([a[:half, :half], a[half:, half:]], axis=1),
            jnp.concatenate([below[:quarter], below[quarter:]], axis=1),
        ],
        axis=0,
    )


def unfold(a):
    half = a.shape[1] // 2
    below = jnp.concatenate([a[half:, :half], a[half:, half:]], axis=0)
    return jnp.concatenate(
        [jnp.concatenate([a[:half, :half], below.T], axis=1), jnp.concatenate([below, a[:half, half:]], axis=1)], axis=0
    )


def pack_kernel(vectors, columns, chunk):
    size = chunk.shape[2]
    for t in range(chunk.shape[0]):
        turned = vectors[pl.ds(t * size, size), :].T
        columns[:, pl.ds(t * size, size)] = turned
        chunk[t] = turned.astype(bf16)


def place(tile, meta):
    start, odd, pair_odd = meta[1], meta[2], meta[3]
    w = tile - start
    back = REACH - 1 - w // 4
    role = jnp.where(back % 2 == 1, 2 + ((back // 2) ^ pair_odd ^ 1), back // 2)
    return role * 4 + 2 * (((w % 4) // 2) ^ odd) + w % 2


def gather(pieces, window, sems):
    return [pltpu.make_async_copy(piece, window.at[pl.ds(2 * s, 2)], sems.at[s]) for s, piece in enumerate(pieces)]


def each_tile(meta, blocks, tiles, sems, ready, product, total):
    used = meta[0]
    groups = (used + GROUP - 1) // GROUP

    def fetch(group):
        part = pl.ds(group * GROUP, GROUP)
        return pltpu.make_async_copy(blocks.at[part], tiles.at[part], sems.at[group])

    for group in range(tiles.shape[0] // GROUP):

        @pl.when(group < groups)
        def _():
            fetch(group).start()

    for copy in ready:
        copy.start()
    total[...] = jnp.zeros_like(total)
    for copy in ready:
        copy.wait()

    def multiply(group, carry):
        fetch(group).wait()
        found = []
        for k in range(GROUP):
            slot = group * GROUP + k
            row, col = meta[SCALARS + slot], meta[SCALARS + blocks.shape[0] + slot]
            weight = jnp.where(slot < used, jnp.where(row == col, 0.5, 1.0), 0.0).astype(f32)
            found.append(product(tiles[slot], place(row, meta), place(col, meta)) + (weight,))
        for at, part, weight in found:
            total[at] += part * weight
        return carry

    lax.fori_loop(0, groups, multiply, 0)


def mirror_kernel(meta, *refs):
    pieces, blocks, out = refs[:2], refs[2], refs[3:-5]
    window, total, tiles, piece_sems, tile_sems = refs[-5:]

    def product(tile, row, col):
        return col, dot_nn(window[row], tile)

    each_tile(meta, blocks, tiles, tile_sems, gather(pieces, window, piece_sems), product, total)
    for s, segment in enumerate(out):
        segment[...] = total[pl.ds(2 * s, 2)].astype(segment.dtype)


def direct_kernel(meta, *refs):
    pieces, blocks = refs[: 2 * REACH], refs[2 * REACH]
    x_other, cross_other, kept, near, kept_out, near_out, inner = refs[2 * REACH + 1 : -5]
    window, total, tiles, piece_sems, tile_sems = refs[-5:]

    def product(tile, row, col):
        return row, dot_nt(window[col], tile)

    each_tile(meta, blocks, tiles, tile_sems, gather(pieces, window, piece_sems), product, total)
    kept_out[...] = kept[...] + total[pl.ds(0, 2)]
    near_out[...] = (near[...] + total[pl.ds(2, 2)]).astype(bf16)
    size = inner.shape[1]
    own = jnp.zeros((size, size), f32)
    other = jnp.zeros((size, size), f32)
    for s in range(4):
        mine = total[s].astype(bf16)
        there = x_other[:, pl.ds(s * size, size)].astype(bf16) if s < 2 else cross_other[s - 2]
        own += dot_nt(mine, window[s])
        other += dot_nt(mine, there)
    inner[pl.ds(0, 3 * size // 4), :] = fold(own + own.T)
    inner[pl.ds(3 * size // 4, size), :] = other


def tiles_call(kernel, out, meta, blocks, pieces, more, window, total):
    size, width = blocks.shape[1], pieces[0].shape[1]
    return pl.pallas_call(
        kernel,
        in_specs=[pl.BlockSpec(memory_space=SMEM)]
        + [pl.BlockSpec(memory_space=pl.ANY)] * len(pieces)
        + [pl.BlockSpec(memory_space=pltpu.HBM)]
        + [pl.BlockSpec(memory_space=VMEM)] * len(more),
        out_specs=[pl.BlockSpec(memory_space=VMEM)] * len(out),
        scratch_shapes=[
            VMEM((window, width, size), bf16),
            VMEM((total, width, size), f32),
            VMEM(blocks.shape, bf16),
            pltpu.SemaphoreType.DMA((len(pieces),)),
            pltpu.SemaphoreType.DMA((blocks.shape[0] // GROUP,)),
        ],
        out_shape=out,
        compiler_params=pltpu.CompilerParams(vmem_limit_bytes=TILES_VMEM << 20),
        cost_estimate=pl.CostEstimate(flops=4 << 30, bytes_accessed=12 << 20, transcendentals=0),
    )(meta, *pieces, blocks, *more)


def descend_kernel(x, kept, near, far, two, out):
    size = kept.shape[2]
    for t in range(x.shape[1] // size):
        part = pl.ds(t * size, size)
        applied = kept[t] + near[t].astype(f32) + (far[t].astype(f32) + two[t].astype(f32))
        out[:, part] = x[:, part] - STEP_RATE * applied


def gram_kernel(core, mine, theirs, out):
    width = mine.shape[0]
    half = width // 2
    own, other = split(mine[...]), split(theirs[...])
    out[pl.ds(0, 3 * width // 4), :] = fold(dot3(dot_nt, own, own))
    ahead = core[0] == 0
    high = jnp.where(ahead, theirs[pl.ds(0, half), :], mine[pl.ds(half, half), :])
    low = [jnp.where(ahead, a, b) for a, b in zip(own, other)]
    out[pl.ds(3 * width // 4, half), :] = dot3(dot_nt, split(high), low)


def inverse_factor(g, w, high, low):
    n = g.shape[0]
    at_row = lax.broadcasted_iota(jnp.int32, (n, n), 0)
    at_col = lax.broadcasted_iota(jnp.int32, (n, n), 1)
    eye = jnp.where(at_row == at_col, 1.0, 0.0).astype(f32)
    diagonal = eye * g[...]
    by_row = lax.rsqrt(jnp.sum(diagonal, axis=1, keepdims=True))
    by_col = lax.rsqrt(jnp.sum(diagonal, axis=0, keepdims=True))
    unit = g[...] * by_row * by_col
    rounded = unit.astype(bf16)
    square = dot_nn(rounded, rounded).astype(bf16)
    fourth = dot_nn(square, square)
    scale = 1.9 / jnp.sqrt(jnp.sqrt(jnp.sqrt(jnp.sum(fourth * fourth, keepdims=True))))
    scaled = unit * scale
    high[...], low[...] = split(scaled)

    half = n // 2
    top, bottom = pl.ds(0, half), pl.ds(half, half)
    small = eye[:half, :half]
    triangle = (at_row > at_col)[:half, :half]

    def lower(e):
        return jnp.where(triangle, e, 0.5 * small * e)

    def read(ref):
        return ref[top, top], ref[bottom, top], ref[bottom, bottom]

    def product(a, b):
        return dot_nn(a[0], b[0]), dot_nn(a[1], b[0]) + dot_nn(a[2], b[1]), dot_nn(a[2], b[2])

    def narrow(blocks):
        return tuple(block.astype(bf16) for block in blocks)

    p = (lower(scaled[:half, :half] - small), scaled[half:, :half], lower(scaled[half:, half:] - small))
    pb = narrow(p)
    square = product(pb, pb)
    w[top, bottom] = jnp.zeros((half, half), f32)
    w[top, top] = small - p[0] + square[0]
    w[bottom, top] = square[1] - p[1]
    w[bottom, bottom] = small - p[2] + square[2]

    def improve(e, old):
        p = (lower(e[0] - small), e[1], lower(e[2] - small))
        pb = narrow(p)
        first = product(pb, narrow(old))
        second = product(pb, narrow(first))
        w[top, top] = old[0] - first[0] + second[0]
        w[bottom, top] = old[1] - first[1] + second[1]
        w[bottom, bottom] = old[2] - first[2] + second[2]
        return jnp.sqrt(sum(jnp.sum(block * block) for block in p))

    def congruence(nn, nt, cut, w, s):
        s00, s10, s11, s01 = s
        left = nn(w[0], s00)
        below, right = nn(w[1], s00) + nn(w[2], s10), nn(w[1], s01) + nn(w[2], s11)
        left, below, right = cut(left), cut(below), cut(right)
        return nt(left, w[0]), nt(below, w[0]), nt(below, w[1]) + nt(right, w[2])

    def whole(ref):
        return read(ref) + (ref[top, bottom],)

    def rough(state):
        old = read(w)
        e = congruence(dot_nn, dot_nt, lambda a: a.astype(bf16), narrow(old), whole(high))
        return state[0] + 1, improve(e, old)

    def fine(state):
        old = read(w)
        nn, nt = (lambda a, b: dot3(dot_nn, a, b)), (lambda a, b: dot3(dot_nt, a, b))
        e = congruence(nn, nt, split, [split(a) for a in old], list(zip(whole(high), whole(low))))
        return state[0] + 1, improve(e, old)

    def until(bound, most):
        return lambda state: (state[0] < most) & jnp.logical_not(state[1] <= bound)

    lax.while_loop(until(0.4, 16), rough, (0, jnp.float32(1e9)))
    _, error = lax.while_loop(until(0.1, 6), fine, (0, jnp.float32(1e9)))
    done = error <= 0.1

    @pl.when(done)
    def _():
        w[...] = w[...] * (by_col * jnp.sqrt(scale))

    @pl.when(jnp.logical_not(done))
    def _():
        w[...] = eye

        def eliminate(k, carry):
            lane = lax.broadcasted_iota(jnp.int32, (1, n), 1)
            below = lax.broadcasted_iota(jnp.int32, (n, 1), 0)
            row = g[pl.ds(k, 1), :]
            pivot = jnp.sum(jnp.where(lane == k, row, 0.0), axis=1, keepdims=True)
            column = jnp.sum(jnp.where(at_col == k, g[...], 0.0), axis=1, keepdims=True)
            ratio = jnp.where(below > k, column / pivot, 0.0)
            solved = w[pl.ds(k, 1), :]
            g[...] = g[...] - ratio * row
            w[...] = w[...] - ratio * solved
            w[pl.ds(k, 1), :] = solved * lax.rsqrt(pivot)
            return carry

        lax.fori_loop(0, n, eliminate, 0)


def lay_out(out, first, second):
    width = first.shape[1]
    folded = 3 * width // 4
    out[pl.ds(0, width), pl.ds(0, width)] = unfold(first[:folded])
    out[pl.ds(width, width), pl.ds(width, width)] = unfold(second[:folded])
    below = jnp.concatenate([first[folded:], second[folded:]], axis=0)
    out[pl.ds(width, width), pl.ds(0, width)] = below
    out[pl.ds(0, width), pl.ds(width, width)] = below.T


def factor_kernel(rows_total, first_step, last, core, v, v_other, x, x_other, sums, sums_other, *refs):
    out, (g, w, high, low, update, rayleigh) = refs[:-6], refs[-6:]
    width, count = v.shape
    ahead = core[0] == 0

    def ordered(mine, theirs):
        mine, theirs = mine / rows_total, theirs / rows_total
        return jnp.where(ahead, mine, theirs), jnp.where(ahead, theirs, mine)

    blocks, rows, _ = sums.shape
    cut = rows - 5 * width // 4 // blocks
    folded, extra = 3 * width // 4, 7 * width // 4

    def joined(ref, low, high):
        return jnp.concatenate([ref[block, pl.ds(low, high - low), :] for block in range(blocks)], axis=0)

    inner, inner_other = joined(sums, 0, cut), joined(sums_other, 0, cut)
    first, second = ordered(inner[:extra], inner_other[:extra])
    rayleigh[pl.ds(0, width), pl.ds(0, width)] = unfold(first[:folded])
    rayleigh[pl.ds(width, width), pl.ds(width, width)] = unfold(second[:folded])
    across = first[folded:] + second[folded:].T
    rayleigh[pl.ds(0, width), pl.ds(width, width)] = across
    rayleigh[pl.ds(width, width), pl.ds(0, width)] = across.T
    lay_out(g, *ordered(joined(sums, cut, rows), joined(sums_other, cut, rows)))
    r = split(rayleigh[...])
    if first_step:
        end = extra + 5 * width // 4
        lay_out(w, *ordered(inner[extra:end], inner_other[extra:end]))
        turned = dot3(dot_nn, split(w[...]), r)
        g[...] += STEP_RATE * (turned + turned.T)
        g[...] += dot3(dot_nn, r, split(STEP_RATE**2 * turned - (2 * STEP_RATE**2) * rayleigh[...]))
    else:
        g[...] += 2 * STEP_RATE * rayleigh[...] - STEP_RATE**2 * dot3(dot_nn, r, r)
    inverse_factor(g, w, high, low)
    start = pl.multiple_of(core[0] * width, width)
    there = width - start
    update[pl.ds(start, width), :] = x[...]
    update[pl.ds(there, width), :] = x_other[...]
    mix = split(w[pl.ds(start, width), :])
    mine = split(rayleigh[pl.ds(start, width), :])
    theirs = split(rayleigh[pl.ds(there, width), :])
    for t in range(count // width):
        part = pl.ds(t * width, width)
        old = split(update[:, part])
        here = v[:, part] + STEP_RATE * dot3(dot_nn, mine, old)
        update[pl.ds(there, width), part] = v_other[:, part] + STEP_RATE * dot3(dot_nn, theirs, old)
        update[pl.ds(start, width), part] = here
        solved = dot3(dot_nn, mix, split(update[:, part]))
        if last:
            out[0][part, :] = solved.T
            out[1][part, :] = ((x[:, part] - here) * (1 / STEP_RATE)).T
        else:
            out[0][:, part] = solved
            out[1][t] = solved.astype(bf16)


def swap_cores(a):
    return lax.ppermute(a, "vec", [(0, 1), (1, 0)])


def flip(a, mask):
    return lax.ppermute(a, "patch", [(i, i ^ mask) for i in range(lax.axis_size("patch"))])


def shift(a, pairs):
    devices = range(lax.axis_size("patch"))
    return lax.ppermute(a, "patch", [(i - 2 * pairs, i) for i in devices if i - 2 * pairs in devices])


def stride(a, back=False):
    devices = range(lax.axis_size("patch"))
    route = [(i - (2 if i // 2 % 2 else 6), i) for i in devices]
    return lax.ppermute(a, "patch", [(d, s) if back else (s, d) for s, d in route if s in devices])


def together(*arrays):
    return lax.optimization_barrier(arrays)


def reach(u, own_x):
    two, far = shift(u, 2), stride(together(u, own_x)[0])
    return two, flip(two, 1), far, flip(two, 2)


def place_order(parts, place):
    radix = len(parts)
    bit = 1
    while bit < radix:
        swapped = [parts[j ^ bit] for j in range(radix)]
        parts = [jnp.where(place & bit, b, a) for a, b in zip(parts, swapped)]
        bit *= 2
    return parts


def stages_of():
    left, step, stages = lax.axis_size("patch"), 1, []
    while left > 1:
        radix = 4 if left % 4 == 0 else 2
        stages.append((radix, step))
        left, step = left // radix, step * radix
    return stages


def scatter(a, stage):
    radix, step = stage
    place = (lax.axis_index("patch") // step) % radix
    parts = a.reshape(radix, a.shape[0] // radix, a.shape[1])
    a = lax.dynamic_index_in_dim(parts, place, 0, False)
    for m in range(1, radix):
        a = a + flip(lax.dynamic_index_in_dim(parts, place ^ m, 0, False), m * step)
    return a


def shared(a, stage):
    radix, step = stage
    return [a] + [flip(a, m * step) for m in range(1, radix)]


def in_order(parts, stage):
    radix, step = stage
    return jnp.concatenate(place_order(parts, (lax.axis_index("patch") // step) % radix), axis=0)


def sum_both(a, b, stages):
    for stage_a, stage_b in zip(stages[1:], stages[:-1], strict=True):
        a, b = together(scatter(a, stage_a), scatter(b, stage_b))
    cut = a.shape[0]
    parts = shared(jnp.concatenate([a, b]), stages[-1])
    joined = jnp.concatenate([in_order([part[:cut] for part in parts], stages[-1]), sum(part[cut:] for part in parts)])
    blocks = 1
    for stage in stages[-2::-1]:
        joined = in_order(shared(joined, stage), stage)
        blocks *= stage[0]
    return joined.reshape(blocks, joined.shape[0] // blocks, joined.shape[1])


def shards(vectors, blocks, block_row, block_col, block_count):
    count, width = vectors.shape
    size = blocks.shape[1]
    rows_total = float(count * lax.axis_size("patch"))
    position = lax.axis_index("patch")
    odd = position % 2
    meta = jnp.stack([block_count[0], 2 * (position - odd) - 4 * (REACH - 1), odd, position // 2 % 2]).astype(jnp.int32)
    meta = jnp.concatenate([meta, block_row, block_col])
    core = lax.axis_index("vec").astype(jnp.int32).reshape(1)
    stages = stages_of()
    flat, chunk = shape(f32, width, count), shape(bf16, count // size, width, size)
    x, u = call(pack_kernel, [flat, chunk], [vectors])
    for step in range(STEPS):
        last = step == STEPS - 1
        own_x = flip(u, 1)
        x_other = swap_cores(x)
        cross_other = swap_cores(own_x)
        table = (meta, blocks)
        segment = (2, width, size)
        sums = tiles_call(
            mirror_kernel, [shape(kind, *segment) for kind in SEGMENT_KINDS], *table, [u, own_x], [], 4, 4 * REACH
        )
        same, cross = sums[::2], sums[1::2]
        two, two_x, far, side = reach(u, own_x)
        out_side_x, out_far, out_side = together(cross[3], cross[2], same[3], far, two_x, side)[:3]
        pieces = [u, own_x, two, two_x, far, flip(far, 1), side, flip(two_x, 2)]
        kept, near, inner = tiles_call(
            direct_kernel,
            [shape(f32, *segment), shape(bf16, *segment), shape(f32, 7 * width // 4, width)],
            *table,
            pieces,
            [x_other, cross_other, same[0], cross[0]],
            4 * REACH,
            4,
        )
        side_x, far_x, side = flip(out_side_x, 2), flip(out_far, 1), flip(out_side, 2)
        two_out = (cross[1] + side_x.astype(f32)).astype(bf16)
        two_x, far = flip(two_out, 1), stride((same[2] + far_x.astype(f32)).astype(bf16), True)
        two = shift((same[1] + (two_x.astype(f32) + side.astype(f32))).astype(bf16), -2)
        inner_out = [inner]
        if step == 0:
            inner_out += call(gram_kernel, [shape(f32, 5 * width // 4, width)], [core, x, x_other], smem=1)
        inner = jnp.concatenate(inner_out)
        inner = jnp.pad(inner, ((0, -inner.shape[0] % lax.axis_size("patch")), (0, 0)))
        inner = scatter(inner, stages[0])
        inner, *joined = together(inner, flip(near, 1), far, two)
        (v,) = call(descend_kernel, [flat], [x, kept, *joined])
        v_other = swap_cores(v)
        (gram,) = call(gram_kernel, [shape(f32, 5 * width // 4, width)], [core, v, v_other], smem=1)
        inner, gram = together(inner, gram)
        sums = sum_both(inner, gram, stages)
        full = (2 * width, 2 * width)
        wide = shape(f32, count, width)
        out = call(
            lambda *refs: factor_kernel(rows_total, step == 0, last, *refs),
            [wide, wide] if last else [flat, chunk],
            [core, v, v_other, x, x_other, sums, swap_cores(sums)],
            scratch=[VMEM(full, f32), VMEM(full, f32), VMEM(full, bf16), VMEM(full, bf16)]
            + [VMEM((2 * width, count), f32), VMEM(full, f32)],
            smem=1,
            flops=16 << 30,
            vmem=28,
        )
        x, u = out
    return x, u


def solution(mesh):
    in_specs = (P("patch", "vec"), P("patch", None, None), P("patch"), P("patch"), P("patch"))
    out_specs = (P("patch", "vec"), P("patch", "vec"))
    return jax.shard_map(shards, mesh=mesh, in_specs=in_specs, out_specs=out_specs, check_vma=False)
```

```python
import jax
import jax.numpy as jnp
from jax import lax
from jax.experimental import pallas as pl
from jax.experimental.pallas import tpu as pltpu
from jax.sharding import PartitionSpec as P

STEPS = 2
STEP_RATE = 0.25
GROUP = 8
REACH = 4

f32, bf16 = jnp.float32, jnp.bfloat16
SEGMENT_KINDS = (f32, f32, f32, f32, f32, bf16, bf16, bf16)
TILES_VMEM = 48
SCALARS = 4
VMEM, SMEM = pltpu.VMEM, pltpu.SMEM


def dot_nn(a, b):
    return lax.dot_general(a, b, (((1,), (0,)), ((), ())), preferred_element_type=f32)


def dot_nt(a, b):
    return lax.dot_general(a, b, (((1,), (1,)), ((), ())), preferred_element_type=f32)


def split(a):
    high = a.astype(bf16)
    return high, (a - high.astype(f32)).astype(bf16)


def dot3(dot, a, b):
    (ah, al), (bh, bl) = a, b
    return dot(ah, bh) + (dot(ah, bl) + dot(al, bh))


def call(kernel, out, args, scratch=(), smem=0, flops=1 << 28, vmem=16):
    moved = sum(a.size * a.dtype.itemsize for a in args) + sum(o.size * o.dtype.itemsize for o in out)
    return pl.pallas_call(
        kernel,
        out_shape=out,
        in_specs=[pl.BlockSpec(memory_space=SMEM)] * smem + [pl.BlockSpec(memory_space=VMEM)] * (len(args) - smem),
        out_specs=[pl.BlockSpec(memory_space=VMEM)] * len(out),
        scratch_shapes=list(scratch),
        compiler_params=pltpu.CompilerParams(vmem_limit_bytes=vmem << 20),
        cost_estimate=pl.CostEstimate(flops=flops, bytes_accessed=moved, transcendentals=0),
    )(*args)


def shape(dtype, *dims):
    return jax.ShapeDtypeStruct(dims, dtype)


def fold(a):
    half, quarter = a.shape[0] // 2, a.shape[0] // 4
    below = a[half:, :half]
    return jnp.concatenate(
        [
            jnp.concatenate([a[:half, :half], a[half:, half:]], axis=1),
            jnp.concatenate([below[:quarter], below[quarter:]], axis=1),
        ],
        axis=0,
    )


def unfold(a):
    half = a.shape[1] // 2
    below = jnp.concatenate([a[half:, :half], a[half:, half:]], axis=0)
    return jnp.concatenate(
        [jnp.concatenate([a[:half, :half], below.T], axis=1), jnp.concatenate([below, a[:half, half:]], axis=1)], axis=0
    )


def pack_kernel(vectors, columns, chunk):
    size = chunk.shape[2]
    for t in range(chunk.shape[0]):
        turned = vectors[pl.ds(t * size, size), :].T
        columns[:, pl.ds(t * size, size)] = turned
        chunk[t] = turned.astype(bf16)


def place(tile, meta):
    start, odd, pair_odd = meta[1], meta[2], meta[3]
    w = tile - start
    back = REACH - 1 - w // 4
    role = jnp.where(back % 2 == 1, 2 + ((back // 2) ^ pair_odd ^ 1), back // 2)
    return role * 4 + 2 * (((w % 4) // 2) ^ odd) + w % 2


def gather(pieces, window, sems):
    return [pltpu.make_async_copy(piece, window.at[pl.ds(2 * s, 2)], sems.at[s]) for s, piece in enumerate(pieces)]


def each_tile(meta, blocks, tiles, sems, ready, product, total):
    used = meta[0]
    groups = (used + GROUP - 1) // GROUP

    def fetch(group):
        part = pl.ds(group * GROUP, GROUP)
        return pltpu.make_async_copy(blocks.at[part], tiles.at[part], sems.at[group])

    for group in range(tiles.shape[0] // GROUP):

        @pl.when(group < groups)
        def _():
            fetch(group).start()

    for copy in ready:
        copy.start()
    total[...] = jnp.zeros_like(total)
    for copy in ready:
        copy.wait()

    def multiply(group, carry):
        fetch(group).wait()
        found = []
        for k in range(GROUP):
            slot = group * GROUP + k
            row, col = meta[SCALARS + slot], meta[SCALARS + blocks.shape[0] + slot]
            weight = jnp.where(slot < used, jnp.where(row == col, 0.5, 1.0), 0.0).astype(f32)
            found.append(product(tiles[slot], place(row, meta), place(col, meta)) + (weight,))
        for at, part, weight in found:
            total[at] += part * weight
        return carry

    lax.fori_loop(0, groups, multiply, 0)


def mirror_kernel(meta, *refs):
    pieces, blocks, out = refs[:2], refs[2], refs[3:-5]
    window, total, tiles, piece_sems, tile_sems = refs[-5:]

    def product(tile, row, col):
        return col, dot_nn(window[row], tile)

    each_tile(meta, blocks, tiles, tile_sems, gather(pieces, window, piece_sems), product, total)
    for s, segment in enumerate(out):
        segment[...] = total[pl.ds(2 * s, 2)].astype(segment.dtype)


def direct_kernel(meta, *refs):
    pieces, blocks = refs[: 2 * REACH], refs[2 * REACH]
    x_other, cross_other, kept, near, kept_out, near_out, inner = refs[2 * REACH + 1 : -5]
    window, total, tiles, piece_sems, tile_sems = refs[-5:]

    def product(tile, row, col):
        return row, dot_nt(window[col], tile)

    each_tile(meta, blocks, tiles, tile_sems, gather(pieces, window, piece_sems), product, total)
    kept_out[...] = kept[...] + total[pl.ds(0, 2)]
    near_out[...] = (near[...] + total[pl.ds(2, 2)]).astype(bf16)
    size = inner.shape[1]
    own = jnp.zeros((size, size), f32)
    other = jnp.zeros((size, size), f32)
    for s in range(4):
        mine = total[s].astype(bf16)
        there = x_other[:, pl.ds(s * size, size)].astype(bf16) if s < 2 else cross_other[s - 2]
        own += dot_nt(mine, window[s])
        other += dot_nt(mine, there)
    inner[pl.ds(0, 3 * size // 4), :] = fold(own + own.T)
    inner[pl.ds(3 * size // 4, size), :] = other


def tiles_call(kernel, out, meta, blocks, pieces, more, window, total):
    size, width = blocks.shape[1], pieces[0].shape[1]
    return pl.pallas_call(
        kernel,
        in_specs=[pl.BlockSpec(memory_space=SMEM)]
        + [pl.BlockSpec(memory_space=pl.ANY)] * len(pieces)
        + [pl.BlockSpec(memory_space=pltpu.HBM)]
        + [pl.BlockSpec(memory_space=VMEM)] * len(more),
        out_specs=[pl.BlockSpec(memory_space=VMEM)] * len(out),
        scratch_shapes=[
            VMEM((window, width, size), bf16),
            VMEM((total, width, size), f32),
            VMEM(blocks.shape, bf16),
            pltpu.SemaphoreType.DMA((len(pieces),)),
            pltpu.SemaphoreType.DMA((blocks.shape[0] // GROUP,)),
        ],
        out_shape=out,
        compiler_params=pltpu.CompilerParams(vmem_limit_bytes=TILES_VMEM << 20),
        cost_estimate=pl.CostEstimate(flops=4 << 30, bytes_accessed=12 << 20, transcendentals=0),
    )(meta, *pieces, blocks, *more)


def descend_kernel(x, kept, near, far, two, out):
    size = kept.shape[2]
    for t in range(x.shape[1] // size):
        part = pl.ds(t * size, size)
        applied = kept[t] + near[t].astype(f32) + (far[t].astype(f32) + two[t].astype(f32))
        out[:, part] = x[:, part] - STEP_RATE * applied


def gram_kernel(core, mine, theirs, out):
    width = mine.shape[0]
    half = width // 2
    own, other = split(mine[...]), split(theirs[...])
    out[pl.ds(0, 3 * width // 4), :] = fold(dot3(dot_nt, own, own))
    ahead = core[0] == 0
    high = jnp.where(ahead, theirs[pl.ds(0, half), :], mine[pl.ds(half, half), :])
    low = [jnp.where(ahead, a, b) for a, b in zip(own, other)]
    out[pl.ds(3 * width // 4, half), :] = dot3(dot_nt, split(high), low)


def inverse_factor(g, w, high, low):
    n = g.shape[0]
    at_row = lax.broadcasted_iota(jnp.int32, (n, n), 0)
    at_col = lax.broadcasted_iota(jnp.int32, (n, n), 1)
    eye = jnp.where(at_row == at_col, 1.0, 0.0).astype(f32)
    diagonal = eye * g[...]
    by_row = lax.rsqrt(jnp.sum(diagonal, axis=1, keepdims=True))
    by_col = lax.rsqrt(jnp.sum(diagonal, axis=0, keepdims=True))
    unit = g[...] * by_row * by_col
    rounded = unit.astype(bf16)
    square = dot_nn(rounded, rounded).astype(bf16)
    fourth = dot_nn(square, square)
    scale = 1.9 / jnp.sqrt(jnp.sqrt(jnp.sqrt(jnp.sum(fourth * fourth, keepdims=True))))
    scaled = unit * scale
    high[...], low[...] = split(scaled)

    half = n // 2
    top, bottom = pl.ds(0, half), pl.ds(half, half)
    small = eye[:half, :half]
    triangle = (at_row > at_col)[:half, :half]

    def lower(e):
        return jnp.where(triangle, e, 0.5 * small * e)

    def read(ref):
        return ref[top, top], ref[bottom, top], ref[bottom, bottom]

    def product(a, b):
        return dot_nn(a[0], b[0]), dot_nn(a[1], b[0]) + dot_nn(a[2], b[1]), dot_nn(a[2], b[2])

    def narrow(blocks):
        return tuple(block.astype(bf16) for block in blocks)

    p = (lower(scaled[:half, :half] - small), scaled[half:, :half], lower(scaled[half:, half:] - small))
    pb = narrow(p)
    square = product(pb, pb)
    w[top, bottom] = jnp.zeros((half, half), f32)
    w[top, top] = small - p[0] + square[0]
    w[bottom, top] = square[1] - p[1]
    w[bottom, bottom] = small - p[2] + square[2]

    def improve(e, old):
        p = (lower(e[0] - small), e[1], lower(e[2] - small))
        pb = narrow(p)
        first = product(pb, narrow(old))
        second = product(pb, narrow(first))
        w[top, top] = old[0] - first[0] + second[0]
        w[bottom, top] = old[1] - first[1] + second[1]
        w[bottom, bottom] = old[2] - first[2] + second[2]
        return jnp.sqrt(sum(jnp.sum(block * block) for block in p))

    def congruence(nn, nt, cut, w, s):
        s00, s10, s11, s01 = s
        left = nn(w[0], s00)
        below, right = nn(w[1], s00) + nn(w[2], s10), nn(w[1], s01) + nn(w[2], s11)
        left, below, right = cut(left), cut(below), cut(right)
        return nt(left, w[0]), nt(below, w[0]), nt(below, w[1]) + nt(right, w[2])

    def whole(ref):
        return read(ref) + (ref[top, bottom],)

    def rough(state):
        old = read(w)
        e = congruence(dot_nn, dot_nt, lambda a: a.astype(bf16), narrow(old), whole(high))
        return state[0] + 1, improve(e, old)

    def fine(state):
        old = read(w)
        nn, nt = (lambda a, b: dot3(dot_nn, a, b)), (lambda a, b: dot3(dot_nt, a, b))
        e = congruence(nn, nt, split, [split(a) for a in old], list(zip(whole(high), whole(low))))
        return state[0] + 1, improve(e, old)

    def until(bound, most):
        return lambda state: (state[0] < most) & jnp.logical_not(state[1] <= bound)

    lax.while_loop(until(0.4, 16), rough, (0, jnp.float32(1e9)))
    _, error = lax.while_loop(until(0.1, 6), fine, (0, jnp.float32(1e9)))
    done = error <= 0.1

    @pl.when(done)
    def _():
        w[...] = w[...] * (by_col * jnp.sqrt(scale))

    @pl.when(jnp.logical_not(done))
    def _():
        w[...] = eye

        def eliminate(k, carry):
            lane = lax.broadcasted_iota(jnp.int32, (1, n), 1)
            below = lax.broadcasted_iota(jnp.int32, (n, 1), 0)
            row = g[pl.ds(k, 1), :]
            pivot = jnp.sum(jnp.where(lane == k, row, 0.0), axis=1, keepdims=True)
            column = jnp.sum(jnp.where(at_col == k, g[...], 0.0), axis=1, keepdims=True)
            ratio = jnp.where(below > k, column / pivot, 0.0)
            solved = w[pl.ds(k, 1), :]
            g[...] = g[...] - ratio * row
            w[...] = w[...] - ratio * solved
            w[pl.ds(k, 1), :] = solved * lax.rsqrt(pivot)
            return carry

        lax.fori_loop(0, n, eliminate, 0)


def lay_out(out, first, second):
    width = first.shape[1]
    folded = 3 * width // 4
    out[pl.ds(0, width), pl.ds(0, width)] = unfold(first[:folded])
    out[pl.ds(width, width), pl.ds(width, width)] = unfold(second[:folded])
    below = jnp.concatenate([first[folded:], second[folded:]], axis=0)
    out[pl.ds(width, width), pl.ds(0, width)] = below
    out[pl.ds(0, width), pl.ds(width, width)] = below.T


def factor_kernel(rows_total, first_step, last, core, v, v_other, x, x_other, sums, sums_other, *refs):
    out, (g, w, high, low, update, rayleigh) = refs[:-6], refs[-6:]
    width, count = v.shape
    ahead = core[0] == 0

    def ordered(mine, theirs):
        mine, theirs = mine / rows_total, theirs / rows_total
        return jnp.where(ahead, mine, theirs), jnp.where(ahead, theirs, mine)

    blocks, rows, _ = sums.shape
    cut = rows - 5 * width // 4 // blocks
    folded, extra = 3 * width // 4, 7 * width // 4

    def joined(ref, low, high):
        return jnp.concatenate([ref[block, pl.ds(low, high - low), :] for block in range(blocks)], axis=0)

    inner, inner_other = joined(sums, 0, cut), joined(sums_other, 0, cut)
    first, second = ordered(inner[:extra], inner_other[:extra])
    rayleigh[pl.ds(0, width), pl.ds(0, width)] = unfold(first[:folded])
    rayleigh[pl.ds(width, width), pl.ds(width, width)] = unfold(second[:folded])
    across = first[folded:] + second[folded:].T
    rayleigh[pl.ds(0, width), pl.ds(width, width)] = across
    rayleigh[pl.ds(width, width), pl.ds(0, width)] = across.T
    lay_out(g, *ordered(joined(sums, cut, rows), joined(sums_other, cut, rows)))
    r = split(rayleigh[...])
    if first_step:
        end = extra + 5 * width // 4
        lay_out(w, *ordered(inner[extra:end], inner_other[extra:end]))
        turned = dot3(dot_nn, split(w[...]), r)
        g[...] += STEP_RATE * (turned + turned.T)
        g[...] += dot3(dot_nn, r, split(STEP_RATE**2 * turned - (2 * STEP_RATE**2) * rayleigh[...]))
    else:
        g[...] += 2 * STEP_RATE * rayleigh[...] - STEP_RATE**2 * dot3(dot_nn, r, r)
    inverse_factor(g, w, high, low)
    start = pl.multiple_of(core[0] * width, width)
    there = width - start
    update[pl.ds(start, width), :] = x[...]
    update[pl.ds(there, width), :] = x_other[...]
    mix = split(w[pl.ds(start, width), :])
    mine = split(rayleigh[pl.ds(start, width), :])
    theirs = split(rayleigh[pl.ds(there, width), :])
    for t in range(count // width):
        part = pl.ds(t * width, width)
        old = split(update[:, part])
        here = v[:, part] + STEP_RATE * dot3(dot_nn, mine, old)
        update[pl.ds(there, width), part] = v_other[:, part] + STEP_RATE * dot3(dot_nn, theirs, old)
        update[pl.ds(start, width), part] = here
        solved = dot3(dot_nn, mix, split(update[:, part]))
        if last:
            out[0][part, :] = solved.T
            out[1][part, :] = ((x[:, part] - here) * (1 / STEP_RATE)).T
        else:
            out[0][:, part] = solved
            out[1][t] = solved.astype(bf16)


def swap_cores(a):
    return lax.ppermute(a, "vec", [(0, 1), (1, 0)])


def flip(a, mask):
    return lax.ppermute(a, "patch", [(i, i ^ mask) for i in range(lax.axis_size("patch"))])


def shift(a, pairs):
    devices = range(lax.axis_size("patch"))
    return lax.ppermute(a, "patch", [(i - 2 * pairs, i) for i in devices if i - 2 * pairs in devices])


def stride(a, back=False):
    devices = range(lax.axis_size("patch"))
    route = [(i - (2 if i // 2 % 2 else 6), i) for i in devices]
    return lax.ppermute(a, "patch", [(d, s) if back else (s, d) for s, d in route if s in devices])


def together(*arrays):
    return lax.optimization_barrier(arrays)


def reach(u, own_x):
    two, far = shift(u, 2), stride(together(u, own_x)[0])
    return two, flip(two, 1), far, flip(two, 2)


def place_order(parts, place):
    radix = len(parts)
    bit = 1
    while bit < radix:
        swapped = [parts[j ^ bit] for j in range(radix)]
        parts = [jnp.where(place & bit, b, a) for a, b in zip(parts, swapped)]
        bit *= 2
    return parts


def stages_of():
    left, step, stages = lax.axis_size("patch"), 1, []
    while left > 1:
        radix = 4 if left % 4 == 0 else 2
        stages.append((radix, step))
        left, step = left // radix, step * radix
    return stages


def scatter(a, stage):
    radix, step = stage
    place = (lax.axis_index("patch") // step) % radix
    parts = a.reshape(radix, a.shape[0] // radix, a.shape[1])
    a = lax.dynamic_index_in_dim(parts, place, 0, False)
    for m in range(1, radix):
        a = a + flip(lax.dynamic_index_in_dim(parts, place ^ m, 0, False), m * step)
    return a


def shared(a, stage):
    radix, step = stage
    return [a] + [flip(a, m * step) for m in range(1, radix)]


def in_order(parts, stage):
    radix, step = stage
    return jnp.concatenate(place_order(parts, (lax.axis_index("patch") // step) % radix), axis=0)


def sum_both(a, b, stages):
    for stage_a, stage_b in zip(stages[1:], stages[:-1], strict=True):
        a, b = together(scatter(a, stage_a), scatter(b, stage_b))
    cut = a.shape[0]
    parts = shared(jnp.concatenate([a, b]), stages[-1])
    joined = jnp.concatenate([in_order([part[:cut] for part in parts], stages[-1]), sum(part[cut:] for part in parts)])
    blocks = 1
    for stage in stages[-2::-1]:
        joined = in_order(shared(joined, stage), stage)
        blocks *= stage[0]
    return joined.reshape(blocks, joined.shape[0] // blocks, joined.shape[1])


def shards(vectors, blocks, block_row, block_col, block_count):
    count, width = vectors.shape
    size = blocks.shape[1]
    rows_total = float(count * lax.axis_size("patch"))
    position = lax.axis_index("patch")
    odd = position % 2
    meta = jnp.stack([block_count[0], 2 * (position - odd) - 4 * (REACH - 1), odd, position // 2 % 2]).astype(jnp.int32)
    meta = jnp.concatenate([meta, block_row, block_col])
    core = lax.axis_index("vec").astype(jnp.int32).reshape(1)
    stages = stages_of()
    flat, chunk = shape(f32, width, count), shape(bf16, count // size, width, size)
    x, u = call(pack_kernel, [flat, chunk], [vectors])
    for step in range(STEPS):
        last = step == STEPS - 1
        own_x = flip(u, 1)
        x_other = swap_cores(x)
        cross_other = swap_cores(own_x)
        table = (meta, blocks)
        segment = (2, width, size)
        sums = tiles_call(
            mirror_kernel, [shape(kind, *segment) for kind in SEGMENT_KINDS], *table, [u, own_x], [], 4, 4 * REACH
        )
        same, cross = sums[::2], sums[1::2]
        two, two_x, far, side = reach(u, own_x)
        out_side_x, out_far, out_side = together(cross[3], cross[2], same[3], far, two_x, side)[:3]
        pieces = [u, own_x, two, two_x, far, flip(far, 1), side, flip(two_x, 2)]
        kept, near, inner = tiles_call(
            direct_kernel,
            [shape(f32, *segment), shape(bf16, *segment), shape(f32, 7 * width // 4, width)],
            *table,
            pieces,
            [x_other, cross_other, same[0], cross[0]],
            4 * REACH,
            4,
        )
        side_x, far_x, side = flip(out_side_x, 2), flip(out_far, 1), flip(out_side, 2)
        two_out = (cross[1] + side_x.astype(f32)).astype(bf16)
        far_sum = (same[2] + far_x.astype(f32)).astype(bf16)
        two_x, far = flip(two_out, 1), stride(far_sum, True)
        two_sum = (same[1] + (two_x.astype(f32) + side.astype(f32))).astype(bf16)
        two = shift(two_sum, -2)
        inner_out = [inner]
        if step == 0:
            inner_out += call(gram_kernel, [shape(f32, 5 * width // 4, width)], [core, x, x_other], smem=1)
        inner = jnp.concatenate(inner_out)
        inner = jnp.pad(inner, ((0, -inner.shape[0] % lax.axis_size("patch")), (0, 0)))
        inner = together(inner, two_sum, far_sum)[0]
        inner = scatter(inner, stages[0])
        inner, *joined = together(inner, flip(near, 1), far, two)
        (v,) = call(descend_kernel, [flat], [x, kept, *joined])
        v_other = swap_cores(v)
        (gram,) = call(gram_kernel, [shape(f32, 5 * width // 4, width)], [core, v, v_other], smem=1)
        inner, gram = together(inner, gram)
        sums = sum_both(inner, gram, stages)
        full = (2 * width, 2 * width)
        wide = shape(f32, count, width)
        out = call(
            lambda *refs: factor_kernel(rows_total, step == 0, last, *refs),
            [wide, wide] if last else [flat, chunk],
            [core, v, v_other, x, x_other, sums, swap_cores(sums)],
            scratch=[VMEM(full, f32), VMEM(full, f32), VMEM(full, bf16), VMEM(full, bf16)]
            + [VMEM((2 * width, count), f32), VMEM(full, f32)],
            smem=1,
            flops=16 << 30,
            vmem=28,
        )
        x, u = out
    return x, u


def solution(mesh):
    in_specs = (P("patch", "vec"), P("patch", None, None), P("patch"), P("patch"), P("patch"))
    out_specs = (P("patch", "vec"), P("patch", "vec"))
    return jax.shard_map(shards, mesh=mesh, in_specs=in_specs, out_specs=out_specs, check_vma=False)
```
